128 devices in a mesh: lat: 8 (over z, x_lo), lon: 16 (over y, x_hi, core).
Axes of the slice: x: 4 (x_hi: 2, x_lo: 2; x = x_hi * 2 + x_lo), y: 4, z: 4, core: 2. Of those that a mesh axis runs over, the one named last changes fastest.
Arguments:
- activations: bfloat16 [192, 768, 512], P('lat', 'lon'), may hold values from -6 to 6
- cotangent: bfloat16 [192, 768, 512], P('lat', 'lon'), may hold values from -6 to 6
- norm_gain: float32 [512], replicated, may hold values from 0.1 to 1.9
- qkv_weight: bfloat16 [512, 1536], replicated, may hold values from -12 to 12
- proj_weight: bfloat16 [512, 512], replicated, may hold values from -0.25 to 0.25
Outputs:
- grad_input: bfloat16 [192, 768, 512], P('lat', 'lon')
- grad_qkv: float32 [512, 1536], P(('lat', 'lon'))
- grad_proj: float32 [512, 512], P(('lat', 'lon'))
- grad_gain: float32 [512], P(('lat', 'lon'))
The draws below stay inside these ranges and needn't reach their ends.
All inputs are finite; a program needn't handle non-finite values.
Results may differ from the reference program's by a relative error of at most 0.0059.
The reference program's roundings to bfloat16 on the way count: a program that leaves them out, or rounds other values in their place, can miss the bound.
Values may be sent and summed in bfloat16 or wider, within the bound.
A program may use at most 128 MiB of HBM per device.

```python
import math
import jax
import jax.numpy as jnp
from jax import lax

C = 512
HEADS = 16
WIN_LAT = 6
WIN_LON = 12
H = 192
W = 768


def draw_qkv_weight(key, part):
    key = jax.random.fold_in(key, 7)
    base = jnp.clip(jax.random.normal(key, (C, 3 * C), jnp.float32), -4.0, 4.0) * C ** (-0.5)
    return jnp.clip(base, -12.0, 12.0).astype(jnp.bfloat16)


def level_of(stream_key, shape, cuts, smallest, high):
    def one(dim, shards_of):
        steps = jax.random.uniform(jax.random.fold_in(jax.random.fold_in(stream_key, 6), dim), (shards_of,), jnp.float32, smallest / len(cuts), high / len(cuts))
        return jnp.repeat(jnp.exp(steps), shape[dim] // shards_of).reshape((-1,) + (1,) * (len(shape) - dim - 1))

    level = one(*cuts[0])
    for cut in cuts[1:]:
        level = level * one(*cut)
    return level


def normal_values(own_key, extent, width, limit, shards=(), dtype=jnp.bfloat16):
    entries = width * jax.random.normal(own_key, extent, jnp.float32)
    if shards:
        entries = entries * level_of(own_key, extent, shards, -0.22, 0.18)
    return jnp.clip(entries, -limit, limit).astype(dtype)


def setup_inputs(seed: int = 0) -> dict:
    arg_keys = jax.random.split(jax.random.key(seed), 6)
    return {
        "activations": normal_values(arg_keys[0], (H, W, C), 1.0, 6.0, ((0, 8), (1, 16))),
        "cotangent": normal_values(arg_keys[1], (H, W, C), 1.0, 6.0, ((0, 8), (1, 16))),
        "norm_gain": jnp.clip(1.0 + 0.18 * jax.random.normal(arg_keys[2], (C,), jnp.float32), 0.1, 1.9),
        "qkv_weight": draw_qkv_weight(jax.random.fold_in(arg_keys[5], 71), 0),
        "proj_weight": normal_values(arg_keys[4], (C, C), C ** -0.5, 0.25),
    }


def window_grads(win_in, win_cot, win_region, norm_gain, qkv_weight, proj_weight):
    n_windows, win_span, channels = win_in.shape
    head_size = channels // HEADS
    scale = head_size ** (-0.5)
    tokens_f = win_in.astype(jnp.float32).reshape(n_windows * win_span, channels)
    center = tokens_f - lax.optimization_barrier(jnp.mean(tokens_f, axis=-1, keepdims=True))
    inv_std = lax.rsqrt(lax.optimization_barrier(jnp.mean(center * center, axis=-1, keepdims=True)) + 1e-05)
    normed = center * inv_std
    scaled_in = (normed * norm_gain).astype(jnp.bfloat16)
    qkv_all = jnp.dot(scaled_in, qkv_weight, preferred_element_type=jnp.float32).astype(jnp.bfloat16)
    qkv_all = qkv_all.reshape(n_windows, win_span, 3, HEADS, head_size)
    query = qkv_all[:, :, 0].astype(jnp.float32)
    key_heads = qkv_all[:, :, 1].astype(jnp.float32)
    val_heads = qkv_all[:, :, 2].astype(jnp.float32)
    scores = jnp.einsum('bqhd,bkhd->bhqk', query, key_heads) * scale
    allowed = (win_region[:, :, None] == win_region[:, None, :])[:, None]
    scores = jnp.where(allowed, scores, -1e+30)
    row_max = lax.optimization_barrier(jnp.max(scores, axis=-1, keepdims=True))
    expon = jnp.exp(scores - row_max)
    prob = expon / lax.optimization_barrier(jnp.sum(expon, axis=-1, keepdims=True))
    prob_b = prob.astype(jnp.bfloat16)
    attended = jnp.einsum('bhqk,bkhd->bqhd', prob_b.astype(jnp.float32), val_heads)
    attended = attended.astype(jnp.bfloat16).reshape(n_windows * win_span, channels)
    cot_flat = win_cot.reshape(n_windows * win_span, channels)
    grad_proj = jnp.dot(attended.T, cot_flat, preferred_element_type=jnp.float32)
    grad_att = jnp.dot(cot_flat, proj_weight.T, preferred_element_type=jnp.float32).astype(jnp.bfloat16)
    grad_att = grad_att.reshape(n_windows, win_span, HEADS, head_size).astype(jnp.float32)
    grad_prob = jnp.einsum('bqhd,bkhd->bhqk', grad_att, val_heads)
    grad_val = jnp.einsum('bhqk,bqhd->bkhd', prob_b.astype(jnp.float32), grad_att).astype(jnp.bfloat16)
    inner = lax.optimization_barrier(jnp.sum(prob * grad_prob, axis=-1, keepdims=True))
    grad_score = (prob * (grad_prob - inner) * scale).astype(jnp.bfloat16).astype(jnp.float32)
    grad_query = jnp.einsum('bhqk,bkhd->bqhd', grad_score, key_heads).astype(jnp.bfloat16)
    grad_key = jnp.einsum('bhqk,bqhd->bkhd', grad_score, query).astype(jnp.bfloat16)
    grad_all = jnp.stack([grad_query, grad_key, grad_val], axis=2).reshape(n_windows * win_span, 3 * channels)
    grad_qkv = jnp.dot(scaled_in.T, grad_all, preferred_element_type=jnp.float32)
    grad_normed = jnp.dot(grad_all, qkv_weight.T, preferred_element_type=jnp.float32)
    grad_gain = lax.optimization_barrier(jnp.sum(grad_normed * normed, axis=0))
    grad_hat = grad_normed * norm_gain
    branch = inv_std * (grad_hat - lax.optimization_barrier(jnp.mean(grad_hat, axis=-1, keepdims=True)) - normed * lax.optimization_barrier(jnp.mean(grad_hat * normed, axis=-1, keepdims=True)))
    return (branch.reshape(n_windows, win_span, channels), grad_qkv, grad_proj, grad_gain)

def to_windows(field, lat_cells, lon_cells):
    channels = field.shape[-1]
    blocks = field.reshape(lat_cells // WIN_LAT, WIN_LAT, lon_cells // WIN_LON, WIN_LON, channels)
    return blocks.transpose(0, 2, 1, 3, 4).reshape(-1, WIN_LAT * WIN_LON, channels)

def from_windows(blocks, lat_cells, lon_cells):
    channels = blocks.shape[-1]
    grid = blocks.reshape(lat_cells // WIN_LAT, lon_cells // WIN_LON, WIN_LAT, WIN_LON, channels)
    return grid.transpose(0, 2, 1, 3, 4).reshape(lat_cells, lon_cells, channels)

def reference(activations, cotangent, norm_gain, qkv_weight, proj_weight):
    lat_cells, lon_cells, channels = activations.shape
    half_lat = WIN_LAT // 2
    half_lon = WIN_LON // 2
    moved_in = jnp.roll(activations, (-half_lat, -half_lon), (0, 1))
    moved_cot = jnp.roll(cotangent, (-half_lat, -half_lon), (0, 1))
    row_region = (jnp.arange(lat_cells) >= lat_cells - half_lat).astype(jnp.int32)
    region_grid = jnp.broadcast_to(row_region[:, None, None], (lat_cells, lon_cells, 1))
    win_in = to_windows(moved_in, lat_cells, lon_cells)
    win_cot = to_windows(moved_cot, lat_cells, lon_cells)
    win_region = to_windows(region_grid, lat_cells, lon_cells)[:, :, 0]
    n_windows, win_span = (win_in.shape[0], win_in.shape[1])
    win_group = math.gcd(n_windows, 64)
    n_steps = n_windows // win_group

    def step_fn(running, pieces):
        branch, g_qkv, g_proj, g_gain = window_grads(pieces[0], pieces[1], pieces[2], norm_gain, qkv_weight, proj_weight)
        return ((running[0] + g_qkv, running[1] + g_proj, running[2] + g_gain), branch)
    start_sums = (jnp.zeros((channels, 3 * channels), jnp.float32), jnp.zeros((channels, channels), jnp.float32), jnp.zeros((channels,), jnp.float32))
    totals, branches = lax.scan(step_fn, start_sums, (win_in.reshape(n_steps, win_group, win_span, channels), win_cot.reshape(n_steps, win_group, win_span, channels), win_region.reshape(n_steps, win_group, win_span)))
    branch_grid = from_windows(branches.reshape(n_windows, win_span, channels), lat_cells, lon_cells)
    branch_grid = jnp.roll(branch_grid, (half_lat, half_lon), (0, 1))
    grad_input = (cotangent.astype(jnp.float32) + branch_grid).astype(jnp.bfloat16)
    token_scale = 1.0 / math.sqrt(lat_cells * lon_cells)
    return (grad_input, totals[0] * token_scale, totals[1] * token_scale, totals[2] * token_scale)
```

```python
import functools
import math

import jax
import jax.numpy as jnp
import numpy as np
from jax import lax
from jax.experimental import pallas as pl
from jax.experimental.pallas import tpu as pltpu
from jax.sharding import PartitionSpec as P

C = 512
HEADS = 16
HEAD = C // HEADS
WIN_LAT = 6
WIN_LON = 12
SPAN = WIN_LAT * WIN_LON
ROWS = 24
COLS = 48
BANDS = ROWS // WIN_LAT
PER_BAND = COLS // WIN_LON
BAND = WIN_LAT * COLS
TOKENS = ROWS * COLS
HALF_LAT = WIN_LAT // 2
HALF_LON = WIN_LON // 2
SIDE = 48
GROUP = 128 // HEAD
F32 = jnp.float32
BF16 = jnp.bfloat16


def window_order():
    perm = np.zeros((BAND, BAND + SIDE), np.float32)
    for b in range(PER_BAND):
        for r in range(WIN_LAT):
            for c in range(WIN_LON):
                col = WIN_LON * b + HALF_LON + c
                src = r * COLS + col if col < COLS else BAND + r * HALF_LON + col - COLS
                perm[b * SPAN + r * WIN_LON + c, src] = 1.0
    return perm


def nn(a, b):
    return lax.dot_general(a, b, (((1,), (0,)), ((), ())), preferred_element_type=F32)


def nt(a, b):
    return lax.dot_general(a, b, (((1,), (1,)), ((), ())), preferred_element_type=F32)


def tn(a, b):
    return lax.dot_general(a, b, (((0,), (0,)), ((), ())), preferred_element_type=F32)


def local_kernel(
    own_in, own_cot, low_in, low_cot, side_in, side_cot, gain, wqkv, wproj, perm, perm_t, bias,
    out_ref, out_low, out_side, gqkv_ref, gproj_ref,
    ext_in, ext_cot, normed, inv_std, scaled, cot_win, qkv, grad_att, att, grad_all, out_ext,
):
    ext_in[0:TOKENS] = own_in[...]
    ext_cot[0:TOKENS] = own_cot[...]
    ext_in[TOKENS:] = low_in[...]
    ext_cot[TOKENS:] = low_cot[...]

    def forward(a, carry):
        src = pl.ds(pl.multiple_of(a * BAND + HALF_LAT * COLS, 16), BAND)
        dst = pl.ds(pl.multiple_of(a * BAND, 16), BAND)
        side = pl.ds(pl.multiple_of(a * SIDE, 16), SIDE)
        x = nn(perm[...], jnp.concatenate([ext_in[src], side_in[side]], axis=0))
        cot = nn(perm[...], jnp.concatenate([ext_cot[src], side_cot[side]], axis=0)).astype(BF16)
        center = x - jnp.mean(x, axis=-1, keepdims=True)
        inv = lax.rsqrt(jnp.mean(center * center, axis=-1, keepdims=True) + 1e-05)
        norm = center * inv
        normed[dst] = norm
        inv_std[dst] = jnp.broadcast_to(inv, (BAND, 128))
        sc = (norm * gain[...]).astype(BF16)
        scaled[dst] = sc
        cot_win[dst] = cot
        qkv[dst] = nn(sc, wqkv[...]).astype(BF16).astype(F32)
        grad_att[dst] = nt(cot, wproj[...]).astype(BF16).astype(F32)
        return carry

    lax.fori_loop(0, BANDS, forward, 0)

    lane = lax.broadcasted_iota(jnp.int32, (1, 128), 1) // HEAD
    masks = [(lane == j).astype(F32) for j in range(GROUP)]

    def stacked(x):
        return jnp.concatenate([x * m for m in masks], axis=0).astype(BF16)

    def by_head(x):
        x = x.reshape(GROUP, SPAN, 128)
        y = x[GROUP - 1]
        for j in range(GROUP - 2, -1, -1):
            y = jnp.where(lane == j, x[j], y)
        return y

    scale = HEAD ** (-0.5)

    def attention(w, carry):
        rows = pl.ds(pl.multiple_of(w * SPAN, 8), SPAN)
        edge = jnp.where(w >= (BANDS - 1) * PER_BAND, 1.0, 0.0)
        shut = bias[...] * edge
        for g in range(C // 128):
            cols = slice(g * 128, (g + 1) * 128)
            q = qkv[rows, g * 128 : (g + 1) * 128].astype(BF16)
            k_st = stacked(qkv[rows, C + g * 128 : C + (g + 1) * 128])
            v_st = stacked(qkv[rows, 2 * C + g * 128 : 2 * C + (g + 1) * 128])
            da = grad_att[rows, cols].astype(BF16)
            s = nt(k_st, q).reshape(GROUP, SPAN, SPAN) * scale + shut
            ex = jnp.exp(s - jnp.max(s, axis=1, keepdims=True))
            prob = ex * (1.0 / jnp.sum(ex, axis=1, keepdims=True))
            gp = nt(v_st, da).reshape(GROUP, SPAN, SPAN)
            inner = jnp.sum(prob * gp, axis=1, keepdims=True)
            gs = (prob * (gp - inner) * scale).reshape(GROUP * SPAN, SPAN).astype(BF16)
            pb = prob.reshape(GROUP * SPAN, SPAN).astype(BF16)
            att[rows, cols] = tn(pb, v_st)
            grad_all[rows, g * 128 : (g + 1) * 128] = tn(gs, k_st)
            grad_all[rows, C + g * 128 : C + (g + 1) * 128] = by_head(nn(gs, q))
            grad_all[rows, 2 * C + g * 128 : 2 * C + (g + 1) * 128] = by_head(nn(pb, da))
        return carry

    lax.fori_loop(0, BANDS * PER_BAND, attention, 0)

    gproj_ref[...] = tn(att[...].astype(BF16), cot_win[...])
    for j in range(3):
        cols = slice(j * C, (j + 1) * C)
        gqkv_ref[:, cols] = tn(scaled[...], grad_all[:, cols].astype(BF16))

    def backward(a, carry):
        dst = pl.ds(pl.multiple_of(a * BAND, 16), BAND)
        gn = nt(grad_all[dst].astype(BF16), wqkv[...]) * gain[...]
        norm = normed[dst]
        branch = inv_std[dst][:, 0:1] * (
            gn
            - jnp.mean(gn, axis=-1, keepdims=True)
            - norm * jnp.mean(gn * norm, axis=-1, keepdims=True)
        )
        out = (cot_win[dst].astype(F32) + branch).astype(BF16)
        slab = nn(perm_t[...], out).astype(BF16)
        out_ext[pl.ds(pl.multiple_of(a * BAND, 16), BAND)] = slab[:BAND]
        out_side[pl.ds(pl.multiple_of(a * SIDE, 16), SIDE)] = slab[BAND:]
        return carry

    lax.fori_loop(0, BANDS, backward, 0)
    lead = HALF_LAT * COLS
    out_ref[0:lead] = jnp.zeros((lead, C), BF16)
    out_ref[lead:] = out_ext[0 : TOKENS - lead]
    out_low[...] = out_ext[TOKENS - lead :]


def local_grads(*args):
    vmem = pl.BlockSpec(memory_space=pltpu.VMEM)
    lead = HALF_LAT * COLS
    return pl.pallas_call(
        local_kernel,
        out_shape=(
            jax.ShapeDtypeStruct((TOKENS, C), BF16),
            jax.ShapeDtypeStruct((lead, C), BF16),
            jax.ShapeDtypeStruct((BANDS * SIDE, C), BF16),
            jax.ShapeDtypeStruct((C, 3 * C), F32),
            jax.ShapeDtypeStruct((C, C), F32),
        ),
        in_specs=[vmem] * 12,
        out_specs=(vmem,) * 5,
        scratch_shapes=[
            pltpu.VMEM((TOKENS + lead, C), BF16),
            pltpu.VMEM((TOKENS + lead, C), BF16),
            pltpu.VMEM((TOKENS, C), F32),
            pltpu.VMEM((TOKENS, 128), F32),
            pltpu.VMEM((TOKENS, C), BF16),
            pltpu.VMEM((TOKENS, C), BF16),
            pltpu.VMEM((TOKENS, 3 * C), F32),
            pltpu.VMEM((TOKENS, C), F32),
            pltpu.VMEM((TOKENS, C), F32),
            pltpu.VMEM((TOKENS, 3 * C), F32),
            pltpu.VMEM((TOKENS, C), BF16),
        ],
        compiler_params=pltpu.CompilerParams(vmem_limit_bytes=60 * 1024 * 1024),
        name="window_grads",
    )(*args)


def shifted(shard, axis, by):
    peers = lax.axis_size(axis)
    return lax.ppermute(shard, axis, [(i, (i + by) % peers) for i in range(peers)])


def on_device(activations, cotangent, norm_gain, qkv_weight, proj_weight):
    both = jnp.stack([activations, cotangent])
    low = shifted(both[:, :HALF_LAT], "lat", -1)
    edge = jnp.concatenate([both[:, HALF_LAT:, :HALF_LON], low[:, :, :HALF_LON]], axis=1)
    side = shifted(edge, "lon", -1)
    side = side.reshape(2, BANDS, WIN_LAT * HALF_LON, C)
    side = jnp.pad(side, ((0, 0), (0, 0), (0, SIDE - WIN_LAT * HALF_LON), (0, 0)))
    side = side.reshape(2, BANDS * SIDE, C)
    low = low.reshape(2, HALF_LAT * COLS, C)
    perm = window_order()
    half = np.arange(SPAN) >= HALF_LAT * WIN_LON
    shut = np.where(half[:, None] == half[None, :], 0.0, -1e30).astype(np.float32)
    last = lax.axis_index("lat") == lax.axis_size("lat") - 1
    bias = jnp.where(last, jnp.asarray(shut), 0.0)
    out, out_low, out_side, gqkv, gproj = local_grads(
        activations.reshape(TOKENS, C),
        cotangent.reshape(TOKENS, C),
        low[0], low[1], side[0], side[1],
        norm_gain.reshape(1, C),
        qkv_weight,
        proj_weight,
        jnp.asarray(perm, BF16),
        jnp.asarray(perm.T, BF16),
        bias,
    )
    out_side = out_side.reshape(BANDS, SIDE, C)[:, : WIN_LAT * HALF_LON].reshape(ROWS, HALF_LON, C)
    left = shifted(out_side, "lon", 1)
    low_rows = out_low.reshape(HALF_LAT, COLS, C)[:, HALF_LON:]
    low_rows = jnp.concatenate([left[ROWS - HALF_LAT :], low_rows], axis=1)
    top = shifted(low_rows, "lat", 1)
    rest = out.reshape(ROWS, COLS, C)[HALF_LAT:, HALF_LON:]
    rest = jnp.concatenate([left[: ROWS - HALF_LAT], rest], axis=1)
    grad_input = jnp.concatenate([top, rest], axis=0)
    token_scale = 1.0 / math.sqrt(TOKENS * lax.axis_size("lat") * lax.axis_size("lon"))
    gqkv = lax.psum_scatter(gqkv, ("lat", "lon"), scatter_dimension=0, tiled=True)
    gproj = lax.psum_scatter(gproj, ("lat", "lon"), scatter_dimension=0, tiled=True)
    gqkv = gqkv * token_scale
    me = lax.axis_index("lat") * lax.axis_size("lon") + lax.axis_index("lon")
    share = gqkv.shape[0]
    w_rows = lax.dynamic_slice_in_dim(qkv_weight, me * share, share, 0).astype(F32)
    gain_rows = lax.dynamic_slice_in_dim(norm_gain, me * share, share, 0)
    ggain = jnp.sum(gqkv * w_rows, axis=1) / gain_rows
    return grad_input, gqkv, gproj * token_scale, ggain


def solution(mesh):
    return jax.shard_map(
        on_device,
        mesh=mesh,
        in_specs=(P("lat", "lon", None), P("lat", "lon", None), P(), P(), P()),
        out_specs=(
            P("lat", "lon", None),
            P(("lat", "lon"), None),
            P(("lat", "lon"), None),
            P(("lat", "lon")),
        ),
        check_vma=False,
    )
```

```python
import math

import jax
import jax.numpy as jnp
import numpy as np
from jax import lax
from jax.experimental import pallas as pl
from jax.experimental.pallas import tpu as pltpu
from jax.sharding import PartitionSpec as P

C = 512
HEADS = 16
HEAD = C // HEADS
WIN_LAT = 6
WIN_LON = 12
SPAN = WIN_LAT * WIN_LON
ROWS = 24
COLS = 48
BANDS = ROWS // WIN_LAT
PER_BAND = COLS // WIN_LON
BAND = WIN_LAT * COLS
TOKENS = ROWS * COLS
HALF_LAT = WIN_LAT // 2
HALF_LON = WIN_LON // 2
SIDE = 48
GROUP = 128 // HEAD
F32 = jnp.float32
BF16 = jnp.bfloat16


def window_order():
    perm = np.zeros((BAND, BAND + SIDE), np.float32)
    for b in range(PER_BAND):
        for r in range(WIN_LAT):
            for c in range(WIN_LON):
                col = WIN_LON * b + HALF_LON + c
                src = r * COLS + col if col < COLS else BAND + r * HALF_LON + col - COLS
                perm[b * SPAN + r * WIN_LON + c, src] = 1.0
    return perm


def nn(a, b):
    return lax.dot_general(a, b, (((1,), (0,)), ((), ())), preferred_element_type=F32)


def nt(a, b):
    return lax.dot_general(a, b, (((1,), (1,)), ((), ())), preferred_element_type=F32)


def tn(a, b):
    return lax.dot_general(a, b, (((0,), (0,)), ((), ())), preferred_element_type=F32)


PARTS = ((0, 256, "zyx"), (256, 128, "xzy"), (384, 128, "yxz"))
MESH = pl.DeviceIdType.MESH
LEAD = HALF_LAT * COLS
PAIR = 2 * SPAN


def place():
    lat, lon = lax.axis_index("lat"), lax.axis_index("lon")
    spot = {"z": lat // 2, "x": (lon // 2) % 2 * 2 + lat % 2, "y": lon // 4}
    return lat, lon, spot, lon % 2


def device_at(spot, core):
    return (spot["z"] * 2 + spot["x"] % 2, spot["y"] * 4 + spot["x"] // 2 * 2 + core)


def along(spot, axis, by):
    return {**spot, axis: (spot[axis] + by) % 4}


def chip_at(at):
    return at["z"] * 16 + at["x"] % 2 * 8 + at["y"] * 2 + at["x"] // 2


def sublayer_kernel(
    own_in, own_cot, gain, wqkv_hbm, wproj_hbm, perm, perm_t, spread,
    out_ref, gqkv_ref, gproj_ref, ggain_ref,
    ext, side, side_out, corner, corner_out, wqkv, wproj,
    normed, inv_std, scaled, cot_win, scaled_t, att_t, qkv, grad_att, att, grad_all,
    out_ext, back_side, top, left, back_corner, grads, mine, theirs, got0,
    *rest,
):
    buffers, (local, send, recv) = rest[:-3], rest[-3:]
    loads = [
        pltpu.make_async_copy(own_in, ext.at[0, pl.ds(0, TOKENS)], local.at[0]),
        pltpu.make_async_copy(own_cot, ext.at[1, pl.ds(0, TOKENS)], local.at[1]),
        pltpu.make_async_copy(wqkv_hbm, wqkv, local.at[2]),
        pltpu.make_async_copy(wproj_hbm, wproj, local.at[3]),
    ]
    for load in loads:
        load.start()

    lat, lon, spot, core = place()
    lats, lons = lax.axis_size("lat"), lax.axis_size("lon")
    sibling = device_at(spot, 1 - core)
    down, up = (lat + 1) % lats, (lat + lats - 1) % lats
    east, west = (lon + 1) % lons, (lon + lons - 1) % lons
    peers = [sibling, (down, lon), (up, lon), (lat, east), (lat, west), (down, east), (up, west)]
    for axis in "xyz":
        peers += [device_at(along(spot, axis, k), core) for k in (1, 2, 3)]
    barrier = pltpu.get_barrier_semaphore()
    for peer in peers:
        pl.semaphore_signal(barrier, inc=1, device_id=peer, device_id_type=MESH)

    count = [0]

    def remote(src, dst, peer):
        i = count[0]
        count[0] += 1
        copy = pltpu.make_async_remote_copy(
            src_ref=src, dst_ref=dst, send_sem=send.at[i], recv_sem=recv.at[i],
            device_id=peer, device_id_type=MESH,
        )
        copy.start()
        return copy

    loads[0].wait()
    loads[1].wait()
    for i in range(2):
        for a in range(BANDS):
            rows = BAND if a < BANDS - 1 else BAND - LEAD
            start = LEAD + a * BAND
            side_out[i, a * SIDE : (a + 1) * SIDE] = tn(
                spread[0:rows], ext[i, start : start + rows]
            ).astype(BF16)
        corner_out[i] = tn(spread[BAND - LEAD :], ext[i, 0:LEAD]).astype(BF16)
    pl.semaphore_wait(barrier, len(peers))
    halo = [
        remote(side_out, side, (lat, west)),
        remote(ext.at[:, pl.ds(0, LEAD)], ext.at[:, pl.ds(TOKENS, LEAD)], (up, lon)),
        remote(corner_out, corner, (up, west)),
    ]

    def forward(pieces):
        gathered = []
        for i in range(2):
            parts = []
            for a, half in pieces:
                start = LEAD + a * BAND
                src = ext[i, start : start + BAND]
                rows = perm[half * PAIR : (half + 1) * PAIR]
                if half == 0:
                    parts.append(nn(rows[:, :BAND], src))
                else:
                    edge = side[i, a * SIDE : (a + 1) * SIDE]
                    if a == BANDS - 1:
                        edge = (edge.astype(F32) + corner[i].astype(F32)).astype(BF16)
                    parts.append(nn(rows, jnp.concatenate([src, edge], axis=0)))
            gathered.append(jnp.concatenate(parts, axis=0))
        x, cot = gathered[0], gathered[1].astype(BF16)
        center = x - jnp.mean(x, axis=-1, keepdims=True)
        inv = lax.rsqrt(jnp.mean(center * center, axis=-1, keepdims=True) + 1e-05)
        norm = center * inv
        sc = (norm * gain[...]).astype(BF16)
        qkv_now = nn(sc, wqkv[...]).astype(BF16).astype(F32)
        att_now = nt(cot, wproj[...]).astype(BF16).astype(F32)
        for i, (a, half) in enumerate(pieces):
            dst = slice(a * BAND + half * PAIR, a * BAND + (half + 1) * PAIR)
            src = slice(i * PAIR, (i + 1) * PAIR)
            normed[dst] = norm[src]
            inv_std[dst] = jnp.broadcast_to(inv[src], (PAIR, 128))
            scaled[dst] = sc[src]
            cot_win[dst] = cot[src]
            qkv[dst] = qkv_now[src]
            grad_att[dst] = att_now[src]

    lane = lax.broadcasted_iota(jnp.int32, (1, 128), 1) // HEAD
    masks = [(lane == j).astype(F32) for j in range(GROUP)]
    key_half = lax.broadcasted_iota(jnp.int32, (SPAN, SPAN), 0) >= HALF_LAT * WIN_LON
    query_half = lax.broadcasted_iota(jnp.int32, (SPAN, SPAN), 1) >= HALF_LAT * WIN_LON
    parted = jnp.where(key_half == query_half, 0.0, -1e30)

    def stacked(x):
        return jnp.concatenate([x * m for m in masks], axis=0).astype(BF16)

    def by_head(x):
        x = x.reshape(GROUP, SPAN, 128)
        y = x[GROUP - 1]
        for j in range(GROUP - 2, -1, -1):
            y = jnp.where(lane == j, x[j], y)
        return y

    scale = HEAD ** (-0.5)

    def attention(w):
        rows = pl.ds(pl.multiple_of(w * SPAN, 8), SPAN)
        edge = jnp.where((lat == lats - 1) & (w >= (BANDS - 1) * PER_BAND), 1.0, 0.0)
        shut = parted * edge
        for g in range(C // 128):
            cols = slice(g * 128, (g + 1) * 128)
            q = qkv[rows, g * 128 : (g + 1) * 128].astype(BF16)
            k_st = stacked(qkv[rows, C + g * 128 : C + (g + 1) * 128])
            v_st = stacked(qkv[rows, 2 * C + g * 128 : 2 * C + (g + 1) * 128])
            da = grad_att[rows, cols].astype(BF16)
            s = nt(k_st, q).reshape(GROUP, SPAN, SPAN) * scale + shut
            ex = jnp.exp(s - jnp.max(s, axis=1, keepdims=True))
            prob = ex * (1.0 / jnp.sum(ex, axis=1, keepdims=True))
            gp = nt(v_st, da).reshape(GROUP, SPAN, SPAN)
            inner = jnp.sum(prob * gp, axis=1, keepdims=True)
            gs = (prob * (gp - inner) * scale).reshape(GROUP * SPAN, SPAN).astype(BF16)
            pb = prob.reshape(GROUP * SPAN, SPAN).astype(BF16)
            att[rows, cols] = tn(pb, v_st)
            grad_all[rows, g * 128 : (g + 1) * 128] = tn(gs, k_st)
            grad_all[rows, C + g * 128 : C + (g + 1) * 128] = by_head(nn(gs, q))
            grad_all[rows, 2 * C + g * 128 : 2 * C + (g + 1) * 128] = by_head(nn(pb, da))

    loads[2].wait()
    loads[3].wait()
    forward([(a, 0) for a in range(BANDS - 1)])

    def early(i, carry):
        attention(i // 2 * PER_BAND + i % 2)
        return carry

    lax.fori_loop(0, 2 * (BANDS - 1), early, 0)
    for copy in halo:
        copy.wait_recv()
    forward([(a, 1) for a in range(BANDS - 1)])
    forward([(BANDS - 1, 0), (BANDS - 1, 1)])

    def late(i, carry):
        attention(jnp.where(i < 6, i // 2 * PER_BAND + 2 + i % 2, i + 6))
        return carry

    lax.fori_loop(0, 2 * (BANDS + 1), late, 0)

    scaled_t[...] = scaled[...].T
    att_t[...] = att[...].astype(BF16).T
    upper = lax.broadcasted_iota(jnp.int32, (1, 8, 1), 1) < 4
    first_core = lax.broadcasted_iota(jnp.int32, (1, 8, 1), 1) * 0 + core == 0
    first = []
    for half in range(2):
        lo = half * 256
        lanes = slice(lo, lo + 256)
        for j in range(3):
            cols = slice(j * C + lo, j * C + lo + 256)
            grads[j] = nn(scaled_t[...], grad_all[:, cols].astype(BF16))
        grads[3] = nn(att_t[...], cot_win[:, lanes])

        def pack(i, carry):
            rows = pl.ds(pl.multiple_of(i * 64, 64), 64)
            chips = pl.ds(i * 8, 8)
            t = [grads[j, rows].reshape(8, 8, 256) for j in range(4)]
            turned = [pltpu.roll(x, 4, 1) for x in t]
            block = []
            for near, far in ((t, turned), (turned, t)):
                block.append(
                    jnp.concatenate(
                        [jnp.where(upper, near[j], far[j + 1]) for j in (0, 2)], axis=1
                    )
                )
            is_first = jnp.concatenate([first_core, first_core], axis=1)
            mine[chips, :, lanes] = jnp.where(is_first, block[0], block[1])
            theirs[chips, :, lanes] = jnp.where(is_first, block[1], block[0]).astype(BF16)
            return carry

        lax.fori_loop(0, 8, pack, 0)
        for start, width, _ in PARTS:
            if lo <= start < lo + 256:
                span = pl.ds(start, width)
                first.append(remote(theirs.at[:, :, span], got0.at[:, :, span], sibling))

    back = []

    def backward(a):
        dst = slice(a * BAND, (a + 1) * BAND)
        gn = nt(grad_all[dst].astype(BF16), wqkv[...]) * gain[...]
        norm = normed[dst]
        branch = inv_std[dst][:, 0:1] * (
            gn
            - jnp.mean(gn, axis=-1, keepdims=True)
            - norm * jnp.mean(gn * norm, axis=-1, keepdims=True)
        )
        done = (cot_win[dst].astype(F32) + branch).astype(BF16)
        slab = nn(perm_t[...], done).astype(BF16)
        out_ext[dst] = slab[:BAND]
        edge = slice(a * SIDE, (a + 1) * SIDE)
        back_side[edge] = slab[BAND:]
        edge = pl.ds(a * SIDE, SIDE)
        if a == BANDS - 1:
            back.append(remote(out_ext.at[pl.ds(TOKENS - LEAD, LEAD)], top, (down, lon)))
            back.append(remote(back_side.at[edge], back_corner, (down, east)))
        back.append(remote(back_side.at[edge], left.at[edge], (lat, east)))

    def summed0(p, chip):
        lo, width, _ = PARTS[p]
        lanes = slice(lo, lo + width)
        return mine[chip, :, lanes] + got0[chip, :, lanes].astype(F32)

    sent = [[] for _ in PARTS]

    def stage0(p):
        lo, width, order = PARTS[p]
        held = buffers[6 * p]
        first[p].wait_recv()

        def add(i, carry):
            at = dict(zip(order, (i // 16, i // 4 % 4, i % 4)))
            held[i // 16, i // 4 % 4, i % 4] = summed0(p, chip_at(at)).astype(BF16)
            return carry

        lax.fori_loop(0, 64, add, 0)
        for k in (1, 2, 3):
            peer = along(spot, order[0], k)
            sent[p].append(
                remote(held.at[peer[order[0]]], buffers[6 * p + 1].at[k - 1], device_at(peer, core))
            )

    def stage1(p):
        lo, width, order = PARTS[p]
        got, nxt, nxt_got = buffers[6 * p + 1 : 6 * p + 4]
        for copy in sent[p][-3:]:
            copy.wait_recv()

        def add(i, carry):
            at = dict(zip(order, (spot[order[0]], i // 4, i % 4)))
            total = summed0(p, chip_at(at))
            for k in range(3):
                total = total + got[k, i // 4, i % 4].astype(F32)
            nxt[i // 4, i % 4] = total
            return carry

        lax.fori_loop(0, 16, add, 0)
        for k in (1, 2, 3):
            peer = along(spot, order[1], k)
            sent[p].append(remote(nxt.at[peer[order[1]]], nxt_got.at[k - 1], device_at(peer, core)))

    def stage2(p):
        lo, width, order = PARTS[p]
        held, got, nxt, nxt_got = buffers[6 * p + 2 : 6 * p + 6]
        for copy in sent[p][-3:]:
            copy.wait_recv()
        nxt[...] = held[spot[order[1]]] + got[0] + got[1] + got[2]
        for k in (1, 2, 3):
            peer = along(spot, order[2], k)
            sent[p].append(remote(nxt.at[peer[order[2]]], nxt_got.at[k - 1], device_at(peer, core)))

    def stage3(p):
        lo, width, order = PARTS[p]
        held, got = buffers[6 * p + 4 : 6 * p + 6]
        for copy in sent[p][-3:]:
            copy.wait_recv()
        return held[spot[order[2]]] + got[0] + got[1] + got[2]

    backward(BANDS - 1)
    for p in range(3):
        stage0(p)
    for a in range(BANDS - 1):
        backward(a)
    for p in range(3):
        stage1(p)

    me = lat * lons + lon
    picked = lax.broadcasted_iota(jnp.int32, (8, C), 0) + me * 4
    picked = (picked == lax.broadcasted_iota(jnp.int32, (8, C), 1)).astype(F32)
    w_rows = nn(picked.astype(BF16), wqkv[...])
    gain_rows = jnp.sum(picked * gain[...], axis=1, keepdims=True)

    for copy in back:
        copy.wait_recv()
    for a in range(BANDS):
        edge = nn(spread[...], left[a * SIDE : (a + 1) * SIDE])
        rows = BAND if a < BANDS - 1 else BAND - LEAD
        start = a * BAND
        out_ref[LEAD + start : LEAD + start + rows] = (
            out_ext[start : start + rows].astype(F32) + edge[:rows]
        ).astype(BF16)
    edge = nn(spread[...], back_corner[...])
    out_ref[0:LEAD] = (top[...].astype(F32) + edge[BAND - LEAD :]).astype(BF16)

    for p in range(3):
        stage2(p)
    total = jnp.concatenate([stage3(p) for p in range(3)], axis=1)
    total = total * (1.0 / math.sqrt(TOKENS * lats * lons))
    gqkv = [total[4 * j : 4 * j + 4] for j in range(3)]
    gqkv_ref[...] = jnp.concatenate(gqkv, axis=1)
    gproj_ref[...] = total[12:16]
    dots = jnp.zeros((4, 1), F32)
    for j in range(3):
        dots = dots + jnp.sum(gqkv[j] * w_rows[0:4, j * C : (j + 1) * C], axis=1, keepdims=True)
    dots = dots / gain_rows[0:4]
    ggain_ref[...] = jnp.broadcast_to(dots, (4, 128))
    for copy in halo + first + back + [c for part in sent for c in part]:
        copy.wait_send()


def sublayer(*args):
    vmem = pl.BlockSpec(memory_space=pltpu.VMEM)
    hbm = pl.BlockSpec(memory_space=pl.ANY)
    scratch = [
        pltpu.VMEM((2, TOKENS + LEAD, C), BF16),
        pltpu.VMEM((2, BANDS * SIDE, C), BF16),
        pltpu.VMEM((2, BANDS * SIDE, C), BF16),
        pltpu.VMEM((2, SIDE, C), BF16),
        pltpu.VMEM((2, SIDE, C), BF16),
        pltpu.VMEM((C, 3 * C), BF16),
        pltpu.VMEM((C, C), BF16),
        pltpu.VMEM((TOKENS, C), F32),
        pltpu.VMEM((TOKENS, 128), F32),
        pltpu.VMEM((TOKENS, C), BF16),
        pltpu.VMEM((TOKENS, C), BF16),
        pltpu.VMEM((C, TOKENS), BF16),
        pltpu.VMEM((C, TOKENS), BF16),
        pltpu.VMEM((TOKENS, 3 * C), F32),
        pltpu.VMEM((TOKENS, C), F32),
        pltpu.VMEM((TOKENS, C), F32),
        pltpu.VMEM((TOKENS, 3 * C), F32),
        pltpu.VMEM((TOKENS, C), BF16),
        pltpu.VMEM((BANDS * SIDE, C), BF16),
        pltpu.VMEM((LEAD, C), BF16),
        pltpu.VMEM((BANDS * SIDE, C), BF16),
        pltpu.VMEM((SIDE, C), BF16),
        pltpu.VMEM((4, C, 256), F32),
        pltpu.VMEM((64, 16, C), F32),
        pltpu.VMEM((64, 16, C), BF16),
        pltpu.VMEM((64, 16, C), BF16),
    ]
    for _, width, _ in PARTS:
        for i, dims in enumerate(((4, 4, 4), (3, 4, 4), (4, 4), (3, 4), (4,), (3,))):
            scratch.append(pltpu.VMEM(dims + (16, width), BF16 if i < 2 else F32))
    copies = 3 + 6 + 10 * len(PARTS)
    return pl.pallas_call(
        sublayer_kernel,
        out_shape=(
            jax.ShapeDtypeStruct((TOKENS, C), BF16),
            jax.ShapeDtypeStruct((4, 3 * C), F32),
            jax.ShapeDtypeStruct((4, C), F32),
            jax.ShapeDtypeStruct((4, 128), F32),
        ),
        in_specs=[hbm, hbm, vmem, hbm, hbm, vmem, vmem, vmem],
        out_specs=(vmem,) * 4,
        scratch_shapes=scratch
        + [
            pltpu.SemaphoreType.DMA((4,)),
            pltpu.SemaphoreType.DMA((copies,)),
            pltpu.SemaphoreType.DMA((copies,)),
        ],
        compiler_params=pltpu.CompilerParams(
            collective_id=1, has_side_effects=True, vmem_limit_bytes=62 * 1024 * 1024
        ),
        name="window_grads",
    )(*args)


def on_device(activations, cotangent, norm_gain, qkv_weight, proj_weight):
    perm = window_order()
    spread = np.zeros((BAND, SIDE), np.float32)
    for r in range(WIN_LAT):
        for c in range(HALF_LON):
            spread[r * COLS + c, r * HALF_LON + c] = 1.0
    grad_input, gqkv, gproj, ggain = sublayer(
        activations.reshape(TOKENS, C),
        cotangent.reshape(TOKENS, C),
        norm_gain.reshape(1, C),
        qkv_weight,
        proj_weight,
        jnp.asarray(perm, BF16),
        jnp.asarray(perm.T, BF16),
        jnp.asarray(spread, BF16),
    )
    return grad_input.reshape(ROWS, COLS, C), gqkv, gproj, ggain[:, 0]


def solution(mesh):
    return jax.shard_map(
        on_device,
        mesh=mesh,
        in_specs=(P("lat", "lon", None), P("lat", "lon", None), P(), P(), P()),
        out_specs=(
            P("lat", "lon", None),
            P(("lat", "lon"), None),
            P(("lat", "lon"), None),
            P(("lat", "lon")),
        ),
        check_vma=False,
    )
```

```python
import math

import jax
import jax.numpy as jnp
import numpy as np
from jax import lax
from jax.experimental import pallas as pl
from jax.experimental.pallas import tpu as pltpu
from jax.sharding import PartitionSpec as P

C = 512
HEADS = 16
HEAD = C // HEADS
WIN_LAT = 6
WIN_LON = 12
SPAN = WIN_LAT * WIN_LON
ROWS = 24
COLS = 48
BANDS = ROWS // WIN_LAT
PER_BAND = COLS // WIN_LON
BAND = WIN_LAT * COLS
TOKENS = ROWS * COLS
HALF_LAT = WIN_LAT // 2
HALF_LON = WIN_LON // 2
SIDE = 48
GROUP = 128 // HEAD
F32 = jnp.float32
BF16 = jnp.bfloat16


def window_order():
    perm = np.zeros((BAND, BAND + SIDE), np.float32)
    for b in range(PER_BAND):
        for r in range(WIN_LAT):
            for c in range(WIN_LON):
                col = WIN_LON * b + HALF_LON + c
                src = r * COLS + col if col < COLS else BAND + r * HALF_LON + col - COLS
                perm[b * SPAN + r * WIN_LON + c, src] = 1.0
    return perm


def nn(a, b):
    return lax.dot_general(a, b, (((1,), (0,)), ((), ())), preferred_element_type=F32)


def nt(a, b):
    return lax.dot_general(a, b, (((1,), (1,)), ((), ())), preferred_element_type=F32)


def tn(a, b):
    return lax.dot_general(a, b, (((0,), (0,)), ((), ())), preferred_element_type=F32)


PARTS = ((0, 256, "zyx"), (256, 128, "xzy"), (384, 128, "yxz"))
MESH = pl.DeviceIdType.MESH
LEAD = HALF_LAT * COLS
PAIR = 2 * SPAN


def place():
    lat, lon = lax.axis_index("lat"), lax.axis_index("lon")
    spot = {"z": lat // 2, "x": (lon // 2) % 2 * 2 + lat % 2, "y": lon // 4}
    return lat, lon, spot, lon % 2


def device_at(spot, core):
    return (spot["z"] * 2 + spot["x"] % 2, spot["y"] * 4 + spot["x"] // 2 * 2 + core)


def along(spot, axis, by):
    return {**spot, axis: (spot[axis] + by) % 4}


def chip_at(at):
    return at["z"] * 16 + at["x"] % 2 * 8 + at["y"] * 2 + at["x"] // 2


def sublayer_kernel(
    own_in, own_cot, gain, wqkv_hbm, wproj_hbm, perm, perm_t, spread,
    out_ref, gqkv_ref, gproj_ref, ggain_ref,
    ext, side, side_out, corner, corner_out, wqkv, wproj,
    normed, inv_std, scaled, cot_win, scaled_t, att_t, qkv, grad_att, att, grad_all,
    out_ext, back_side, top, left, back_corner, grads, mine, theirs, got0,
    *rest,
):
    buffers, (local, send, recv) = rest[:-3], rest[-3:]
    loads = [
        pltpu.make_async_copy(own_in, ext.at[0, pl.ds(0, TOKENS)], local.at[0]),
        pltpu.make_async_copy(own_cot, ext.at[1, pl.ds(0, TOKENS)], local.at[1]),
        pltpu.make_async_copy(wqkv_hbm, wqkv, local.at[2]),
        pltpu.make_async_copy(wproj_hbm, wproj, local.at[3]),
    ]
    for load in loads:
        load.start()

    lat, lon, spot, core = place()
    lats, lons = lax.axis_size("lat"), lax.axis_size("lon")
    sibling = device_at(spot, 1 - core)
    down, up = (lat + 1) % lats, (lat + lats - 1) % lats
    east, west = (lon + 1) % lons, (lon + lons - 1) % lons
    peers = [sibling, (down, lon), (up, lon), (lat, east), (lat, west), (down, east), (up, west)]
    for axis in "xyz":
        peers += [device_at(along(spot, axis, k), core) for k in (1, 2, 3)]
    barrier = pltpu.get_barrier_semaphore()
    for peer in peers:
        pl.semaphore_signal(barrier, inc=1, device_id=peer, device_id_type=MESH)

    count = [0]

    def remote(src, dst, peer):
        i = count[0]
        count[0] += 1
        copy = pltpu.make_async_remote_copy(
            src_ref=src, dst_ref=dst, send_sem=send.at[i], recv_sem=recv.at[i],
            device_id=peer, device_id_type=MESH,
        )
        copy.start()
        return copy

    loads[0].wait()
    loads[1].wait()
    for i in range(2):
        for a in range(BANDS):
            rows = BAND if a < BANDS - 1 else BAND - LEAD
            start = LEAD + a * BAND
            side_out[i, a * SIDE : (a + 1) * SIDE] = tn(
                spread[0:rows], ext[i, start : start + rows]
            ).astype(BF16)
        corner_out[i] = tn(spread[BAND - LEAD :], ext[i, 0:LEAD]).astype(BF16)
    pl.semaphore_wait(barrier, len(peers))
    halo = [
        remote(side_out, side, (lat, west)),
        remote(ext.at[:, pl.ds(0, LEAD)], ext.at[:, pl.ds(TOKENS, LEAD)], (up, lon)),
        remote(corner_out, corner, (up, west)),
    ]

    def forward(pieces):
        gathered = []
        for i in range(2):
            parts = []
            for a, half in pieces:
                start = LEAD + a * BAND
                src = ext[i, start : start + BAND]
                rows = perm[half * PAIR : (half + 1) * PAIR]
                if half == 0:
                    parts.append(nn(rows[:, :BAND], src))
                else:
                    edge = side[i, a * SIDE : (a + 1) * SIDE]
                    if a == BANDS - 1:
                        edge = (edge.astype(F32) + corner[i].astype(F32)).astype(BF16)
                    parts.append(nn(rows, jnp.concatenate([src, edge], axis=0)))
            gathered.append(jnp.concatenate(parts, axis=0))
        x, cot = gathered[0], gathered[1].astype(BF16)
        center = x - jnp.mean(x, axis=-1, keepdims=True)
        inv = lax.rsqrt(jnp.mean(center * center, axis=-1, keepdims=True) + 1e-05)
        norm = center * inv
        sc = (norm * gain[...]).astype(BF16)
        qkv_now = nn(sc, wqkv[...]).astype(BF16).astype(F32)
        att_now = nt(cot, wproj[...]).astype(BF16).astype(F32)
        for i, (a, half) in enumerate(pieces):
            dst = slice(a * BAND + half * PAIR, a * BAND + (half + 1) * PAIR)
            src = slice(i * PAIR, (i + 1) * PAIR)
            normed[dst] = norm[src]
            inv_std[dst] = jnp.broadcast_to(inv[src], (PAIR, 128))
            scaled[dst] = sc[src]
            cot_win[dst] = cot[src]
            qkv[dst] = qkv_now[src]
            grad_att[dst] = att_now[src]

    lane = lax.broadcasted_iota(jnp.int32, (1, 128), 1) // HEAD
    masks = [(lane == j).astype(F32) for j in range(GROUP)]
    key_half = lax.broadcasted_iota(jnp.int32, (SPAN, SPAN), 0) >= HALF_LAT * WIN_LON
    query_half = lax.broadcasted_iota(jnp.int32, (SPAN, SPAN), 1) >= HALF_LAT * WIN_LON
    parted = jnp.where(key_half == query_half, 0.0, -1e30)
    parted = jnp.concatenate([parted] * GROUP, axis=1)

    def stacked(x):
        return jnp.concatenate([x * m for m in masks], axis=0).astype(BF16)

    def by_head(x):
        x = x.reshape(GROUP, SPAN, 128)
        y = x[GROUP - 1]
        for j in range(GROUP - 2, -1, -1):
            y = jnp.where(lane == j, x[j], y)
        return y

    scale = HEAD ** (-0.5)

    def attention(pair):
        edge = jnp.where((lat == lats - 1) & (pair >= (BANDS - 1) * PER_BAND // 2), 1.0, 0.0)
        shut = parted * edge
        todo = []
        for i in range(2):
            rows = pl.ds(pl.multiple_of(pair * PAIR + i * SPAN, 8), SPAN)
            todo += [(rows, [slice(j * C + lo, j * C + lo + 128) for j in range(3)])
                     for lo in range(0, C, 128)]
        q = [stacked(qkv[rows, cols[0]]) for rows, cols in todo]
        k = [qkv[rows, cols[1]].astype(BF16) for rows, cols in todo]
        v = [qkv[rows, cols[2]].astype(BF16) for rows, cols in todo]
        da = [stacked(grad_att[rows, cols[0]]) for rows, cols in todo]
        n = range(len(todo))
        s = [nt(k[i], q[i]) * scale + shut for i in n]
        gp = [nt(v[i], da[i]) for i in n]
        ex = [jnp.exp(x - jnp.max(x, axis=0, keepdims=True)) for x in s]
        prob = [x * (1.0 / jnp.sum(x, axis=0, keepdims=True)) for x in ex]
        inner = [jnp.sum(prob[i] * gp[i], axis=0, keepdims=True) for i in n]
        gs = [(prob[i] * (gp[i] - inner[i]) * scale).astype(BF16) for i in n]
        pb = [x.astype(BF16) for x in prob]
        found = [by_head(tn(pb[i], v[i])) for i in n]
        grad_q = [by_head(tn(gs[i], k[i])) for i in n]
        grad_k = [nn(gs[i], q[i]) for i in n]
        grad_v = [nn(pb[i], da[i]) for i in n]
        for i, (rows, cols) in enumerate(todo):
            att[rows, cols[0]] = found[i]
            grad_all[rows, cols[0]] = grad_q[i]
            grad_all[rows, cols[1]] = grad_k[i]
            grad_all[rows, cols[2]] = grad_v[i]

    loads[2].wait()
    loads[3].wait()
    forward([(a, 0) for a in range(BANDS - 1)])

    def early(i, carry):
        attention(i * 2)
        return carry

    lax.fori_loop(0, BANDS - 1, early, 0)
    for copy in halo:
        copy.wait_recv()
    forward([(a, 1) for a in range(BANDS - 1)])
    forward([(BANDS - 1, 0), (BANDS - 1, 1)])

    def late(i, carry):
        attention(jnp.where(i < BANDS - 1, i * 2 + 1, i + BANDS - 1))
        return carry

    lax.fori_loop(0, BANDS + 1, late, 0)

    scaled_t[...] = scaled[...].T
    att_t[...] = att[...].astype(BF16).T
    upper = lax.broadcasted_iota(jnp.int32, (1, 8, 1), 1) < 4
    first_core = lax.broadcasted_iota(jnp.int32, (1, 8, 1), 1) * 0 + core == 0
    first = []
    for half in range(2):
        lo = half * 256
        lanes = slice(lo, lo + 256)
        for j in range(3):
            cols = slice(j * C + lo, j * C + lo + 256)
            grads[j] = nn(scaled_t[...], grad_all[:, cols].astype(BF16))
        grads[3] = nn(att_t[...], cot_win[:, lanes])

        def pack(i, carry):
            rows = pl.ds(pl.multiple_of(i * 64, 64), 64)
            chips = pl.ds(i * 8, 8)
            t = [grads[j, rows].reshape(8, 8, 256) for j in range(4)]
            turned = [pltpu.roll(x, 4, 1) for x in t]
            block = []
            for near, far in ((t, turned), (turned, t)):
                block.append(
                    jnp.concatenate(
                        [jnp.where(upper, near[j], far[j + 1]) for j in (0, 2)], axis=1
                    )
                )
            is_first = jnp.concatenate([first_core, first_core], axis=1)
            mine[chips, :, lanes] = jnp.where(is_first, block[0], block[1])
            theirs[chips, :, lanes] = jnp.where(is_first, block[1], block[0]).astype(BF16)
            return carry

        lax.fori_loop(0, 8, pack, 0)
        for start, width, _ in PARTS:
            if lo <= start < lo + 256:
                span = pl.ds(start, width)
                first.append(remote(theirs.at[:, :, span], got0.at[:, :, span], sibling))

    back = []

    def backward(a):
        dst = slice(a * BAND, (a + 1) * BAND)
        gn = nt(grad_all[dst].astype(BF16), wqkv[...]) * gain[...]
        norm = normed[dst]
        branch = inv_std[dst][:, 0:1] * (
            gn
            - jnp.mean(gn, axis=-1, keepdims=True)
            - norm * jnp.mean(gn * norm, axis=-1, keepdims=True)
        )
        done = (cot_win[dst].astype(F32) + branch).astype(BF16)
        slab = nn(perm_t[...], done).astype(BF16)
        out_ext[dst] = slab[:BAND]
        edge = slice(a * SIDE, (a + 1) * SIDE)
        back_side[edge] = slab[BAND:]
        edge = pl.ds(a * SIDE, SIDE)
        if a == BANDS - 1:
            back.append(remote(out_ext.at[pl.ds(TOKENS - LEAD, LEAD)], top, (down, lon)))
            back.append(remote(back_side.at[edge], back_corner, (down, east)))
        back.append(remote(back_side.at[edge], left.at[edge], (lat, east)))

    def summed0(p, chip):
        lo, width, _ = PARTS[p]
        lanes = slice(lo, lo + width)
        return mine[chip, :, lanes] + got0[chip, :, lanes].astype(F32)

    sent = [[] for _ in PARTS]

    def stage0(p):
        lo, width, order = PARTS[p]
        held = buffers[6 * p]
        first[p].wait_recv()

        def add(i, carry):
            at = dict(zip(order, (i // 16, i // 4 % 4, i % 4)))
            held[i // 16, i // 4 % 4, i % 4] = summed0(p, chip_at(at)).astype(BF16)
            return carry

        lax.fori_loop(0, 64, add, 0)
        for k in (1, 2, 3):
            peer = along(spot, order[0], k)
            sent[p].append(
                remote(held.at[peer[order[0]]], buffers[6 * p + 1].at[k - 1], device_at(peer, core))
            )

    def stage1(p):
        lo, width, order = PARTS[p]
        got, nxt, nxt_got = buffers[6 * p + 1 : 6 * p + 4]
        for copy in sent[p][-3:]:
            copy.wait_recv()

        def add(i, carry):
            at = dict(zip(order, (spot[order[0]], i // 4, i % 4)))
            total = summed0(p, chip_at(at))
            for k in range(3):
                total = total + got[k, i // 4, i % 4].astype(F32)
            nxt[i // 4, i % 4] = total
            return carry

        lax.fori_loop(0, 16, add, 0)
        for k in (1, 2, 3):
            peer = along(spot, order[1], k)
            sent[p].append(remote(nxt.at[peer[order[1]]], nxt_got.at[k - 1], device_at(peer, core)))

    def stage2(p):
        lo, width, order = PARTS[p]
        held, got, nxt, nxt_got = buffers[6 * p + 2 : 6 * p + 6]
        for copy in sent[p][-3:]:
            copy.wait_recv()
        nxt[...] = held[spot[order[1]]] + got[0] + got[1] + got[2]
        for k in (1, 2, 3):
            peer = along(spot, order[2], k)
            sent[p].append(remote(nxt.at[peer[order[2]]], nxt_got.at[k - 1], device_at(peer, core)))

    def stage3(p):
        lo, width, order = PARTS[p]
        held, got = buffers[6 * p + 4 : 6 * p + 6]
        for copy in sent[p][-3:]:
            copy.wait_recv()
        return held[spot[order[2]]] + got[0] + got[1] + got[2]

    backward(BANDS - 1)
    for p in range(3):
        stage0(p)
    for a in range(BANDS - 1):
        backward(a)
    for p in range(3):
        stage1(p)

    me = lat * lons + lon
    picked = lax.broadcasted_iota(jnp.int32, (8, C), 0) + me * 4
    picked = (picked == lax.broadcasted_iota(jnp.int32, (8, C), 1)).astype(F32)
    w_rows = nn(picked.astype(BF16), wqkv[...])
    gain_rows = jnp.sum(picked * gain[...], axis=1, keepdims=True)

    for copy in back:
        copy.wait_recv()
    for a in range(BANDS):
        edge = nn(spread[...], left[a * SIDE : (a + 1) * SIDE])
        rows = BAND if a < BANDS - 1 else BAND - LEAD
        start = a * BAND
        out_ref[LEAD + start : LEAD + start + rows] = (
            out_ext[start : start + rows].astype(F32) + edge[:rows]
        ).astype(BF16)
    edge = nn(spread[...], back_corner[...])
    out_ref[0:LEAD] = (top[...].astype(F32) + edge[BAND - LEAD :]).astype(BF16)

    for p in range(3):
        stage2(p)
    total = jnp.concatenate([stage3(p) for p in range(3)], axis=1)
    total = total * (1.0 / math.sqrt(TOKENS * lats * lons))
    gqkv = [total[4 * j : 4 * j + 4] for j in range(3)]
    gqkv_ref[...] = jnp.concatenate(gqkv, axis=1)
    gproj_ref[...] = total[12:16]
    dots = jnp.zeros((4, 1), F32)
    for j in range(3):
        dots = dots + jnp.sum(gqkv[j] * w_rows[0:4, j * C : (j + 1) * C], axis=1, keepdims=True)
    dots = dots / gain_rows[0:4]
    ggain_ref[...] = jnp.broadcast_to(dots, (4, 128))
    for copy in halo + first + back + [c for part in sent for c in part]:
        copy.wait_send()


def sublayer(*args):
    vmem = pl.BlockSpec(memory_space=pltpu.VMEM)
    hbm = pl.BlockSpec(memory_space=pl.ANY)
    scratch = [
        pltpu.VMEM((2, TOKENS + LEAD, C), BF16),
        pltpu.VMEM((2, BANDS * SIDE, C), BF16),
        pltpu.VMEM((2, BANDS * SIDE, C), BF16),
        pltpu.VMEM((2, SIDE, C), BF16),
        pltpu.VMEM((2, SIDE, C), BF16),
        pltpu.VMEM((C, 3 * C), BF16),
        pltpu.VMEM((C, C), BF16),
        pltpu.VMEM((TOKENS, C), F32),
        pltpu.VMEM((TOKENS, 128), F32),
        pltpu.VMEM((TOKENS, C), BF16),
        pltpu.VMEM((TOKENS, C), BF16),
        pltpu.VMEM((C, TOKENS), BF16),
        pltpu.VMEM((C, TOKENS), BF16),
        pltpu.VMEM((TOKENS, 3 * C), F32),
        pltpu.VMEM((TOKENS, C), F32),
        pltpu.VMEM((TOKENS, C), F32),
        pltpu.VMEM((TOKENS, 3 * C), F32),
        pltpu.VMEM((TOKENS, C), BF16),
        pltpu.VMEM((BANDS * SIDE, C), BF16),
        pltpu.VMEM((LEAD, C), BF16),
        pltpu.VMEM((BANDS * SIDE, C), BF16),
        pltpu.VMEM((SIDE, C), BF16),
        pltpu.VMEM((4, C, 256), F32),
        pltpu.VMEM((64, 16, C), F32),
        pltpu.VMEM((64, 16, C), BF16),
        pltpu.VMEM((64, 16, C), BF16),
    ]
    for _, width, _ in PARTS:
        for i, dims in enumerate(((4, 4, 4), (3, 4, 4), (4, 4), (3, 4), (4,), (3,))):
            scratch.append(pltpu.VMEM(dims + (16, width), BF16 if i < 2 else F32))
    copies = 3 + 6 + 10 * len(PARTS)
    return pl.pallas_call(
        sublayer_kernel,
        out_shape=(
            jax.ShapeDtypeStruct((TOKENS, C), BF16),
            jax.ShapeDtypeStruct((4, 3 * C), F32),
            jax.ShapeDtypeStruct((4, C), F32),
            jax.ShapeDtypeStruct((4, 128), F32),
        ),
        in_specs=[hbm, hbm, vmem, hbm, hbm, vmem, vmem, vmem],
        out_specs=(vmem,) * 4,
        scratch_shapes=scratch
        + [
            pltpu.SemaphoreType.DMA((4,)),
            pltpu.SemaphoreType.DMA((copies,)),
            pltpu.SemaphoreType.DMA((copies,)),
        ],
        compiler_params=pltpu.CompilerParams(
            collective_id=1, has_side_effects=True, vmem_limit_bytes=62 * 1024 * 1024
        ),
        name="window_grads",
    )(*args)


def on_device(activations, cotangent, norm_gain, qkv_weight, proj_weight):
    perm = window_order()
    spread = np.zeros((BAND, SIDE), np.float32)
    for r in range(WIN_LAT):
        for c in range(HALF_LON):
            spread[r * COLS + c, r * HALF_LON + c] = 1.0
    grad_input, gqkv, gproj, ggain = sublayer(
        activations.reshape(TOKENS, C),
        cotangent.reshape(TOKENS, C),
        norm_gain.reshape(1, C),
        qkv_weight,
        proj_weight,
        jnp.asarray(perm, BF16),
        jnp.asarray(perm.T, BF16),
        jnp.asarray(spread, BF16),
    )
    return grad_input.reshape(ROWS, COLS, C), gqkv, gproj, ggain[:, 0]


def solution(mesh):
    return jax.shard_map(
        on_device,
        mesh=mesh,
        in_specs=(P("lat", "lon", None), P("lat", "lon", None), P(), P(), P()),
        out_specs=(
            P("lat", "lon", None),
            P(("lat", "lon"), None),
            P(("lat", "lon"), None),
            P(("lat", "lon")),
        ),
        check_vma=False,
    )
```

```python
import math

import jax
import jax.numpy as jnp
import numpy as np
from jax import lax
from jax.experimental import pallas as pl
from jax.experimental.pallas import tpu as pltpu
from jax.sharding import PartitionSpec as P

C = 512
HEADS = 16
HEAD = C // HEADS
WIN_LAT = 6
WIN_LON = 12
SPAN = WIN_LAT * WIN_LON
ROWS = 24
COLS = 48
BANDS = ROWS // WIN_LAT
PER_BAND = COLS // WIN_LON
BAND = WIN_LAT * COLS
TOKENS = ROWS * COLS
HALF_LAT = WIN_LAT // 2
HALF_LON = WIN_LON // 2
SIDE = 48
GROUP = 128 // HEAD
F32 = jnp.float32
BF16 = jnp.bfloat16


def window_order():
    perm = np.zeros((BAND, BAND + SIDE), np.float32)
    for b in range(PER_BAND):
        for r in range(WIN_LAT):
            for c in range(WIN_LON):
                col = WIN_LON * b + HALF_LON + c
                src = r * COLS + col if col < COLS else BAND + r * HALF_LON + col - COLS
                perm[b * SPAN + r * WIN_LON + c, src] = 1.0
    return perm


def nn(a, b):
    return lax.dot_general(a, b, (((1,), (0,)), ((), ())), preferred_element_type=F32)


def nt(a, b):
    return lax.dot_general(a, b, (((1,), (1,)), ((), ())), preferred_element_type=F32)


def tn(a, b):
    return lax.dot_general(a, b, (((0,), (0,)), ((), ())), preferred_element_type=F32)


PARTS = ((0, 256, "zyx", "xzy"), (256, 128, "xzy", "yxz"), (384, 128, "yxz", "zyx"))
MESH = pl.DeviceIdType.MESH
LEAD = HALF_LAT * COLS


def place():
    lat, lon = lax.axis_index("lat"), lax.axis_index("lon")
    spot = {"z": lat // 2, "x": (lon // 2) % 2 * 2 + lat % 2, "y": lon // 4}
    return lat, lon, spot, lon % 2


def device_at(spot, core):
    return (spot["z"] * 2 + spot["x"] % 2, spot["y"] * 4 + spot["x"] // 2 * 2 + core)


def chip_at(at):
    return at["z"] * 16 + at["x"] % 2 * 8 + at["y"] * 2 + at["x"] // 2


def sublayer_kernel(
    own_in, own_cot, gain, wqkv_hbm, wproj_hbm, perm, perm_t, spread,
    out_hbm, gqkv_ref, gproj_ref, ggain_ref,
    ext, side, side_out, corner, corner_out, wqkv, wproj,
    normed, inv_std, scaled, cot_win, scaled_t, att_t, qkv, grad_att, att, grad_all,
    out_ext, back_side, top, left, back_corner, grads, mine, theirs, got0,
    out_ref, *rest,
):
    buffers, (local, send, recv) = rest[:-3], rest[-3:]
    loads = [
        pltpu.make_async_copy(own_in, ext.at[0, pl.ds(0, TOKENS)], local.at[0]),
        pltpu.make_async_copy(own_cot, ext.at[1, pl.ds(0, TOKENS)], local.at[1]),
        pltpu.make_async_copy(wqkv_hbm, wqkv, local.at[2]),
        pltpu.make_async_copy(wproj_hbm, wproj, local.at[3]),
    ]
    for load in loads:
        load.start()

    lat, lon, spot, core = place()
    lats, lons = lax.axis_size("lat"), lax.axis_size("lon")
    sibling = device_at(spot, 1 - core)
    down, up = (lat + 1) % lats, (lat + lats - 1) % lats
    east, west = (lon + 1) % lons, (lon + lons - 1) % lons
    peers = [sibling, (down, lon), (up, lon), (lat, east), (lat, west), (down, east), (up, west)]
    for i in range(4):
        for j in range(4):
            for axes in ("xy", "yz", "zx") if i and j else ("x", "y", "z") if i else ():
                if j == 0 or len(axes) == 2:
                    steps = dict(zip(axes, (i, j)))
                    there = {axis: (spot[axis] + steps.get(axis, 0)) % 4 for axis in "xyz"}
                    peers.append(device_at(there, core))
    barrier = pltpu.get_barrier_semaphore()
    for peer in peers:
        pl.semaphore_signal(barrier, inc=1, device_id=peer, device_id_type=MESH)

    count = [0]

    def remote(src, dst, peer):
        i = count[0]
        count[0] += 1
        copy = pltpu.make_async_remote_copy(
            src_ref=src, dst_ref=dst, send_sem=send.at[i], recv_sem=recv.at[i],
            device_id=peer, device_id_type=MESH,
        )
        copy.start()
        return copy

    loads[0].wait()
    loads[1].wait()
    for i in range(2):
        for a in range(BANDS):
            rows = BAND if a < BANDS - 1 else BAND - LEAD
            start = LEAD + a * BAND
            side_out[i, a * SIDE : (a + 1) * SIDE] = tn(
                spread[0:rows], ext[i, start : start + rows]
            ).astype(BF16)
        corner_out[i] = tn(spread[BAND - LEAD :], ext[i, 0:LEAD]).astype(BF16)
    pl.semaphore_wait(barrier, len(peers))
    halo = [
        remote(side_out, side, (lat, west)),
        remote(ext.at[:, pl.ds(0, LEAD)], ext.at[:, pl.ds(TOKENS, LEAD)], (up, lon)),
        remote(corner_out, corner, (up, west)),
    ]

    def forward(pieces):
        gathered = []
        for i in range(2):
            parts = []
            for a, lo, hi in pieces:
                start = LEAD + a * BAND
                src = ext[i, start : start + BAND]
                first_row, last_row = lo // 16 * 16, -(-hi // 16) * 16
                rows = perm[first_row:last_row]
                if hi < BAND:
                    got = nn(rows[:, :BAND], src)
                else:
                    edge = side[i, a * SIDE : (a + 1) * SIDE]
                    if a == BANDS - 1:
                        edge = (edge.astype(F32) + corner[i].astype(F32)).astype(BF16)
                    got = nn(rows, jnp.concatenate([src, edge], axis=0))
                parts.append(got[lo - first_row : hi - first_row])
            gathered.append(jnp.concatenate(parts, axis=0))
        x, cot = gathered
        center = x - jnp.mean(x, axis=-1, keepdims=True)
        inv = lax.rsqrt(jnp.mean(center * center, axis=-1, keepdims=True) + 1e-05)
        norm = center * inv
        sc = norm * gain[...]
        qkv_now = nn(sc.astype(BF16), wqkv[...]).astype(BF16).astype(F32)
        att_now = nt(cot.astype(BF16), wproj[...]).astype(BF16).astype(F32)
        at = 0
        for a, lo, hi in pieces:
            dst = slice(a * BAND + lo, a * BAND + hi)
            src = slice(at, at + hi - lo)
            at += hi - lo
            normed[dst] = norm[src]
            inv_std[dst] = jnp.broadcast_to(inv[src], (hi - lo, 128))
            scaled[dst] = sc[src]
            cot_win[dst] = cot[src]
            qkv[dst] = qkv_now[src]
            grad_att[dst] = att_now[src]

    lane = lax.broadcasted_iota(jnp.int32, (1, 128), 1) // HEAD
    masks = [(lane == j).astype(F32) for j in range(GROUP)]
    key_half = lax.broadcasted_iota(jnp.int32, (SPAN, SPAN), 0) >= HALF_LAT * WIN_LON
    query_half = lax.broadcasted_iota(jnp.int32, (SPAN, SPAN), 1) >= HALF_LAT * WIN_LON
    parted = jnp.where(key_half == query_half, 0.0, -1e30)
    parted = jnp.concatenate([parted] * GROUP, axis=1)

    def stacked(x):
        return jnp.concatenate([x * m for m in masks], axis=0).astype(BF16)

    def by_head(x):
        x = x.reshape(GROUP, SPAN, 128)
        y = x[GROUP - 1]
        for j in range(GROUP - 2, -1, -1):
            y = jnp.where(lane == j, x[j], y)
        return y

    scale = HEAD ** (-0.5)

    def attention(windows, edge=False):
        shut = parted * jnp.where(lat == lats - 1, 1.0, 0.0)
        todo = []
        for w in windows:
            rows = pl.ds(pl.multiple_of(w * SPAN, 8), SPAN)
            todo += [(rows, [slice(j * C + lo, j * C + lo + 128) for j in range(3)])
                     for lo in range(0, C, 128)]
        q = [stacked(qkv[rows, cols[0]]) for rows, cols in todo]
        k = [qkv[rows, cols[1]].astype(BF16) for rows, cols in todo]
        v = [qkv[rows, cols[2]].astype(BF16) for rows, cols in todo]
        da = [stacked(grad_att[rows, cols[0]]) for rows, cols in todo]
        n = range(len(todo))
        s = [nt(k[i], q[i]) * scale for i in n]
        if edge:
            s = [x + shut for x in s]
        gp = [nt(v[i], da[i]) for i in n]
        ex = [jnp.exp(x - jnp.max(x, axis=0, keepdims=True)) for x in s]
        prob = [x * (1.0 / jnp.sum(x, axis=0, keepdims=True)) for x in ex]
        inner = [jnp.sum(prob[i] * gp[i], axis=0, keepdims=True) for i in n]
        gs = [(prob[i] * (gp[i] - inner[i]) * scale).astype(BF16) for i in n]
        pb = [x.astype(BF16) for x in prob]
        found = [by_head(tn(pb[i], v[i])) for i in n]
        grad_q = [by_head(tn(gs[i], k[i])) for i in n]
        grad_k = [nn(gs[i], q[i]) for i in n]
        grad_v = [nn(pb[i], da[i]) for i in n]
        for i, (rows, cols) in enumerate(todo):
            att[rows, cols[0]] = found[i]
            grad_all[rows, cols[0]] = grad_q[i]
            grad_all[rows, cols[1]] = grad_k[i]
            grad_all[rows, cols[2]] = grad_v[i]

    loads[2].wait()
    loads[3].wait()
    inner = (PER_BAND - 1) * SPAN
    forward([(a, 0, inner) for a in range(BANDS - 1)])

    def early(i, carry):
        attention([i * PER_BAND + b for b in range(PER_BAND - 1)])
        return carry

    lax.fori_loop(0, BANDS - 1, early, 0)
    for copy in halo:
        copy.wait_recv()
    forward([(a, inner, BAND) for a in range(BANDS - 1)])
    forward([(BANDS - 1, 0, BAND)])
    attention([a * PER_BAND + PER_BAND - 1 for a in range(BANDS - 1)])

    def late(i, carry):
        attention([(BANDS - 1) * PER_BAND + 2 * i + b for b in range(2)], edge=True)
        return carry

    lax.fori_loop(0, PER_BAND // 2, late, 0)

    scaled_t[...] = scaled[...].astype(BF16).T
    att_t[...] = att[...].astype(BF16).T
    upper = lax.broadcasted_iota(jnp.int32, (1, 8, 1), 1) < 4
    first_core = lax.broadcasted_iota(jnp.int32, (1, 8, 1), 1) * 0 + core == 0
    first = []
    for half in range(2):
        lo = half * 256
        lanes = slice(lo, lo + 256)
        for j in range(3):
            cols = slice(j * C + lo, j * C + lo + 256)
            grads[j] = nn(scaled_t[...], grad_all[:, cols].astype(BF16))
        grads[3] = nn(att_t[...], cot_win[:, lanes].astype(BF16))

        def pack(i, carry):
            rows = pl.ds(pl.multiple_of(i * 64, 64), 64)
            chips = pl.ds(i * 8, 8)
            t = [grads[j, rows].reshape(8, 8, 256) for j in range(4)]
            turned = [pltpu.roll(x, 4, 1) for x in t]
            block = []
            for near, far in ((t, turned), (turned, t)):
                block.append(
                    jnp.concatenate(
                        [jnp.where(upper, near[j], far[j + 1]) for j in (0, 2)], axis=1
                    )
                )
            is_first = jnp.concatenate([first_core, first_core], axis=1)
            mine[chips, :, lanes] = jnp.where(is_first, block[0], block[1])
            theirs[chips, :, lanes] = jnp.where(is_first, block[1], block[0]).astype(BF16)
            return carry

        lax.fori_loop(0, 8, pack, 0)
        for start, width, _, _ in PARTS:
            if lo <= start < lo + 256:
                span = pl.ds(start, width)
                first.append(remote(theirs.at[:, :, span], got0.at[:, :, span], sibling))

    back = []

    def backward(a):
        dst = slice(a * BAND, (a + 1) * BAND)
        gn = nt(grad_all[dst].astype(BF16), wqkv[...]) * gain[...]
        norm = normed[dst]
        branch = inv_std[dst][:, 0:1] * (
            gn
            - jnp.mean(gn, axis=-1, keepdims=True)
            - norm * jnp.mean(gn * norm, axis=-1, keepdims=True)
        )
        done = (cot_win[dst] + branch).astype(BF16)
        slab = nn(perm_t[...], done).astype(BF16)
        out_ext[dst] = slab[:BAND]
        edge = slice(a * SIDE, (a + 1) * SIDE)
        back_side[edge] = slab[BAND:]
        edge = pl.ds(a * SIDE, SIDE)
        if a == BANDS - 1:
            back.append(remote(out_ext.at[pl.ds(TOKENS - LEAD, LEAD)], top, (down, lon)))
            back.append(remote(back_side.at[edge], back_corner, (down, east)))
        back.append(remote(back_side.at[edge], left.at[edge], (lat, east)))

    def role(p, r, axis):
        first_order, second_order = PARTS[p][2:]
        return (1 - core) * int(first_order[r] == axis) + core * int(second_order[r] == axis)

    def by_role(p, steps):
        return {axis: sum(role(p, r, axis) * steps[r] for r in range(3)) for axis in "xyz"}

    def my_role(p, r):
        return sum(role(p, r, axis) * spot[axis] for axis in "xyz")

    def peer_at(p, steps):
        moved = by_role(p, steps)
        return device_at({axis: (spot[axis] + moved[axis]) % 4 for axis in "xyz"}, core)

    def summed0(p, chip):
        lo, width = PARTS[p][:2]
        lanes = slice(lo, lo + width)
        return mine[chip, :, lanes] + got0[chip, :, lanes].astype(F32)

    sent = [[] for _ in PARTS]

    def stage0(p):
        held, got = buffers[5 * p : 5 * p + 2]
        first[p].wait_recv()

        def add(i, carry):
            at = (i // 16, i // 4 % 4, i % 4)
            held[at] = summed0(p, chip_at(by_role(p, at))).astype(BF16)
            return carry

        lax.fori_loop(0, 64, add, 0)
        for k in (2, 1, 3):
            sent[p].append(
                remote(held.at[(my_role(p, 0) + k) % 4], got.at[k - 1], peer_at(p, (k, 0, 0)))
            )

    def stage1(p):
        got, nxt, nxt_got, keep = buffers[5 * p + 1 : 5 * p + 5]
        for copy in sent[p]:
            copy.wait_recv()
        here = my_role(p, 0)
        b, c = my_role(p, 1), my_role(p, 2)

        def total(i, j):
            x = summed0(p, chip_at(by_role(p, (here, i, j))))
            for k in range(3):
                x = x + got[k, i, j].astype(F32)
            return x

        def add(i, carry):
            nxt[i // 4, i % 4] = total(i // 4, i % 4).astype(BF16)
            return carry

        lax.fori_loop(0, 16, add, 0)
        keep[...] = total(b, c)
        for i in (2, 1, 3, 0):
            for j in (2, 1, 3, 0):
                if i or j:
                    sent[p].append(
                        remote(
                            nxt.at[(b + i) % 4, (c + j) % 4],
                            nxt_got.at[4 * i + j - 1],
                            peer_at(p, (0, i, j)),
                        )
                    )

    def stage2(p):
        got, keep = buffers[5 * p + 3 : 5 * p + 5]
        for copy in sent[p][3:]:
            copy.wait_recv()
        x = keep[...]
        for i in range(15):
            x = x + got[i].astype(F32)
        return x

    stage0(0)
    backward(BANDS - 1)
    stage0(1)
    stage0(2)
    for a in range(BANDS - 1):
        backward(a)
    for p in range(3):
        stage1(p)

    me = lat * lons + lon
    picked = lax.broadcasted_iota(jnp.int32, (8, C), 0) + me * 4
    picked = (picked == lax.broadcasted_iota(jnp.int32, (8, C), 1)).astype(F32)
    w_rows = nn(picked.astype(BF16), wqkv[...])
    gain_rows = jnp.sum(picked * gain[...], axis=1, keepdims=True)

    for copy in back:
        copy.wait_recv()
    for a in range(BANDS):
        edge = nn(spread[...], left[a * SIDE : (a + 1) * SIDE])
        rows = BAND if a < BANDS - 1 else BAND - LEAD
        start = a * BAND
        out_ref[LEAD + start : LEAD + start + rows] = (
            out_ext[start : start + rows].astype(F32) + edge[:rows]
        ).astype(BF16)
    edge = nn(spread[...], back_corner[...])
    out_ref[0:LEAD] = (top[...].astype(F32) + edge[BAND - LEAD :]).astype(BF16)
    store = pltpu.make_async_copy(out_ref, out_hbm, local.at[4])
    store.start()

    total = jnp.concatenate([stage2(p) for p in range(3)], axis=1)
    total = total * (1.0 / math.sqrt(TOKENS * lats * lons))
    gqkv = [total[4 * j : 4 * j + 4] for j in range(3)]
    gqkv_ref[...] = jnp.concatenate(gqkv, axis=1)
    gproj_ref[...] = total[12:16]
    dots = jnp.zeros((4, 1), F32)
    for j in range(3):
        dots = dots + jnp.sum(gqkv[j] * w_rows[0:4, j * C : (j + 1) * C], axis=1, keepdims=True)
    dots = dots / gain_rows[0:4]
    diagonal = lax.broadcasted_iota(jnp.int32, (4, 128), 0)
    diagonal = diagonal == lax.broadcasted_iota(jnp.int32, (4, 128), 1)
    ggain_ref[...] = jnp.sum(jnp.where(diagonal, dots, 0.0), axis=0, keepdims=True)
    for copy in halo + first + back + [c for part in sent for c in part]:
        copy.wait_send()
    store.wait()


def sublayer(*args):
    vmem = pl.BlockSpec(memory_space=pltpu.VMEM)
    hbm = pl.BlockSpec(memory_space=pl.ANY)
    scratch = [
        pltpu.VMEM((2, TOKENS + LEAD, C), BF16),
        pltpu.VMEM((2, BANDS * SIDE, C), BF16),
        pltpu.VMEM((2, BANDS * SIDE, C), BF16),
        pltpu.VMEM((2, SIDE, C), BF16),
        pltpu.VMEM((2, SIDE, C), BF16),
        pltpu.VMEM((C, 3 * C), BF16),
        pltpu.VMEM((C, C), BF16),
        pltpu.VMEM((TOKENS, C), F32),
        pltpu.VMEM((TOKENS, 128), F32),
        pltpu.VMEM((TOKENS, C), F32),
        pltpu.VMEM((TOKENS, C), F32),
        pltpu.VMEM((C, TOKENS), BF16),
        pltpu.VMEM((C, TOKENS), BF16),
        pltpu.VMEM((TOKENS, 3 * C), F32),
        pltpu.VMEM((TOKENS, C), F32),
        pltpu.VMEM((TOKENS, C), F32),
        pltpu.VMEM((TOKENS, 3 * C), F32),
        pltpu.VMEM((TOKENS, C), BF16),
        pltpu.VMEM((BANDS * SIDE, C), BF16),
        pltpu.VMEM((LEAD, C), BF16),
        pltpu.VMEM((BANDS * SIDE, C), BF16),
        pltpu.VMEM((SIDE, C), BF16),
        pltpu.VMEM((4, C, 256), F32),
        pltpu.VMEM((64, 16, C), F32),
        pltpu.VMEM((64, 16, C), BF16),
        pltpu.VMEM((64, 16, C), BF16),
        pltpu.VMEM((TOKENS, C), BF16),
    ]
    for _, width, _, _ in PARTS:
        for dims in ((4, 4, 4), (3, 4, 4), (4, 4), (15,)):
            scratch.append(pltpu.VMEM(dims + (16, width), BF16))
        scratch.append(pltpu.VMEM((16, width), F32))
    copies = 3 + 6 + 19 * len(PARTS)
    return pl.pallas_call(
        sublayer_kernel,
        out_shape=(
            jax.ShapeDtypeStruct((TOKENS, C), BF16),
            jax.ShapeDtypeStruct((4, 3 * C), F32),
            jax.ShapeDtypeStruct((4, C), F32),
            jax.ShapeDtypeStruct((1, 128), F32),
        ),
        in_specs=[hbm, hbm, vmem, hbm, hbm, vmem, vmem, vmem],
        out_specs=(hbm, vmem, vmem, vmem),
        scratch_shapes=scratch
        + [
            pltpu.SemaphoreType.DMA((5,)),
            pltpu.SemaphoreType.DMA((copies,)),
            pltpu.SemaphoreType.DMA((copies,)),
        ],
        compiler_params=pltpu.CompilerParams(
            collective_id=1, has_side_effects=True, vmem_limit_bytes=62 * 1024 * 1024
        ),
        name="window_grads",
    )(*args)


def hand_on_kernel(out_ref, gqkv_ref, gproj_ref, gain_ref, out, gqkv, gproj, ggain, sem):
    copy = pltpu.make_async_copy(out_ref, out, sem)
    copy.start()
    gqkv[...] = gqkv_ref[...]
    gproj[...] = gproj_ref[...]
    ggain[...] = gain_ref[0, 0:4]
    copy.wait()


def hand_on(*args):
    vmem = pl.BlockSpec(memory_space=pltpu.VMEM)
    return pl.pallas_call(
        hand_on_kernel,
        out_shape=(
            jax.ShapeDtypeStruct((TOKENS, C), BF16),
            jax.ShapeDtypeStruct((4, 3 * C), F32),
            jax.ShapeDtypeStruct((4, C), F32),
            jax.ShapeDtypeStruct((4,), F32),
        ),
        in_specs=[vmem] * 4,
        out_specs=(pl.BlockSpec(memory_space=pl.ANY), vmem, vmem, vmem),
        scratch_shapes=[pltpu.SemaphoreType.DMA],
        name="hand_on",
    )(*args)


def on_device(activations, cotangent, norm_gain, qkv_weight, proj_weight):
    perm = window_order()
    spread = np.zeros((BAND, SIDE), np.float32)
    for r in range(WIN_LAT):
        for c in range(HALF_LON):
            spread[r * COLS + c, r * HALF_LON + c] = 1.0
    results = sublayer(
        activations.reshape(TOKENS, C),
        cotangent.reshape(TOKENS, C),
        norm_gain.reshape(1, C),
        qkv_weight,
        proj_weight,
        jnp.asarray(perm, BF16),
        jnp.asarray(perm.T, BF16),
        jnp.asarray(spread, BF16),
    )
    grad_input, gqkv, gproj, ggain = hand_on(*results)
    return grad_input.reshape(ROWS, COLS, C), gqkv, gproj, ggain


def solution(mesh):
    return jax.shard_map(
        on_device,
        mesh=mesh,
        in_specs=(P("lat", "lon", None), P("lat", "lon", None), P(), P(), P()),
        out_specs=(
            P("lat", "lon", None),
            P(("lat", "lon"), None),
            P(("lat", "lon"), None),
            P(("lat", "lon")),
        ),
        check_vma=False,
    )
```

```python
import math

import jax
import jax.numpy as jnp
import numpy as np
from jax import lax
from jax.experimental import pallas as pl
from jax.experimental.pallas import tpu as pltpu
from jax.sharding import PartitionSpec as P

C = 512
HEADS = 16
HEAD = C // HEADS
WIN_LAT = 6
WIN_LON = 12
SPAN = WIN_LAT * WIN_LON
ROWS = 24
COLS = 48
BANDS = ROWS // WIN_LAT
PER_BAND = COLS // WIN_LON
BAND = WIN_LAT * COLS
TOKENS = ROWS * COLS
HALF_LAT = WIN_LAT // 2
HALF_LON = WIN_LON // 2
SIDE = 128
EDGE = SIDE + 32
LAST = 208
GROUP = 128 // HEAD
F32 = jnp.float32
BF16 = jnp.bfloat16


def orders():
    perm = np.zeros((BAND, BAND), np.float32)
    beside = np.zeros((BANDS, BAND - LAST, EDGE), np.float32)
    pick = np.zeros((EDGE, TOKENS), np.float32)
    for b in range(PER_BAND):
        for r in range(WIN_LAT):
            for c in range(WIN_LON):
                col = WIN_LON * b + HALF_LON + c
                token = b * SPAN + r * WIN_LON + c
                if col < COLS:
                    perm[token, r * COLS + col] = 1.0
                    continue
                for a in range(BANDS):
                    beside[a, token - LAST, edge_row(a * WIN_LAT + HALF_LAT + r, col - COLS)] = 1.0
    for row in range(ROWS):
        for c in range(HALF_LON):
            pick[edge_row(row + (ROWS if row < HALF_LAT else 0), c), row * COLS + c] = 1.0
    return [jnp.asarray(x, BF16) for x in (perm, perm.T, beside, beside.transpose(0, 2, 1), pick, pick.T)]


def edge_row(row, col):
    if row < ROWS:
        return (row - HALF_LAT) * HALF_LON + col
    return SIDE + (row - ROWS) * HALF_LON + col


def nn(a, b):
    return lax.dot_general(a, b, (((1,), (0,)), ((), ())), preferred_element_type=F32)


def nt(a, b):
    return lax.dot_general(a, b, (((1,), (1,)), ((), ())), preferred_element_type=F32)


def tn(a, b):
    return lax.dot_general(a, b, (((0,), (0,)), ((), ())), preferred_element_type=F32)


PARTS = ((0, 256, "zyx"), (256, 256, "yxz"))
MESH = pl.DeviceIdType.MESH
LEAD = HALF_LAT * COLS


def place():
    lat, lon = lax.axis_index("lat"), lax.axis_index("lon")
    spot = {"z": lat // 2, "x": (lon // 2) % 2 * 2 + lat % 2, "y": lon // 4}
    return lat, lon, spot, lon % 2


def device_at(spot, core):
    return (spot["z"] * 2 + spot["x"] % 2, spot["y"] * 4 + spot["x"] // 2 * 2 + core)


def chip_at(at):
    return at["z"] * 16 + at["x"] % 2 * 8 + at["y"] * 2 + at["x"] // 2


def sublayer_kernel(
    own_in, own_cot, gain, wqkv_hbm, wproj_hbm, perm, perm_t_hbm, beside, beside_t, pick, pick_t_hbm,
    out_hbm, gqkv_ref, gproj_ref, ggain_ref,
    ext, side, side_out, wqkv, wproj, perm_t, pick_t,
    normed, inv_std, scaled, cot_win, qkv, grad_att, att, grad_all,
    out_ext, back_side, top, left, grads, mine, theirs, got0,
    out_ref, *rest,
):
    buffers, (local, send, recv) = rest[:-3], rest[-3:]
    loads = [
        pltpu.make_async_copy(own_in, ext.at[0, pl.ds(0, TOKENS)], local.at[0]),
        pltpu.make_async_copy(own_cot, ext.at[1, pl.ds(0, TOKENS)], local.at[1]),
        pltpu.make_async_copy(wqkv_hbm, wqkv, local.at[2]),
        pltpu.make_async_copy(wproj_hbm, wproj, local.at[3]),
        pltpu.make_async_copy(perm_t_hbm, perm_t, local.at[5]),
        pltpu.make_async_copy(pick_t_hbm, pick_t, local.at[6]),
    ]
    for load in loads:
        load.start()

    lat, lon, spot, core = place()
    lats, lons = lax.axis_size("lat"), lax.axis_size("lon")
    sibling = device_at(spot, 1 - core)
    down, up = (lat + 1) % lats, (lat + lats - 1) % lats
    east, west = (lon + 1) % lons, (lon + lons - 1) % lons
    peers = [sibling, (down, lon), (up, lon), (lat, east), (lat, west), (down, east), (up, west)]
    for axes in ("xy", "xz"):
        for i in range(4):
            for j in range(4):
                if (i or j) and (j or axes == "xy"):
                    there = {axis: spot[axis] for axis in "xyz"}
                    there[axes[0]] = (spot[axes[0]] + i) % 4
                    there[axes[1]] = (spot[axes[1]] + j) % 4
                    peers.append(device_at(there, core))
    barrier = pltpu.get_barrier_semaphore()
    for peer in peers:
        pl.semaphore_signal(barrier, inc=1, device_id=peer, device_id_type=MESH)

    count = [0]

    def remote(src, dst, peer):
        i = count[0]
        count[0] += 1
        copy = pltpu.make_async_remote_copy(
            src_ref=src, dst_ref=dst, send_sem=send.at[i], recv_sem=recv.at[i],
            device_id=peer, device_id_type=MESH,
        )
        copy.start()
        return copy

    loads[0].wait()
    loads[1].wait()
    for i in range(2):
        side_out[i] = nn(pick[...], ext[i, 0:TOKENS]).astype(BF16)
    pl.semaphore_wait(barrier, len(peers))
    main, angle = pl.ds(0, SIDE), pl.ds(SIDE, EDGE - SIDE)
    halo = [
        remote(ext.at[:, pl.ds(0, LEAD)], ext.at[:, pl.ds(TOKENS, LEAD)], (up, lon)),
        remote(side_out.at[:, main], side.at[:, main], (lat, west)),
        remote(side_out.at[:, angle], side.at[:, angle], (up, west)),
    ]

    def forward(pieces):
        gathered = []
        for i in range(2):
            parts = []
            for a, lo, hi in pieces:
                start = LEAD + a * BAND
                src = ext[i, start : start + BAND]
                first_row, last_row = lo // 16 * 16, -(-hi // 16) * 16
                got = nn(perm[first_row:last_row], src)[lo - first_row : hi - first_row]
                if hi == BAND:
                    edge = nn(beside[a], side[i])
                    if lo < LAST:
                        got = jnp.concatenate([got[: LAST - lo], got[LAST - lo :] + edge], axis=0)
                    else:
                        got = got + edge[lo - LAST :]
                parts.append(got)
            gathered.append(jnp.concatenate(parts, axis=0))
        x, cot = gathered
        center = x - jnp.mean(x, axis=-1, keepdims=True)
        inv = lax.rsqrt(jnp.mean(center * center, axis=-1, keepdims=True) + 1e-05)
        norm = center * inv
        sc = norm * gain[...]
        qkv_now = nn(sc.astype(BF16), wqkv[...]).astype(BF16).astype(F32)
        att_now = nt(cot.astype(BF16), wproj[...]).astype(BF16).astype(F32)
        at = 0
        for a, lo, hi in pieces:
            dst = slice(a * BAND + lo, a * BAND + hi)
            src = slice(at, at + hi - lo)
            at += hi - lo
            normed[dst] = norm[src]
            inv_std[dst] = jnp.broadcast_to(inv[src], (hi - lo, 128))
            scaled[dst] = sc[src]
            cot_win[dst] = cot[src]
            qkv[dst] = qkv_now[src]
            grad_att[dst] = att_now[src]

    lane = lax.broadcasted_iota(jnp.int32, (1, 128), 1) // HEAD
    masks = [(lane == j).astype(F32) for j in range(GROUP)]
    key_half = lax.broadcasted_iota(jnp.int32, (SPAN, SPAN), 0) >= HALF_LAT * WIN_LON
    query_half = lax.broadcasted_iota(jnp.int32, (SPAN, SPAN), 1) >= HALF_LAT * WIN_LON
    parted = jnp.where(key_half == query_half, 0.0, -1e30)
    parted = jnp.concatenate([parted] * GROUP, axis=1)

    def stacked(x):
        return jnp.concatenate([x * m for m in masks], axis=0).astype(BF16)

    def by_head(x):
        x = x.reshape(GROUP, SPAN, 128)
        y = x[GROUP - 1]
        for j in range(GROUP - 2, -1, -1):
            y = jnp.where(lane == j, x[j], y)
        return y

    scale = HEAD ** (-0.5)

    def attention(windows, edge=False):
        shut = parted * jnp.where(lat == lats - 1, 1.0, 0.0)
        todo = []
        for w in windows:
            rows = pl.ds(pl.multiple_of(w * SPAN, 8), SPAN)
            todo += [(rows, [slice(j * C + lo, j * C + lo + 128) for j in range(3)])
                     for lo in range(0, C, 128)]
        q = [stacked(qkv[rows, cols[0]]) for rows, cols in todo]
        k = [qkv[rows, cols[1]].astype(BF16) for rows, cols in todo]
        v = [qkv[rows, cols[2]].astype(BF16) for rows, cols in todo]
        da = [stacked(grad_att[rows, cols[0]]) for rows, cols in todo]
        n = range(len(todo))
        s = [nt(k[i], q[i]) * scale for i in n]
        if edge:
            s = [x + shut for x in s]
        gp = [nt(v[i], da[i]) for i in n]
        ex = [jnp.exp(x - jnp.max(x, axis=0, keepdims=True)) for x in s]
        prob = [x * (1.0 / jnp.sum(x, axis=0, keepdims=True)) for x in ex]
        inner = [jnp.sum(prob[i] * gp[i], axis=0, keepdims=True) for i in n]
        gs = [(prob[i] * (gp[i] - inner[i]) * scale).astype(BF16) for i in n]
        pb = [x.astype(BF16) for x in prob]
        found = [by_head(tn(pb[i], v[i])) for i in n]
        grad_q = [by_head(tn(gs[i], k[i])) for i in n]
        grad_k = [nn(gs[i], q[i]) for i in n]
        grad_v = [nn(pb[i], da[i]) for i in n]
        for i, (rows, cols) in enumerate(todo):
            att[rows, cols[0]] = found[i]
            grad_all[rows, cols[0]] = grad_q[i]
            grad_all[rows, cols[1]] = grad_k[i]
            grad_all[rows, cols[2]] = grad_v[i]

    loads[2].wait()
    loads[3].wait()
    inner = (PER_BAND - 1) * SPAN
    forward([(a, 0, inner) for a in range(BANDS - 1)])

    def early(i, carry):
        attention([i * PER_BAND + b for b in range(PER_BAND - 1)])
        return carry

    lax.fori_loop(0, BANDS - 1, early, 0)
    def weight_sums(pieces, halves, found):
        def tokens(ref, cols):
            parts = [ref[lo:hi, cols] for lo, hi in pieces]
            return jnp.concatenate(parts, axis=0).astype(BF16)

        if not found:
            found += [tokens(scaled, slice(0, C)).T, tokens(att, slice(0, C)).T]
        for half in halves:
            lo = half * 256
            for j in range(3):
                yield 4 * half + j, nn(found[0], tokens(grad_all, slice(j * C + lo, j * C + lo + 256)))
            yield 4 * half + 3, nn(found[1], tokens(cot_win, slice(lo, lo + 256)))

    starts = [a * BAND for a in range(BANDS - 1)]
    for i, value in weight_sums([(start, start + inner) for start in starts], (0, 1), []):
        grads[i] = value
    for copy in halo:
        copy.wait_recv()
    forward([(a, inner, BAND) for a in range(BANDS - 1)])
    forward([(BANDS - 1, 0, BAND)])
    attention([a * PER_BAND + PER_BAND - 1 for a in range(BANDS - 1)])

    def late(i, carry):
        attention([(BANDS - 1) * PER_BAND + 2 * i + b for b in range(2)], edge=True)
        return carry

    lax.fori_loop(0, PER_BAND // 2, late, 0)

    late_rows = [(start + inner, start + BAND) for start in starts] + [(TOKENS - BAND, TOKENS)]
    turned_once = []
    upper = lax.broadcasted_iota(jnp.int32, (1, 8, 1), 1) < 4
    first_core = lax.broadcasted_iota(jnp.int32, (1, 8, 1), 1) * 0 + core == 0
    first = []
    for half in range(2):
        lo = half * 256
        lanes = slice(lo, lo + 256)
        for i, value in weight_sums(late_rows, (half,), turned_once):
            grads[i] += value

        def pack(i, carry):
            rows = pl.ds(pl.multiple_of(i * 64, 64), 64)
            chips = pl.ds(i * 8, 8)
            t = [grads[4 * half + j, rows].reshape(8, 8, 256) for j in range(4)]
            turned = [pltpu.roll(x, 4, 1) for x in t]
            block = []
            for near, far in ((t, turned), (turned, t)):
                block.append(
                    jnp.concatenate(
                        [jnp.where(upper, near[j], far[j + 1]) for j in (0, 2)], axis=1
                    )
                )
            is_first = jnp.concatenate([first_core, first_core], axis=1)
            mine[chips, :, lanes] = jnp.where(is_first, block[0], block[1])
            theirs[chips, :, lanes] = jnp.where(is_first, block[1], block[0]).astype(BF16)
            return carry

        lax.fori_loop(0, 8, pack, 0)
        for start, width, _ in PARTS:
            if lo <= start < lo + 256:
                span = pl.ds(start, width)
                first.append(remote(theirs.at[:, :, span], got0.at[:, :, span], sibling))

    back, edges = [], []
    loads[4].wait()
    loads[5].wait()

    def backward(a):
        dst = slice(a * BAND, (a + 1) * BAND)
        gn = nt(grad_all[dst].astype(BF16), wqkv[...]) * gain[...]
        norm = normed[dst]
        branch = inv_std[dst][:, 0:1] * (
            gn
            - jnp.mean(gn, axis=-1, keepdims=True)
            - norm * jnp.mean(gn * norm, axis=-1, keepdims=True)
        )
        done = (cot_win[dst] + branch).astype(BF16)
        out_ext[dst] = nn(perm_t[...], done).astype(BF16)
        edges.append(nn(beside_t[a], done[LAST:]))
        if a == BANDS - 1:
            back.append(remote(out_ext.at[pl.ds(TOKENS - LEAD, LEAD)], top, (down, lon)))
        if len(edges) == BANDS:
            back_side[...] = (edges[0] + edges[1] + edges[2] + edges[3]).astype(BF16)
            back.append(remote(back_side.at[main], left.at[main], (lat, east)))
            back.append(remote(back_side.at[angle], left.at[angle], (down, east)))

    def by_role(p, steps):
        return dict(zip(PARTS[p][2], steps))

    def my_role(p, r):
        return spot[PARTS[p][2][r]]

    def peer_at(p, steps):
        moved = by_role(p, steps)
        return device_at({axis: (spot[axis] + moved[axis]) % 4 for axis in "xyz"}, core)

    def summed0(p, chip):
        lo, width = PARTS[p][:2]
        lanes = slice(lo, lo + width)
        return mine[chip, :, lanes] + got0[chip, :, lanes].astype(F32)

    sent = [[] for _ in PARTS]

    def stage0(p):
        held, got = buffers[5 * p : 5 * p + 2]
        first[p].wait_recv()

        def add(i, carry):
            at = (i // 16, i // 4 % 4, i % 4)
            held[at] = summed0(p, chip_at(by_role(p, at))).astype(BF16)
            return carry

        lax.fori_loop(0, 64, add, 0)
        for k in (2, 1, 3):
            sent[p].append(
                remote(held.at[(my_role(p, 0) + k) % 4], got.at[k - 1], peer_at(p, (k, 0, 0)))
            )

    def stage1(p):
        got, nxt, nxt_got, keep = buffers[5 * p + 1 : 5 * p + 5]
        for copy in sent[p]:
            copy.wait_recv()
        here = my_role(p, 0)
        b, c = my_role(p, 1), my_role(p, 2)

        def total(i, j):
            x = summed0(p, chip_at(by_role(p, (here, i, j))))
            for k in range(3):
                x = x + got[k, i, j].astype(F32)
            return x

        def add(i, carry):
            nxt[i // 4, i % 4] = total(i // 4, i % 4).astype(BF16)
            return carry

        lax.fori_loop(0, 16, add, 0)
        keep[...] = total(b, c)
        for i in (2, 1, 3, 0):
            for j in (2, 1, 3, 0):
                if i or j:
                    sent[p].append(
                        remote(
                            nxt.at[(b + i) % 4, (c + j) % 4],
                            nxt_got.at[4 * i + j - 1],
                            peer_at(p, (0, i, j)),
                        )
                    )

    def stage2(p):
        got, keep = buffers[5 * p + 3 : 5 * p + 5]
        for copy in sent[p][3:]:
            copy.wait_recv()
        x = keep[...]
        for i in range(15):
            x = x + got[i].astype(F32)
        return x

    stage0(0)
    backward(BANDS - 1)
    stage0(1)
    for a in range(BANDS - 1):
        backward(a)
    for p in range(len(PARTS)):
        stage1(p)

    me = lat * lons + lon
    picked = lax.broadcasted_iota(jnp.int32, (8, C), 0) + me * 4
    picked = (picked == lax.broadcasted_iota(jnp.int32, (8, C), 1)).astype(F32)
    w_rows = nn(picked.astype(BF16), wqkv[...])
    gain_rows = jnp.sum(picked * gain[...], axis=1, keepdims=True)

    for copy in back:
        copy.wait_recv()
    out_ref[LEAD:] = (
        out_ext[0 : TOKENS - LEAD].astype(F32) + nn(pick_t[LEAD:, 0:SIDE], left[0:SIDE])
    ).astype(BF16)
    out_ref[0:LEAD] = (top[...].astype(F32) + nn(pick_t[0:LEAD], left[...])).astype(BF16)
    store = pltpu.make_async_copy(out_ref, out_hbm, local.at[4])
    store.start()

    total = jnp.concatenate([stage2(p) for p in range(len(PARTS))], axis=1)
    total = total * (1.0 / math.sqrt(TOKENS * lats * lons))
    gqkv = [total[4 * j : 4 * j + 4] for j in range(3)]
    gqkv_ref[...] = jnp.concatenate(gqkv, axis=1)
    gproj_ref[...] = total[12:16]
    dots = jnp.zeros((4, 1), F32)
    for j in range(3):
        dots = dots + jnp.sum(gqkv[j] * w_rows[0:4, j * C : (j + 1) * C], axis=1, keepdims=True)
    dots = dots / gain_rows[0:4]
    diagonal = lax.broadcasted_iota(jnp.int32, (4, 128), 0)
    diagonal = diagonal == lax.broadcasted_iota(jnp.int32, (4, 128), 1)
    ggain_ref[...] = jnp.sum(jnp.where(diagonal, dots, 0.0), axis=0, keepdims=True)
    for copy in halo + first + back + [c for part in sent for c in part]:
        copy.wait_send()
    store.wait()


def sublayer(*args):
    vmem = pl.BlockSpec(memory_space=pltpu.VMEM)
    hbm = pl.BlockSpec(memory_space=pl.ANY)
    scratch = [
        pltpu.VMEM((2, TOKENS + LEAD, C), BF16),
        pltpu.VMEM((2, EDGE, C), BF16),
        pltpu.VMEM((2, EDGE, C), BF16),
        pltpu.VMEM((C, 3 * C), BF16),
        pltpu.VMEM((C, C), BF16),
        pltpu.VMEM((BAND, BAND), BF16),
        pltpu.VMEM((TOKENS, EDGE), BF16),
        pltpu.VMEM((TOKENS, C), F32),
        pltpu.VMEM((TOKENS, 128), F32),
        pltpu.VMEM((TOKENS, C), F32),
        pltpu.VMEM((TOKENS, C), F32),
        pltpu.VMEM((TOKENS, 3 * C), F32),
        pltpu.VMEM((TOKENS, C), F32),
        pltpu.VMEM((TOKENS, C), F32),
        pltpu.VMEM((TOKENS, 3 * C), F32),
        pltpu.VMEM((TOKENS, C), BF16),
        pltpu.VMEM((EDGE, C), BF16),
        pltpu.VMEM((LEAD, C), BF16),
        pltpu.VMEM((EDGE, C), BF16),
        pltpu.VMEM((8, C, 256), F32),
        pltpu.VMEM((64, 16, C), F32),
        pltpu.VMEM((64, 16, C), BF16),
        pltpu.VMEM((64, 16, C), BF16),
        pltpu.VMEM((TOKENS, C), BF16),
    ]
    for _, width, _ in PARTS:
        for dims in ((4, 4, 4), (3, 4, 4), (4, 4), (15,)):
            scratch.append(pltpu.VMEM(dims + (16, width), BF16))
        scratch.append(pltpu.VMEM((16, width), F32))
    copies = 3 + 3 + 19 * len(PARTS)
    return pl.pallas_call(
        sublayer_kernel,
        out_shape=(
            jax.ShapeDtypeStruct((TOKENS, C), BF16),
            jax.ShapeDtypeStruct((4, 3 * C), F32),
            jax.ShapeDtypeStruct((4, C), F32),
            jax.ShapeDtypeStruct((1, 128), F32),
        ),
        in_specs=[hbm, hbm, vmem, hbm, hbm, vmem, hbm, vmem, vmem, vmem, hbm],
        out_specs=(hbm, vmem, vmem, vmem),
        scratch_shapes=scratch
        + [
            pltpu.SemaphoreType.DMA((7,)),
            pltpu.SemaphoreType.DMA((copies,)),
            pltpu.SemaphoreType.DMA((copies,)),
        ],
        compiler_params=pltpu.CompilerParams(
            collective_id=1, has_side_effects=True, vmem_limit_bytes=62 * 1024 * 1024
        ),
        name="window_grads",
    )(*args)


def hand_on_kernel(out_ref, gqkv_ref, gproj_ref, gain_ref, out, gqkv, gproj, ggain):
    out[...] = out_ref[...]
    gqkv[...] = gqkv_ref[...]
    gproj[...] = gproj_ref[...]
    ggain[...] = gain_ref[0, 0:4]


def hand_on(*args):
    def whole(*shape):
        return pl.BlockSpec(shape, lambda i: (0,) * len(shape))

    tokens = pl.BlockSpec((TOKENS // 2, C), lambda i: (i, 0))
    return pl.pallas_call(
        hand_on_kernel,
        grid=(2,),
        out_shape=(
            jax.ShapeDtypeStruct((TOKENS, C), BF16),
            jax.ShapeDtypeStruct((4, 3 * C), F32),
            jax.ShapeDtypeStruct((4, C), F32),
            jax.ShapeDtypeStruct((4,), F32),
        ),
        in_specs=[tokens, whole(4, 3 * C), whole(4, C), whole(1, 128)],
        out_specs=(tokens, whole(4, 3 * C), whole(4, C), whole(4)),
        compiler_params=pltpu.CompilerParams(vmem_limit_bytes=62 * 1024 * 1024),
        name="hand_on",
    )(*args)


def on_device(activations, cotangent, norm_gain, qkv_weight, proj_weight):
    results = sublayer(
        activations.reshape(TOKENS, C),
        cotangent.reshape(TOKENS, C),
        norm_gain.reshape(1, C),
        qkv_weight,
        proj_weight,
        *orders(),
    )
    grad_input, gqkv, gproj, ggain = hand_on(*results)
    return grad_input.reshape(ROWS, COLS, C), gqkv, gproj, ggain


def solution(mesh):
    return jax.shard_map(
        on_device,
        mesh=mesh,
        in_specs=(P("lat", "lon", None), P("lat", "lon", None), P(), P(), P()),
        out_specs=(
            P("lat", "lon", None),
            P(("lat", "lon"), None),
            P(("lat", "lon"), None),
            P(("lat", "lon")),
        ),
        check_vma=False,
    )
```

```python
import math

import jax
import jax.numpy as jnp
import numpy as np
from jax import lax
from jax.experimental import pallas as pl
from jax.experimental.pallas import tpu as pltpu
from jax.sharding import PartitionSpec as P

C = 512
HEADS = 16
HEAD = C // HEADS
WIN_LAT = 6
WIN_LON = 12
SPAN = WIN_LAT * WIN_LON
ROWS = 24
COLS = 48
BANDS = ROWS // WIN_LAT
PER_BAND = COLS // WIN_LON
BAND = WIN_LAT * COLS
TOKENS = ROWS * COLS
HALF_LAT = WIN_LAT // 2
HALF_LON = WIN_LON // 2
SIDE = 128
EDGE = SIDE + 32
LAST = 208
GROUP = 128 // HEAD
F32 = jnp.float32
BF16 = jnp.bfloat16


def orders():
    perm = np.zeros((BAND, BAND), np.float32)
    beside = np.zeros((BANDS, BAND - LAST, EDGE), np.float32)
    pick = np.zeros((EDGE, TOKENS), np.float32)
    for b in range(PER_BAND):
        for r in range(WIN_LAT):
            for c in range(WIN_LON):
                col = WIN_LON * b + HALF_LON + c
                token = b * SPAN + r * WIN_LON + c
                if col < COLS:
                    perm[token, r * COLS + col] = 1.0
                    continue
                for a in range(BANDS):
                    beside[a, token - LAST, edge_row(a * WIN_LAT + HALF_LAT + r, col - COLS)] = 1.0
    for row in range(ROWS):
        for c in range(HALF_LON):
            pick[edge_row(row + (ROWS if row < HALF_LAT else 0), c), row * COLS + c] = 1.0
    return [jnp.asarray(x, BF16) for x in (perm, perm.T, beside, beside.transpose(0, 2, 1), pick, pick.T)]


def edge_row(row, col):
    if row < ROWS:
        return (row - HALF_LAT) * HALF_LON + col
    return SIDE + (row - ROWS) * HALF_LON + col


def nn(a, b):
    return lax.dot_general(a, b, (((1,), (0,)), ((), ())), preferred_element_type=F32)


def nt(a, b):
    return lax.dot_general(a, b, (((1,), (1,)), ((), ())), preferred_element_type=F32)


def tn(a, b):
    return lax.dot_general(a, b, (((0,), (0,)), ((), ())), preferred_element_type=F32)


PARTS = ((0, 256, "zyx"), (256, 256, "yxz"))
MESH = pl.DeviceIdType.MESH
LEAD = HALF_LAT * COLS


def place():
    lat, lon = lax.axis_index("lat"), lax.axis_index("lon")
    spot = {"z": lat // 2, "x": (lon // 2) % 2 * 2 + lat % 2, "y": lon // 4}
    return lat, lon, spot, lon % 2


def device_at(spot, core):
    return (spot["z"] * 2 + spot["x"] % 2, spot["y"] * 4 + spot["x"] // 2 * 2 + core)


def chip_at(at):
    return at["z"] * 16 + at["x"] % 2 * 8 + at["y"] * 2 + at["x"] // 2


def sublayer_kernel(
    own_in, own_cot, gain, wqkv_hbm, wproj_hbm, perm, perm_t_hbm, beside, beside_t, pick, pick_t_hbm,
    out_hbm, gqkv_ref, gproj_ref, ggain_ref,
    ext, side, side_out, wqkv, wproj, perm_t, pick_t,
    normed, inv_std, scaled, cot_win, qkv, grad_att, att, grad_all,
    out_ext, back_side, top, left, grads, mine, theirs, got0,
    out_ref, *rest,
):
    buffers, (local, send, recv) = rest[:-3], rest[-3:]
    loads = [
        pltpu.make_async_copy(own_in, ext.at[0, pl.ds(0, TOKENS)], local.at[0]),
        pltpu.make_async_copy(own_cot, ext.at[1, pl.ds(0, TOKENS)], local.at[1]),
        pltpu.make_async_copy(wqkv_hbm, wqkv, local.at[2]),
        pltpu.make_async_copy(wproj_hbm, wproj, local.at[3]),
        pltpu.make_async_copy(perm_t_hbm, perm_t, local.at[5]),
        pltpu.make_async_copy(pick_t_hbm, pick_t, local.at[6]),
    ]
    for load in loads:
        load.start()

    lat, lon, spot, core = place()
    lats, lons = lax.axis_size("lat"), lax.axis_size("lon")
    sibling = device_at(spot, 1 - core)
    down, up = (lat + 1) % lats, (lat + lats - 1) % lats
    east, west = (lon + 1) % lons, (lon + lons - 1) % lons
    peers = [sibling, (down, lon), (up, lon), (lat, east), (lat, west), (down, east), (up, west)]
    for axes in ("xy", "xz"):
        for i in range(4):
            for j in range(4):
                if (i or j) and (j or axes == "xy"):
                    there = {axis: spot[axis] for axis in "xyz"}
                    there[axes[0]] = (spot[axes[0]] + i) % 4
                    there[axes[1]] = (spot[axes[1]] + j) % 4
                    peers.append(device_at(there, core))
    barrier = pltpu.get_barrier_semaphore()
    for peer in peers:
        pl.semaphore_signal(barrier, inc=1, device_id=peer, device_id_type=MESH)

    count = [0]

    def remote(src, dst, peer):
        i = count[0]
        count[0] += 1
        copy = pltpu.make_async_remote_copy(
            src_ref=src, dst_ref=dst, send_sem=send.at[i], recv_sem=recv.at[i],
            device_id=peer, device_id_type=MESH,
        )
        copy.start()
        return copy

    loads[0].wait()
    loads[1].wait()
    for i in range(2):
        side_out[i] = nn(pick[...], ext[i, 0:TOKENS]).astype(BF16)
    pl.semaphore_wait(barrier, len(peers))
    main, angle = pl.ds(0, SIDE), pl.ds(SIDE, EDGE - SIDE)
    halo = [
        remote(side_out.at[:, main], side.at[:, main], (lat, west)),
        remote(ext.at[:, pl.ds(0, LEAD)], ext.at[:, pl.ds(TOKENS, LEAD)], (up, lon)),
        remote(side_out.at[:, angle], side.at[:, angle], (up, west)),
    ]

    def forward(pieces):
        gathered = []
        for i in range(2):
            parts = []
            for a, lo, hi in pieces:
                start = LEAD + a * BAND
                src = ext[i, start : start + BAND]
                first_row, last_row = lo // 16 * 16, -(-hi // 16) * 16
                got = nn(perm[first_row:last_row], src)[lo - first_row : hi - first_row]
                if hi == BAND:
                    width = EDGE if a == BANDS - 1 else SIDE
                    edge = nn(beside[a, :, 0:width], side[i, 0:width])
                    if lo < LAST:
                        got = jnp.concatenate([got[: LAST - lo], got[LAST - lo :] + edge], axis=0)
                    else:
                        got = got + edge[lo - LAST :]
                parts.append(got)
            gathered.append(jnp.concatenate(parts, axis=0))
        x, cot = gathered
        center = x - jnp.mean(x, axis=-1, keepdims=True)
        inv = lax.rsqrt(jnp.mean(center * center, axis=-1, keepdims=True) + 1e-05)
        norm = center * inv
        sc = norm * gain[...]
        qkv_now = nn(sc.astype(BF16), wqkv[...]).astype(BF16).astype(F32)
        att_now = nt(cot.astype(BF16), wproj[...]).astype(BF16).astype(F32)
        at = 0
        for a, lo, hi in pieces:
            dst = slice(a * BAND + lo, a * BAND + hi)
            src = slice(at, at + hi - lo)
            at += hi - lo
            normed[dst] = norm[src]
            inv_std[dst] = jnp.broadcast_to(inv[src], (hi - lo, 128))
            scaled[dst] = sc[src]
            cot_win[dst] = cot[src]
            qkv[dst] = qkv_now[src]
            grad_att[dst] = att_now[src]

    lane = lax.broadcasted_iota(jnp.int32, (1, 128), 1) // HEAD
    masks = [(lane == j).astype(F32) for j in range(GROUP)]
    key_half = lax.broadcasted_iota(jnp.int32, (SPAN, SPAN), 0) >= HALF_LAT * WIN_LON
    query_half = lax.broadcasted_iota(jnp.int32, (SPAN, SPAN), 1) >= HALF_LAT * WIN_LON
    parted = jnp.where(key_half == query_half, 0.0, -1e30)
    parted = jnp.concatenate([parted] * GROUP, axis=1)

    def stacked(x):
        return jnp.concatenate([x * m for m in masks], axis=0).astype(BF16)

    def by_head(x):
        x = x.reshape(GROUP, SPAN, 128)
        y = x[GROUP - 1]
        for j in range(GROUP - 2, -1, -1):
            y = jnp.where(lane == j, x[j], y)
        return y

    scale = HEAD ** (-0.5)

    def attention(windows, edge=False):
        shut = parted * jnp.where(lat == lats - 1, 1.0, 0.0)
        todo = []
        for w in windows:
            rows = pl.ds(pl.multiple_of(w * SPAN, 8), SPAN)
            todo += [(rows, [slice(j * C + lo, j * C + lo + 128) for j in range(3)])
                     for lo in range(0, C, 128)]
        q = [stacked(qkv[rows, cols[0]]) for rows, cols in todo]
        k = [qkv[rows, cols[1]].astype(BF16) for rows, cols in todo]
        v = [qkv[rows, cols[2]].astype(BF16) for rows, cols in todo]
        da = [stacked(grad_att[rows, cols[0]]) for rows, cols in todo]
        n = range(len(todo))
        s = [nt(k[i], q[i]) * scale for i in n]
        if edge:
            s = [x + shut for x in s]
        gp = [nt(v[i], da[i]) for i in n]
        ex = [jnp.exp(x - jnp.max(x, axis=0, keepdims=True)) for x in s]
        prob = [x * (1.0 / jnp.sum(x, axis=0, keepdims=True)) for x in ex]
        inner = [jnp.sum(prob[i] * gp[i], axis=0, keepdims=True) for i in n]
        gs = [(prob[i] * (gp[i] - inner[i]) * scale).astype(BF16) for i in n]
        pb = [x.astype(BF16) for x in prob]
        found = [by_head(tn(pb[i], v[i])) for i in n]
        grad_q = [by_head(tn(gs[i], k[i])) for i in n]
        grad_k = [nn(gs[i], q[i]) for i in n]
        grad_v = [nn(pb[i], da[i]) for i in n]
        for i, (rows, cols) in enumerate(todo):
            att[rows, cols[0]] = found[i]
            grad_all[rows, cols[0]] = grad_q[i]
            grad_all[rows, cols[1]] = grad_k[i]
            grad_all[rows, cols[2]] = grad_v[i]

    loads[2].wait()
    loads[3].wait()
    inner = (PER_BAND - 1) * SPAN
    forward([(a, 0, inner) for a in range(BANDS - 1)])

    def early(i, carry):
        attention([i * PER_BAND + b for b in range(PER_BAND - 1)])
        return carry

    lax.fori_loop(0, BANDS - 1, early, 0)
    def weight_sums(pieces, halves, found):
        def tokens(ref, cols):
            parts = [ref[lo:hi, cols] for lo, hi in pieces]
            return jnp.concatenate(parts, axis=0).astype(BF16)

        if not found:
            found += [tokens(scaled, slice(0, C)).T, tokens(att, slice(0, C)).T]
        for half in halves:
            lo = half * 256
            for j in range(3):
                yield 4 * half + j, nn(found[0], tokens(grad_all, slice(j * C + lo, j * C + lo + 256)))
            yield 4 * half + 3, nn(found[1], tokens(cot_win, slice(lo, lo + 256)))

    starts = [a * BAND for a in range(BANDS - 1)]
    for i, value in weight_sums([(start, start + inner) for start in starts], (0, 1), []):
        grads[i] = value
    halo[0].wait_recv()
    forward([(a, inner, BAND) for a in range(BANDS - 1)])
    attention([a * PER_BAND + PER_BAND - 1 for a in range(BANDS - 1)])
    halo[1].wait_recv()
    halo[2].wait_recv()
    forward([(BANDS - 1, 0, BAND)])

    def late(i, carry):
        attention([(BANDS - 1) * PER_BAND + 2 * i + b for b in range(2)], edge=True)
        return carry

    lax.fori_loop(0, PER_BAND // 2, late, 0)

    late_rows = [(start + inner, start + BAND) for start in starts] + [(TOKENS - BAND, TOKENS)]
    turned_once = []
    upper = lax.broadcasted_iota(jnp.int32, (1, 8, 1), 1) < 4
    first_core = lax.broadcasted_iota(jnp.int32, (1, 8, 1), 1) * 0 + core == 0
    first = []
    for half in range(2):
        lo = half * 256
        lanes = slice(lo, lo + 256)
        for i, value in weight_sums(late_rows, (half,), turned_once):
            grads[i] += value

        def pack(i, carry):
            rows = pl.ds(pl.multiple_of(i * 64, 64), 64)
            chips = pl.ds(i * 8, 8)
            t = [grads[4 * half + j, rows].reshape(8, 8, 256) for j in range(4)]
            turned = [pltpu.roll(x, 4, 1) for x in t]
            block = []
            for near, far in ((t, turned), (turned, t)):
                block.append(
                    jnp.concatenate(
                        [jnp.where(upper, near[j], far[j + 1]) for j in (0, 2)], axis=1
                    )
                )
            is_first = jnp.concatenate([first_core, first_core], axis=1)
            mine[chips, :, lanes] = jnp.where(is_first, block[0], block[1])
            theirs[chips, :, lanes] = jnp.where(is_first, block[1], block[0]).astype(BF16)
            return carry

        lax.fori_loop(0, 8, pack, 0, unroll=2)
        for start, width, _ in PARTS:
            if lo <= start < lo + 256:
                span = pl.ds(start, width)
                first.append(remote(theirs.at[:, :, span], got0.at[:, :, span], sibling))

    back, edges = [], []
    loads[4].wait()
    loads[5].wait()

    def backward(a):
        dst = slice(a * BAND, (a + 1) * BAND)
        gn = nt(grad_all[dst].astype(BF16), wqkv[...]) * gain[...]
        norm = normed[dst]
        branch = inv_std[dst][:, 0:1] * (
            gn
            - jnp.mean(gn, axis=-1, keepdims=True)
            - norm * jnp.mean(gn * norm, axis=-1, keepdims=True)
        )
        done = (cot_win[dst] + branch).astype(BF16)
        out_ext[dst] = nn(perm_t[...], done).astype(BF16)
        edges.append(nn(beside_t[a], done[LAST:]))
        if a == BANDS - 1:
            back.append(remote(out_ext.at[pl.ds(TOKENS - LEAD, LEAD)], top, (down, lon)))
        if len(edges) == BANDS:
            back_side[...] = (edges[0] + edges[1] + edges[2] + edges[3]).astype(BF16)
            back.append(remote(back_side.at[main], left.at[main], (lat, east)))
            back.append(remote(back_side.at[angle], left.at[angle], (down, east)))

    def by_role(p, steps):
        return dict(zip(PARTS[p][2], steps))

    def my_role(p, r):
        return spot[PARTS[p][2][r]]

    def peer_at(p, steps):
        moved = by_role(p, steps)
        return device_at({axis: (spot[axis] + moved[axis]) % 4 for axis in "xyz"}, core)

    def summed0(p, chip):
        lo, width = PARTS[p][:2]
        lanes = slice(lo, lo + width)
        return mine[chip, :, lanes] + got0[chip, :, lanes].astype(F32)

    sent = [[] for _ in PARTS]

    def stage0(p):
        held, got = buffers[5 * p : 5 * p + 2]
        first[p].wait_recv()

        def add(i, carry):
            at = (i // 16, i // 4 % 4, i % 4)
            held[at] = summed0(p, chip_at(by_role(p, at))).astype(BF16)
            return carry

        lax.fori_loop(0, 64, add, 0, unroll=4)
        for k in (2, 1, 3):
            sent[p].append(
                remote(held.at[(my_role(p, 0) + k) % 4], got.at[k - 1], peer_at(p, (k, 0, 0)))
            )

    def stage1(p):
        got, nxt, nxt_got, keep = buffers[5 * p + 1 : 5 * p + 5]
        for copy in sent[p]:
            copy.wait_recv()
        here = my_role(p, 0)
        b, c = my_role(p, 1), my_role(p, 2)

        def total(i, j):
            x = summed0(p, chip_at(by_role(p, (here, i, j))))
            for k in range(3):
                x = x + got[k, i, j].astype(F32)
            return x

        def add(i, carry):
            nxt[i // 4, i % 4] = total(i // 4, i % 4).astype(BF16)
            return carry

        lax.fori_loop(0, 16, add, 0, unroll=4)
        keep[...] = total(b, c)
        for i in (2, 1, 3, 0):
            for j in (2, 1, 3, 0):
                if i or j:
                    sent[p].append(
                        remote(
                            nxt.at[(b + i) % 4, (c + j) % 4],
                            nxt_got.at[4 * i + j - 1],
                            peer_at(p, (0, i, j)),
                        )
                    )

    def stage2(p):
        got, keep = buffers[5 * p + 3 : 5 * p + 5]
        for copy in sent[p][3:]:
            copy.wait_recv()
        x = keep[...]
        for i in range(15):
            x = x + got[i].astype(F32)
        return x

    backward(BANDS - 1)
    stage0(0)
    stage0(1)
    for a in range(BANDS - 1):
        backward(a)
    for p in range(len(PARTS)):
        stage1(p)

    me = lat * lons + lon
    picked = lax.broadcasted_iota(jnp.int32, (8, C), 0) + me * 4
    picked = (picked == lax.broadcasted_iota(jnp.int32, (8, C), 1)).astype(F32)
    w_rows = nn(picked.astype(BF16), wqkv[...])
    gain_rows = jnp.sum(picked * gain[...], axis=1, keepdims=True)

    for copy in back:
        copy.wait_recv()
    out_ref[LEAD:] = (
        out_ext[0 : TOKENS - LEAD].astype(F32) + nn(pick_t[LEAD:, 0:SIDE], left[0:SIDE])
    ).astype(BF16)
    out_ref[0:LEAD] = (top[...].astype(F32) + nn(pick_t[0:LEAD], left[...])).astype(BF16)
    store = pltpu.make_async_copy(out_ref, out_hbm, local.at[4])
    store.start()

    total = jnp.concatenate([stage2(p) for p in range(len(PARTS))], axis=1)
    total = total * (1.0 / math.sqrt(TOKENS * lats * lons))
    gqkv = [total[4 * j : 4 * j + 4] for j in range(3)]
    gqkv_ref[...] = jnp.concatenate(gqkv, axis=1)
    gproj_ref[...] = total[12:16]
    dots = jnp.zeros((4, 1), F32)
    for j in range(3):
        dots = dots + jnp.sum(gqkv[j] * w_rows[0:4, j * C : (j + 1) * C], axis=1, keepdims=True)
    dots = dots / gain_rows[0:4]
    diagonal = lax.broadcasted_iota(jnp.int32, (4, 128), 0)
    diagonal = diagonal == lax.broadcasted_iota(jnp.int32, (4, 128), 1)
    ggain_ref[...] = jnp.sum(jnp.where(diagonal, dots, 0.0), axis=0, keepdims=True)
    for copy in halo + first + back + [c for part in sent for c in part]:
        copy.wait_send()
    store.wait()


def sublayer(*args):
    vmem = pl.BlockSpec(memory_space=pltpu.VMEM)
    hbm = pl.BlockSpec(memory_space=pl.ANY)
    scratch = [
        pltpu.VMEM((2, TOKENS + LEAD, C), BF16),
        pltpu.VMEM((2, EDGE, C), BF16),
        pltpu.VMEM((2, EDGE, C), BF16),
        pltpu.VMEM((C, 3 * C), BF16),
        pltpu.VMEM((C, C), BF16),
        pltpu.VMEM((BAND, BAND), BF16),
        pltpu.VMEM((TOKENS, EDGE), BF16),
        pltpu.VMEM((TOKENS, C), F32),
        pltpu.VMEM((TOKENS, 128), F32),
        pltpu.VMEM((TOKENS, C), F32),
        pltpu.VMEM((TOKENS, C), F32),
        pltpu.VMEM((TOKENS, 3 * C), F32),
        pltpu.VMEM((TOKENS, C), F32),
        pltpu.VMEM((TOKENS, C), F32),
        pltpu.VMEM((TOKENS, 3 * C), F32),
        pltpu.VMEM((TOKENS, C), BF16),
        pltpu.VMEM((EDGE, C), BF16),
        pltpu.VMEM((LEAD, C), BF16),
        pltpu.VMEM((EDGE, C), BF16),
        pltpu.VMEM((8, C, 256), F32),
        pltpu.VMEM((64, 16, C), F32),
        pltpu.VMEM((64, 16, C), BF16),
        pltpu.VMEM((64, 16, C), BF16),
        pltpu.VMEM((TOKENS, C), BF16),
    ]
    for _, width, _ in PARTS:
        for dims in ((4, 4, 4), (3, 4, 4), (4, 4), (15,)):
            scratch.append(pltpu.VMEM(dims + (16, width), BF16))
        scratch.append(pltpu.VMEM((16, width), F32))
    copies = 3 + 3 + 19 * len(PARTS)
    return pl.pallas_call(
        sublayer_kernel,
        out_shape=(
            jax.ShapeDtypeStruct((TOKENS, C), BF16),
            jax.ShapeDtypeStruct((4, 3 * C), F32),
            jax.ShapeDtypeStruct((4, C), F32),
            jax.ShapeDtypeStruct((1, 128), F32),
        ),
        in_specs=[hbm, hbm, vmem, hbm, hbm, vmem, hbm, vmem, vmem, vmem, hbm],
        out_specs=(hbm, vmem, vmem, vmem),
        scratch_shapes=scratch
        + [
            pltpu.SemaphoreType.DMA((7,)),
            pltpu.SemaphoreType.DMA((copies,)),
            pltpu.SemaphoreType.DMA((copies,)),
        ],
        compiler_params=pltpu.CompilerParams(
            collective_id=1, has_side_effects=True, vmem_limit_bytes=62 * 1024 * 1024
        ),
        name="window_grads",
    )(*args)


def hand_on_kernel(out_ref, gqkv_ref, gproj_ref, gain_ref, out, gqkv, gproj, ggain):
    out[...] = out_ref[...]
    gqkv[...] = gqkv_ref[...]
    gproj[...] = gproj_ref[...]
    ggain[...] = gain_ref[0, 0:4]


def hand_on(*args):
    def whole(*shape):
        return pl.BlockSpec(shape, lambda i: (0,) * len(shape))

    tokens = pl.BlockSpec((TOKENS // 2, C), lambda i: (i, 0))
    return pl.pallas_call(
        hand_on_kernel,
        grid=(2,),
        out_shape=(
            jax.ShapeDtypeStruct((TOKENS, C), BF16),
            jax.ShapeDtypeStruct((4, 3 * C), F32),
            jax.ShapeDtypeStruct((4, C), F32),
            jax.ShapeDtypeStruct((4,), F32),
        ),
        in_specs=[tokens, whole(4, 3 * C), whole(4, C), whole(1, 128)],
        out_specs=(tokens, whole(4, 3 * C), whole(4, C), whole(4)),
        compiler_params=pltpu.CompilerParams(vmem_limit_bytes=62 * 1024 * 1024),
        name="hand_on",
    )(*args)


def on_device(activations, cotangent, norm_gain, qkv_weight, proj_weight):
    results = sublayer(
        activations.reshape(TOKENS, C),
        cotangent.reshape(TOKENS, C),
        norm_gain.reshape(1, C),
        qkv_weight,
        proj_weight,
        *orders(),
    )
    grad_input, gqkv, gproj, ggain = hand_on(*results)
    return grad_input.reshape(ROWS, COLS, C), gqkv, gproj, ggain


def solution(mesh):
    return jax.shard_map(
        on_device,
        mesh=mesh,
        in_specs=(P("lat", "lon", None), P("lat", "lon", None), P(), P(), P()),
        out_specs=(
            P("lat", "lon", None),
            P(("lat", "lon"), None),
            P(("lat", "lon"), None),
            P(("lat", "lon")),
        ),
        check_vma=False,
    )
```

```python
import math

import jax
import jax.numpy as jnp
import numpy as np
from jax import lax
from jax.experimental import pallas as pl
from jax.experimental.pallas import tpu as pltpu
from jax.sharding import PartitionSpec as P

C = 512
HEADS = 16
HEAD = C // HEADS
WIN_LAT = 6
WIN_LON = 12
SPAN = WIN_LAT * WIN_LON
ROWS = 24
COLS = 48
BANDS = ROWS // WIN_LAT
PER_BAND = COLS // WIN_LON
BAND = WIN_LAT * COLS
TOKENS = ROWS * COLS
HALF_LAT = WIN_LAT // 2
HALF_LON = WIN_LON // 2
SIDE = 128
EDGE = SIDE + 32
LAST = 208
TWO = 2 * COLS
PIECE = 2 * WIN_LON
GROUP = 128 // HEAD
F32 = jnp.float32
BF16 = jnp.bfloat16


def orders():
    perm = np.zeros((TWO, TWO), np.float32)
    beside = np.zeros((BANDS, BAND - LAST, EDGE), np.float32)
    pick = np.zeros((EDGE, TOKENS), np.float32)
    for b in range(PER_BAND):
        for r in range(WIN_LAT):
            for c in range(WIN_LON):
                col = WIN_LON * b + HALF_LON + c
                token = b * SPAN + r * WIN_LON + c
                if col < COLS:
                    if r < 2:
                        perm[b * PIECE + r * WIN_LON + c, r * COLS + col] = 1.0
                    continue
                for a in range(BANDS):
                    beside[a, token - LAST, edge_row(a * WIN_LAT + HALF_LAT + r, col - COLS)] = 1.0
    for row in range(ROWS):
        for c in range(HALF_LON):
            pick[edge_row(row + (ROWS if row < HALF_LAT else 0), c), row * COLS + c] = 1.0
    return [jnp.asarray(x, BF16) for x in (perm, perm.T, beside, beside.transpose(0, 2, 1), pick, pick.T)]


def edge_row(row, col):
    if row < ROWS:
        return (row - HALF_LAT) * HALF_LON + col
    return SIDE + (row - ROWS) * HALF_LON + col


def nn(a, b):
    return lax.dot_general(a, b, (((1,), (0,)), ((), ())), preferred_element_type=F32)


def nt(a, b):
    return lax.dot_general(a, b, (((1,), (1,)), ((), ())), preferred_element_type=F32)


def tn(a, b):
    return lax.dot_general(a, b, (((0,), (0,)), ((), ())), preferred_element_type=F32)


PARTS = ((0, 256, "zyx"), (256, 256, "yxz"))
MESH = pl.DeviceIdType.MESH
LEAD = HALF_LAT * COLS


def place():
    lat, lon = lax.axis_index("lat"), lax.axis_index("lon")
    spot = {"z": lat // 2, "x": (lon // 2) % 2 * 2 + lat % 2, "y": lon // 4}
    return lat, lon, spot, lon % 2


def device_at(spot, core):
    return (spot["z"] * 2 + spot["x"] % 2, spot["y"] * 4 + spot["x"] // 2 * 2 + core)


def chip_at(at):
    return at["z"] * 16 + at["x"] % 2 * 8 + at["y"] * 2 + at["x"] // 2


def sublayer_kernel(
    own_in, own_cot, *rest,
):
    fetched, rest = rest[:9], rest[9:]
    (
        out_hbm, gqkv_ref, gproj_ref, ggain_ref,
        ext, side, side_out,
        normed, inv_std, scaled, cot_win, qkv, grad_att, att, grad_all,
        out_ext, back_side, top, left, grads, mine, theirs, got0, out_ref,
    ) = rest[:24]
    held_here, rest = rest[24:33], rest[33:]
    gain, wqkv, wproj, perm, perm_t, beside, beside_t, pick, pick_t = held_here
    buffers, (local, send, recv) = rest[:-3], rest[-3:]
    loads = [
        pltpu.make_async_copy(own_in, ext.at[0, pl.ds(0, TOKENS)], local.at[0]),
        pltpu.make_async_copy(own_cot, ext.at[1, pl.ds(0, TOKENS)], local.at[1]),
    ]
    for i in (7, 1, 3, 0, 2, 5, 4, 6, 8):
        loads.append(pltpu.make_async_copy(fetched[i], held_here[i], local.at[3 + i]))
    for load in loads:
        load.start()

    lat, lon, spot, core = place()
    lats, lons = lax.axis_size("lat"), lax.axis_size("lon")
    sibling = device_at(spot, 1 - core)
    down, up = (lat + 1) % lats, (lat + lats - 1) % lats
    east, west = (lon + 1) % lons, (lon + lons - 1) % lons
    peers = [sibling, (down, lon), (up, lon), (lat, east), (lat, west), (down, east), (up, west)]
    for axes in ("xy", "xz"):
        for i in range(4):
            for j in range(4):
                if (i or j) and (j or axes == "xy"):
                    there = {axis: spot[axis] for axis in "xyz"}
                    there[axes[0]] = (spot[axes[0]] + i) % 4
                    there[axes[1]] = (spot[axes[1]] + j) % 4
                    peers.append(device_at(there, core))
    barrier = pltpu.get_barrier_semaphore()
    for peer in peers:
        pl.semaphore_signal(barrier, inc=1, device_id=peer, device_id_type=MESH)

    count = [0]

    def remote(src, dst, peer):
        i = count[0]
        count[0] += 1
        copy = pltpu.make_async_remote_copy(
            src_ref=src, dst_ref=dst, send_sem=send.at[i], recv_sem=recv.at[i],
            device_id=peer, device_id_type=MESH,
        )
        copy.start()
        return copy

    for load in loads[:3]:
        load.wait()
    for i in range(2):
        side_out[i] = nn(pick[...], ext[i, 0:TOKENS]).astype(BF16)
    pl.semaphore_wait(barrier, len(peers))
    main, angle = pl.ds(0, SIDE), pl.ds(SIDE, EDGE - SIDE)
    halo = [
        remote(side_out.at[:, main], side.at[:, main], (lat, west)),
        remote(ext.at[:, pl.ds(0, LEAD)], ext.at[:, pl.ds(TOKENS, LEAD)], (up, lon)),
        remote(side_out.at[:, angle], side.at[:, angle], (up, west)),
    ]

    def forward(pieces):
        gathered = []
        for i in range(2):
            parts = []
            for a, lo, hi in pieces:
                start = LEAD + a * BAND
                first = lo // SPAN * PIECE
                first_row = first // 16 * 16
                last = hi // SPAN * PIECE
                rows = perm[first_row : -(-last // 16) * 16]
                thirds = [
                    nn(rows, ext[i, start + j * TWO : start + (j + 1) * TWO])[first - first_row :]
                    for j in range(3)
                ]
                got = [
                    third[at : at + PIECE] for at in range(0, last - first, PIECE) for third in thirds
                ]
                got = jnp.concatenate(got, axis=0)
                if hi == BAND:
                    width = EDGE if a == BANDS - 1 else SIDE
                    edge = nn(beside[a, :, 0:width], side[i, 0:width])
                    if lo < LAST:
                        got = jnp.concatenate([got[: LAST - lo], got[LAST - lo :] + edge], axis=0)
                    else:
                        got = got + edge[lo - LAST :]
                parts.append(got)
            gathered.append(jnp.concatenate(parts, axis=0))
        x, cot = gathered
        center = x - jnp.mean(x, axis=-1, keepdims=True)
        inv = lax.rsqrt(jnp.mean(center * center, axis=-1, keepdims=True) + 1e-05)
        norm = center * inv
        sc = norm * gain[...]
        qkv_now = nn(sc.astype(BF16), wqkv[...]).astype(BF16).astype(F32)
        att_now = nt(cot.astype(BF16), wproj[...]).astype(BF16).astype(F32)
        at = 0
        for a, lo, hi in pieces:
            dst = slice(a * BAND + lo, a * BAND + hi)
            src = slice(at, at + hi - lo)
            at += hi - lo
            normed[dst] = norm[src]
            inv_std[dst] = jnp.broadcast_to(inv[src], (hi - lo, 128))
            scaled[dst] = sc[src]
            cot_win[dst] = cot[src]
            qkv[dst] = qkv_now[src]
            grad_att[dst] = att_now[src]

    lane = lax.broadcasted_iota(jnp.int32, (1, 128), 1) // HEAD
    masks = [(lane == j).astype(F32) for j in range(GROUP)]
    key_half = lax.broadcasted_iota(jnp.int32, (SPAN, SPAN), 0) >= HALF_LAT * WIN_LON
    query_half = lax.broadcasted_iota(jnp.int32, (SPAN, SPAN), 1) >= HALF_LAT * WIN_LON
    parted = jnp.where(key_half == query_half, 0.0, -1e30)
    parted = jnp.concatenate([parted] * GROUP, axis=1)

    def stacked(x):
        return jnp.concatenate([x * m for m in masks], axis=0).astype(BF16)

    def by_head(x):
        x = x.reshape(GROUP, SPAN, 128)
        y = x[GROUP - 1]
        for j in range(GROUP - 2, -1, -1):
            y = jnp.where(lane == j, x[j], y)
        return y

    scale = HEAD ** (-0.5)

    def attention(windows, edge=False):
        shut = parted * jnp.where(lat == lats - 1, 1.0, 0.0)
        todo = []
        for w in windows:
            rows = pl.ds(pl.multiple_of(w * SPAN, 8), SPAN)
            todo += [(rows, [slice(j * C + lo, j * C + lo + 128) for j in range(3)])
                     for lo in range(0, C, 128)]
        q = [stacked(qkv[rows, cols[0]]) for rows, cols in todo]
        k = [qkv[rows, cols[1]].astype(BF16) for rows, cols in todo]
        v = [qkv[rows, cols[2]].astype(BF16) for rows, cols in todo]
        da = [stacked(grad_att[rows, cols[0]]) for rows, cols in todo]
        n = range(len(todo))
        s = [nt(k[i], q[i]) * scale for i in n]
        if edge:
            s = [x + shut for x in s]
        gp = [nt(v[i], da[i]) for i in n]
        ex = [jnp.exp(x - jnp.max(x, axis=0, keepdims=True)) for x in s]
        prob = [x * (1.0 / jnp.sum(x, axis=0, keepdims=True)) for x in ex]
        inner = [jnp.sum(prob[i] * gp[i], axis=0, keepdims=True) for i in n]
        gs = [(prob[i] * (gp[i] - inner[i]) * scale).astype(BF16) for i in n]
        pb = [x.astype(BF16) for x in prob]
        found = [by_head(tn(pb[i], v[i])) for i in n]
        grad_q = [by_head(tn(gs[i], k[i])) for i in n]
        grad_k = [nn(gs[i], q[i]) for i in n]
        grad_v = [nn(pb[i], da[i]) for i in n]
        for i, (rows, cols) in enumerate(todo):
            att[rows, cols[0]] = found[i]
            grad_all[rows, cols[0]] = grad_q[i]
            grad_all[rows, cols[1]] = grad_k[i]
            grad_all[rows, cols[2]] = grad_v[i]

    for load in loads[3:8]:
        load.wait()
    inner = (PER_BAND - 1) * SPAN
    forward([(a, 0, inner) for a in range(BANDS - 1)])

    def early(i, carry):
        attention([i * PER_BAND + b for b in range(PER_BAND - 1)])
        return carry

    lax.fori_loop(0, BANDS - 1, early, 0)
    def weight_sums(pieces, halves, found):
        def tokens(ref, cols):
            parts = [ref[lo:hi, cols] for lo, hi in pieces]
            return jnp.concatenate(parts, axis=0).astype(BF16)

        if not found:
            found += [tokens(scaled, slice(0, C)).T, tokens(att, slice(0, C)).T]
        for half in halves:
            lo = half * 256
            for j in range(3):
                yield 4 * half + j, nn(found[0], tokens(grad_all, slice(j * C + lo, j * C + lo + 256)))
            yield 4 * half + 3, nn(found[1], tokens(cot_win, slice(lo, lo + 256)))

    starts = [a * BAND for a in range(BANDS - 1)]
    for i, value in weight_sums([(start, start + inner) for start in starts], (0, 1), []):
        grads[i] = value
    halo[0].wait_recv()
    forward([(a, inner, BAND) for a in range(BANDS - 1)])
    attention([a * PER_BAND + PER_BAND - 1 for a in range(BANDS - 1)])
    halo[1].wait_recv()
    halo[2].wait_recv()
    forward([(BANDS - 1, 0, BAND)])

    def late(i, carry):
        attention([(BANDS - 1) * PER_BAND + 2 * i + b for b in range(2)], edge=True)
        return carry

    lax.fori_loop(0, PER_BAND // 2, late, 0)

    late_rows = [(start + inner, start + BAND) for start in starts] + [(TOKENS - BAND, TOKENS)]
    turned_once = []
    upper = lax.broadcasted_iota(jnp.int32, (1, 8, 1), 1) < 4
    first_core = lax.broadcasted_iota(jnp.int32, (1, 8, 1), 1) * 0 + core == 0
    first = []
    for half in range(2):
        lo = half * 256
        lanes = slice(lo, lo + 256)
        for i, value in weight_sums(late_rows, (half,), turned_once):
            grads[i] += value

        def pack(i, carry):
            rows = pl.ds(pl.multiple_of(i * 64, 64), 64)
            chips = pl.ds(i * 8, 8)
            t = [grads[4 * half + j, rows].reshape(8, 8, 256) for j in range(4)]
            turned = [pltpu.roll(x, 4, 1) for x in t]
            block = []
            for near, far in ((t, turned), (turned, t)):
                block.append(
                    jnp.concatenate(
                        [jnp.where(upper, near[j], far[j + 1]) for j in (0, 2)], axis=1
                    )
                )
            is_first = jnp.concatenate([first_core, first_core], axis=1)
            mine[chips, :, lanes] = jnp.where(is_first, block[0], block[1])
            theirs[chips, :, lanes] = jnp.where(is_first, block[1], block[0]).astype(BF16)
            return carry

        lax.fori_loop(0, 8, pack, 0, unroll=2)
        for start, width, _ in PARTS:
            if lo <= start < lo + 256:
                span = pl.ds(start, width)
                first.append(remote(theirs.at[:, :, span], got0.at[:, :, span], sibling))

    back, edges = [], []
    for load in loads[8:]:
        load.wait()

    def backward(a):
        dst = slice(a * BAND, (a + 1) * BAND)
        gn = nt(grad_all[dst].astype(BF16), wqkv[...]) * gain[...]
        norm = normed[dst]
        branch = inv_std[dst][:, 0:1] * (
            gn
            - jnp.mean(gn, axis=-1, keepdims=True)
            - norm * jnp.mean(gn * norm, axis=-1, keepdims=True)
        )
        done = cot_win[dst] + branch
        for j in range(3):
            at = [b * SPAN + j * PIECE for b in range(PER_BAND)]
            part = jnp.concatenate([done[i : i + PIECE] for i in at], axis=0).astype(BF16)
            slab = slice(a * BAND + j * TWO, a * BAND + (j + 1) * TWO)
            out_ext[slab] = nn(perm_t[...], part).astype(BF16)
        edges.append(nn(beside_t[a], done[LAST:].astype(BF16)))
        if a == BANDS - 1:
            back.append(remote(out_ext.at[pl.ds(TOKENS - LEAD, LEAD)], top, (down, lon)))
        if len(edges) == BANDS:
            back_side[...] = (edges[0] + edges[1] + edges[2] + edges[3]).astype(BF16)
            back.append(remote(back_side.at[main], left.at[main], (lat, east)))
            back.append(remote(back_side.at[angle], left.at[angle], (down, east)))

    def by_role(p, steps):
        return dict(zip(PARTS[p][2], steps))

    def my_role(p, r):
        return spot[PARTS[p][2][r]]

    def peer_at(p, steps):
        moved = by_role(p, steps)
        return device_at({axis: (spot[axis] + moved[axis]) % 4 for axis in "xyz"}, core)

    def summed0(p, chip):
        lo, width = PARTS[p][:2]
        lanes = slice(lo, lo + width)
        return mine[chip, :, lanes] + got0[chip, :, lanes].astype(F32)

    sent = [[] for _ in PARTS]

    def stage0(p):
        held, got = buffers[5 * p : 5 * p + 2]
        first[p].wait_recv()

        def add(i, carry):
            at = (i // 16, i // 4 % 4, i % 4)
            held[at] = summed0(p, chip_at(by_role(p, at))).astype(BF16)
            return carry

        lax.fori_loop(0, 64, add, 0, unroll=4)
        for k in (2, 1, 3):
            sent[p].append(
                remote(held.at[(my_role(p, 0) + k) % 4], got.at[k - 1], peer_at(p, (k, 0, 0)))
            )

    def stage1(p):
        got, nxt, nxt_got, keep = buffers[5 * p + 1 : 5 * p + 5]
        for copy in sent[p]:
            copy.wait_recv()
        here = my_role(p, 0)
        b, c = my_role(p, 1), my_role(p, 2)

        def total(i, j):
            x = summed0(p, chip_at(by_role(p, (here, i, j))))
            for k in range(3):
                x = x + got[k, i, j].astype(F32)
            return x

        def add(i, carry):
            nxt[i // 4, i % 4] = total(i // 4, i % 4).astype(BF16)
            return carry

        lax.fori_loop(0, 16, add, 0, unroll=4)
        keep[...] = total(b, c)
        for i in (2, 1, 3, 0):
            for j in (2, 1, 3, 0):
                if i or j:
                    sent[p].append(
                        remote(
                            nxt.at[(b + i) % 4, (c + j) % 4],
                            nxt_got.at[4 * i + j - 1],
                            peer_at(p, (0, i, j)),
                        )
                    )

    def stage2(p):
        got, keep = buffers[5 * p + 3 : 5 * p + 5]
        for copy in sent[p][3:]:
            copy.wait_recv()
        x = keep[...]
        for i in range(15):
            x = x + got[i].astype(F32)
        return x

    backward(BANDS - 1)
    stage0(0)
    stage0(1)
    for a in range(BANDS - 1):
        backward(a)
    for p in range(len(PARTS)):
        stage1(p)

    me = lat * lons + lon
    picked = lax.broadcasted_iota(jnp.int32, (8, C), 0) + me * 4
    picked = (picked == lax.broadcasted_iota(jnp.int32, (8, C), 1)).astype(F32)
    w_rows = nn(picked.astype(BF16), wqkv[...])
    gain_rows = jnp.sum(picked * gain[...], axis=1, keepdims=True)

    for copy in back:
        copy.wait_recv()
    out_ref[LEAD:] = (
        out_ext[0 : TOKENS - LEAD].astype(F32) + nn(pick_t[LEAD:, 0:SIDE], left[0:SIDE])
    ).astype(BF16)
    out_ref[0:LEAD] = (top[...].astype(F32) + nn(pick_t[0:LEAD], left[...])).astype(BF16)
    store = pltpu.make_async_copy(out_ref, out_hbm, local.at[2])
    store.start()

    total = jnp.concatenate([stage2(p) for p in range(len(PARTS))], axis=1)
    total = total * (1.0 / math.sqrt(TOKENS * lats * lons))
    gqkv = [total[4 * j : 4 * j + 4] for j in range(3)]
    gqkv_ref[...] = jnp.concatenate(gqkv, axis=1)
    gproj_ref[...] = total[12:16]
    dots = jnp.zeros((4, 1), F32)
    for j in range(3):
        dots = dots + jnp.sum(gqkv[j] * w_rows[0:4, j * C : (j + 1) * C], axis=1, keepdims=True)
    dots = dots / gain_rows[0:4]
    diagonal = lax.broadcasted_iota(jnp.int32, (4, 128), 0)
    diagonal = diagonal == lax.broadcasted_iota(jnp.int32, (4, 128), 1)
    ggain_ref[...] = jnp.sum(jnp.where(diagonal, dots, 0.0), axis=0, keepdims=True)
    for copy in halo + first + back + [c for part in sent for c in part]:
        copy.wait_send()
    store.wait()


def sublayer(*args):
    vmem = pl.BlockSpec(memory_space=pltpu.VMEM)
    hbm = pl.BlockSpec(memory_space=pl.ANY)
    scratch = [
        pltpu.VMEM((2, TOKENS + LEAD, C), BF16),
        pltpu.VMEM((2, EDGE, C), BF16),
        pltpu.VMEM((2, EDGE, C), BF16),
        pltpu.VMEM((TOKENS, C), F32),
        pltpu.VMEM((TOKENS, 128), F32),
        pltpu.VMEM((TOKENS, C), F32),
        pltpu.VMEM((TOKENS, C), F32),
        pltpu.VMEM((TOKENS, 3 * C), F32),
        pltpu.VMEM((TOKENS, C), F32),
        pltpu.VMEM((TOKENS, C), F32),
        pltpu.VMEM((TOKENS, 3 * C), F32),
        pltpu.VMEM((TOKENS, C), BF16),
        pltpu.VMEM((EDGE, C), BF16),
        pltpu.VMEM((LEAD, C), BF16),
        pltpu.VMEM((EDGE, C), BF16),
        pltpu.VMEM((8, C, 256), F32),
        pltpu.VMEM((64, 16, C), F32),
        pltpu.VMEM((64, 16, C), BF16),
        pltpu.VMEM((64, 16, C), BF16),
        pltpu.VMEM((TOKENS, C), BF16),
    ]
    scratch += [pltpu.VMEM(x.shape, x.dtype) for x in args[2:]]
    for _, width, _ in PARTS:
        for dims in ((4, 4, 4), (3, 4, 4), (4, 4), (15,)):
            scratch.append(pltpu.VMEM(dims + (16, width), BF16))
        scratch.append(pltpu.VMEM((16, width), F32))
    copies = 3 + 3 + 19 * len(PARTS)
    return pl.pallas_call(
        sublayer_kernel,
        out_shape=(
            jax.ShapeDtypeStruct((TOKENS, C), BF16),
            jax.ShapeDtypeStruct((4, 3 * C), F32),
            jax.ShapeDtypeStruct((4, C), F32),
            jax.ShapeDtypeStruct((1, 128), F32),
        ),
        in_specs=[hbm] * 11,
        out_specs=(hbm, vmem, vmem, vmem),
        scratch_shapes=scratch
        + [
            pltpu.SemaphoreType.DMA((12,)),
            pltpu.SemaphoreType.DMA((copies,)),
            pltpu.SemaphoreType.DMA((copies,)),
        ],
        compiler_params=pltpu.CompilerParams(
            collective_id=1, has_side_effects=True, vmem_limit_bytes=62 * 1024 * 1024
        ),
        name="window_grads",
    )(*args)


def hand_on_kernel(out_ref, gqkv_ref, gproj_ref, gain_ref, out, gqkv, gproj, ggain):
    out[...] = out_ref[...]
    gqkv[...] = gqkv_ref[...]
    gproj[...] = gproj_ref[...]
    ggain[...] = gain_ref[0, 0:4]


def hand_on(*args):
    def whole(*shape):
        return pl.BlockSpec(shape, lambda i: (0,) * len(shape))

    tokens = pl.BlockSpec((TOKENS // 2, C), lambda i: (i, 0))
    return pl.pallas_call(
        hand_on_kernel,
        grid=(2,),
        out_shape=(
            jax.ShapeDtypeStruct((TOKENS, C), BF16),
            jax.ShapeDtypeStruct((4, 3 * C), F32),
            jax.ShapeDtypeStruct((4, C), F32),
            jax.ShapeDtypeStruct((4,), F32),
        ),
        in_specs=[tokens, whole(4, 3 * C), whole(4, C), whole(1, 128)],
        out_specs=(tokens, whole(4, 3 * C), whole(4, C), whole(4)),
        compiler_params=pltpu.CompilerParams(vmem_limit_bytes=62 * 1024 * 1024),
        name="hand_on",
    )(*args)


def on_device(activations, cotangent, norm_gain, qkv_weight, proj_weight):
    results = sublayer(
        activations.reshape(TOKENS, C),
        cotangent.reshape(TOKENS, C),
        norm_gain.reshape(1, C),
        qkv_weight,
        proj_weight,
        *orders(),
    )
    grad_input, gqkv, gproj, ggain = hand_on(*results)
    return grad_input.reshape(ROWS, COLS, C), gqkv, gproj, ggain


def solution(mesh):
    return jax.shard_map(
        on_device,
        mesh=mesh,
        in_specs=(P("lat", "lon", None), P("lat", "lon", None), P(), P(), P()),
        out_specs=(
            P("lat", "lon", None),
            P(("lat", "lon"), None),
            P(("lat", "lon"), None),
            P(("lat", "lon")),
        ),
        check_vma=False,
    )
```

```python
import math

import jax
import jax.numpy as jnp
import numpy as np
from jax import lax
from jax.experimental import pallas as pl
from jax.experimental.pallas import tpu as pltpu
from jax.sharding import PartitionSpec as P

C = 512
HEADS = 16
HEAD = C // HEADS
WIN_LAT = 6
WIN_LON = 12
SPAN = WIN_LAT * WIN_LON
ROWS = 24
COLS = 48
BANDS = ROWS // WIN_LAT
PER_BAND = COLS // WIN_LON
BAND = WIN_LAT * COLS
TOKENS = ROWS * COLS
HALF_LAT = WIN_LAT // 2
HALF_LON = WIN_LON // 2
SIDE = 128
EDGE = SIDE + 32
LAST = 208
TWO = 2 * COLS
PIECE = 2 * WIN_LON
GROUP = 128 // HEAD
F32 = jnp.float32
BF16 = jnp.bfloat16


def orders():
    perm = np.zeros((TWO, TWO), np.float32)
    beside = np.zeros((BANDS, BAND - LAST, EDGE), np.float32)
    pick = np.zeros((EDGE, TOKENS), np.float32)
    for b in range(PER_BAND):
        for r in range(WIN_LAT):
            for c in range(WIN_LON):
                col = WIN_LON * b + HALF_LON + c
                token = b * SPAN + r * WIN_LON + c
                if col < COLS:
                    if r < 2:
                        perm[b * PIECE + r * WIN_LON + c, r * COLS + col] = 1.0
                    continue
                for a in range(BANDS):
                    beside[a, token - LAST, edge_row(a * WIN_LAT + HALF_LAT + r, col - COLS)] = 1.0
    for row in range(ROWS):
        for c in range(HALF_LON):
            pick[edge_row(row + (ROWS if row < HALF_LAT else 0), c), row * COLS + c] = 1.0
    return [jnp.asarray(x, BF16) for x in (perm, perm.T, beside, beside.transpose(0, 2, 1), pick, pick.T)]


def edge_row(row, col):
    if row < ROWS:
        return (row - HALF_LAT) * HALF_LON + col
    return SIDE + (row - ROWS) * HALF_LON + col


def nn(a, b):
    return lax.dot_general(a, b, (((1,), (0,)), ((), ())), preferred_element_type=F32)


def nt(a, b):
    return lax.dot_general(a, b, (((1,), (1,)), ((), ())), preferred_element_type=F32)


def tn(a, b):
    return lax.dot_general(a, b, (((0,), (0,)), ((), ())), preferred_element_type=F32)


PARTS = ((0, 256, "zyx", "yxz"), (256, 128, "yxz", "zyx"), (384, 128, "xzy", "xzy"))
MESH = pl.DeviceIdType.MESH
LEAD = HALF_LAT * COLS


def place():
    lat, lon = lax.axis_index("lat"), lax.axis_index("lon")
    spot = {"z": lat // 2, "x": (lon // 2) % 2 * 2 + lat % 2, "y": lon // 4}
    return lat, lon, spot, lon % 2


def device_at(spot, core):
    return (spot["z"] * 2 + spot["x"] % 2, spot["y"] * 4 + spot["x"] // 2 * 2 + core)


def chip_at(at):
    return at["z"] * 16 + at["x"] % 2 * 8 + at["y"] * 2 + at["x"] // 2


def sublayer_kernel(
    own_in, own_cot, *rest,
):
    fetched, rest = rest[:9], rest[9:]
    (
        out_hbm, gqkv_ref, gproj_ref, ggain_ref,
        ext, side, side_out,
        normed, inv_std, scaled, cot_win, qkv, grad_att, att, grad_all,
        out_ext, back_side, top, left, grads, mine, theirs, got0, out_ref,
    ) = rest[:24]
    held_here, rest = rest[24:33], rest[33:]
    gain, wqkv, wproj, perm, perm_t, beside, beside_t, pick, pick_t = held_here
    buffers, (local, send, recv) = rest[:-3], rest[-3:]
    loads = [
        pltpu.make_async_copy(own_in, ext.at[0, pl.ds(0, TOKENS)], local.at[0]),
        pltpu.make_async_copy(own_cot, ext.at[1, pl.ds(0, TOKENS)], local.at[1]),
    ]
    for i in (7, 1, 3, 0, 2, 5, 4, 6, 8):
        loads.append(pltpu.make_async_copy(fetched[i], held_here[i], local.at[3 + i]))
    for load in loads:
        load.start()

    lat, lon, spot, core = place()
    lats, lons = lax.axis_size("lat"), lax.axis_size("lon")
    sibling = device_at(spot, 1 - core)
    down, up = (lat + 1) % lats, (lat + lats - 1) % lats
    east, west = (lon + 1) % lons, (lon + lons - 1) % lons
    peers = [sibling, (down, lon), (up, lon), (lat, east), (lat, west), (down, east), (up, west)]
    for axes in ("xy", "xz", "yz"):
        for i in range(4):
            for j in range(4):
                if (i or j) and (j or axes == "xy") and (i or axes != "yz"):
                    there = {axis: spot[axis] for axis in "xyz"}
                    there[axes[0]] = (spot[axes[0]] + i) % 4
                    there[axes[1]] = (spot[axes[1]] + j) % 4
                    peers.append(device_at(there, core))
    barrier = pltpu.get_barrier_semaphore()
    for peer in peers:
        pl.semaphore_signal(barrier, inc=1, device_id=peer, device_id_type=MESH)

    count = [0]

    def remote(src, dst, peer):
        i = count[0]
        count[0] += 1
        copy = pltpu.make_async_remote_copy(
            src_ref=src, dst_ref=dst, send_sem=send.at[i], recv_sem=recv.at[i],
            device_id=peer, device_id_type=MESH,
        )
        copy.start()
        return copy

    for load in loads[:3]:
        load.wait()
    for i in range(2):
        side_out[i] = nn(pick[...], ext[i, 0:TOKENS]).astype(BF16)
    pl.semaphore_wait(barrier, len(peers))
    main, angle = pl.ds(0, SIDE), pl.ds(SIDE, EDGE - SIDE)
    halo = [
        remote(side_out.at[:, main], side.at[:, main], (lat, west)),
        remote(ext.at[:, pl.ds(0, LEAD)], ext.at[:, pl.ds(TOKENS, LEAD)], (up, lon)),
        remote(side_out.at[:, angle], side.at[:, angle], (up, west)),
    ]

    def forward(pieces):
        gathered = []
        for i in range(2):
            parts = []
            for a, lo, hi in pieces:
                start = LEAD + a * BAND
                first = lo // SPAN * PIECE
                first_row = first // 16 * 16
                last = hi // SPAN * PIECE
                rows = perm[first_row : -(-last // 16) * 16]
                thirds = [
                    nn(rows, ext[i, start + j * TWO : start + (j + 1) * TWO])[first - first_row :]
                    for j in range(3)
                ]
                got = [
                    third[at : at + PIECE] for at in range(0, last - first, PIECE) for third in thirds
                ]
                got = jnp.concatenate(got, axis=0)
                if hi == BAND:
                    width = EDGE if a == BANDS - 1 else SIDE
                    edge = nn(beside[a, :, 0:width], side[i, 0:width])
                    if lo < LAST:
                        got = jnp.concatenate([got[: LAST - lo], got[LAST - lo :] + edge], axis=0)
                    else:
                        got = got + edge[lo - LAST :]
                parts.append(got)
            gathered.append(jnp.concatenate(parts, axis=0))
        x, cot = gathered
        center = x - jnp.mean(x, axis=-1, keepdims=True)
        inv = lax.rsqrt(jnp.mean(center * center, axis=-1, keepdims=True) + 1e-05)
        norm = center * inv
        sc = norm * gain[...]
        qkv_now = nn(sc.astype(BF16), wqkv[...]).astype(BF16).astype(F32)
        att_now = nt(cot.astype(BF16), wproj[...]).astype(BF16).astype(F32)
        at = 0
        for a, lo, hi in pieces:
            dst = slice(a * BAND + lo, a * BAND + hi)
            src = slice(at, at + hi - lo)
            at += hi - lo
            normed[dst] = norm[src]
            inv_std[dst] = jnp.broadcast_to(inv[src], (hi - lo, 128))
            scaled[dst] = sc[src]
            cot_win[dst] = cot[src]
            qkv[dst] = qkv_now[src]
            grad_att[dst] = att_now[src]

    lane = lax.broadcasted_iota(jnp.int32, (1, 128), 1) // HEAD
    masks = [(lane == j).astype(F32) for j in range(GROUP)]
    key_half = lax.broadcasted_iota(jnp.int32, (SPAN, SPAN), 0) >= HALF_LAT * WIN_LON
    query_half = lax.broadcasted_iota(jnp.int32, (SPAN, SPAN), 1) >= HALF_LAT * WIN_LON
    parted = jnp.where(key_half == query_half, 0.0, -1e30)
    parted = jnp.concatenate([parted] * GROUP, axis=1)

    def stacked(x):
        return jnp.concatenate([x * m for m in masks], axis=0).astype(BF16)

    def by_head(x):
        x = x.reshape(GROUP, SPAN, 128)
        y = x[GROUP - 1]
        for j in range(GROUP - 2, -1, -1):
            y = jnp.where(lane == j, x[j], y)
        return y

    scale = HEAD ** (-0.5)

    def attention(windows, edge=False):
        shut = parted * jnp.where(lat == lats - 1, 1.0, 0.0)
        todo = []
        for w in windows:
            rows = pl.ds(pl.multiple_of(w * SPAN, 8), SPAN)
            todo += [(rows, [slice(j * C + lo, j * C + lo + 128) for j in range(3)])
                     for lo in range(0, C, 128)]
        q = [stacked(qkv[rows, cols[0]]) for rows, cols in todo]
        k = [qkv[rows, cols[1]].astype(BF16) for rows, cols in todo]
        v = [qkv[rows, cols[2]].astype(BF16) for rows, cols in todo]
        da = [stacked(grad_att[rows, cols[0]]) for rows, cols in todo]
        n = range(len(todo))
        s = [nt(k[i], q[i]) * scale for i in n]
        if edge:
            s = [x + shut for x in s]
        gp = [nt(v[i], da[i]) for i in n]
        ex = [jnp.exp(x - jnp.max(x, axis=0, keepdims=True)) for x in s]
        prob = [x * (1.0 / jnp.sum(x, axis=0, keepdims=True)) for x in ex]
        inner = [jnp.sum(prob[i] * gp[i], axis=0, keepdims=True) for i in n]
        gs = [(prob[i] * (gp[i] - inner[i]) * scale).astype(BF16) for i in n]
        pb = [x.astype(BF16) for x in prob]
        found = [by_head(tn(pb[i], v[i])) for i in n]
        grad_q = [by_head(tn(gs[i], k[i])) for i in n]
        grad_k = [nn(gs[i], q[i]) for i in n]
        grad_v = [nn(pb[i], da[i]) for i in n]
        for i, (rows, cols) in enumerate(todo):
            att[rows, cols[0]] = found[i]
            grad_all[rows, cols[0]] = grad_q[i]
            grad_all[rows, cols[1]] = grad_k[i]
            grad_all[rows, cols[2]] = grad_v[i]

    for load in loads[3:8]:
        load.wait()
    inner = (PER_BAND - 1) * SPAN
    forward([(a, 0, inner) for a in range(BANDS - 1)])

    def early(i, carry):
        attention([i * PER_BAND + b for b in range(PER_BAND - 1)])
        return carry

    lax.fori_loop(0, BANDS - 1, early, 0)
    def weight_sums(pieces, halves, found):
        def tokens(ref, cols):
            parts = [ref[lo:hi, cols] for lo, hi in pieces]
            return jnp.concatenate(parts, axis=0).astype(BF16)

        if not found:
            found += [tokens(scaled, slice(0, C)).T, tokens(att, slice(0, C)).T]
        for half in halves:
            lo = half * 256
            for j in range(3):
                yield 4 * half + j, nn(found[0], tokens(grad_all, slice(j * C + lo, j * C + lo + 256)))
            yield 4 * half + 3, nn(found[1], tokens(cot_win, slice(lo, lo + 256)))

    starts = [a * BAND for a in range(BANDS - 1)]
    for i, value in weight_sums([(start, start + inner) for start in starts], (0, 1), []):
        grads[i] = value
    halo[0].wait_recv()
    forward([(a, inner, BAND) for a in range(BANDS - 1)])
    attention([a * PER_BAND + PER_BAND - 1 for a in range(BANDS - 1)])
    halo[1].wait_recv()
    halo[2].wait_recv()
    forward([(BANDS - 1, 0, BAND)])

    def late(i, carry):
        attention([(BANDS - 1) * PER_BAND + 2 * i + b for b in range(2)], edge=True)
        return carry

    lax.fori_loop(0, PER_BAND // 2, late, 0)

    late_rows = [(start + inner, start + BAND) for start in starts] + [(TOKENS - BAND, TOKENS)]
    turned_once = []
    upper = lax.broadcasted_iota(jnp.int32, (1, 8, 1), 1) < 4
    first_core = lax.broadcasted_iota(jnp.int32, (1, 8, 1), 1) * 0 + core == 0
    first = []
    for half in range(2):
        lo = half * 256
        lanes = slice(lo, lo + 256)
        for i, value in weight_sums(late_rows, (half,), turned_once):
            grads[i] += value

        def pack(i, carry):
            rows = pl.ds(pl.multiple_of(i * 64, 64), 64)
            chips = pl.ds(i * 8, 8)
            t = [grads[4 * half + j, rows].reshape(8, 8, 256) for j in range(4)]
            turned = [pltpu.roll(x, 4, 1) for x in t]
            block = []
            for near, far in ((t, turned), (turned, t)):
                block.append(
                    jnp.concatenate(
                        [jnp.where(upper, near[j], far[j + 1]) for j in (0, 2)], axis=1
                    )
                )
            is_first = jnp.concatenate([first_core, first_core], axis=1)
            mine[chips, :, lanes] = jnp.where(is_first, block[0], block[1])
            theirs[chips, :, lanes] = jnp.where(is_first, block[1], block[0]).astype(BF16)
            return carry

        lax.fori_loop(0, 8, pack, 0, unroll=2)
        for start, width, _, _ in PARTS:
            if lo <= start < lo + 256:
                span = pl.ds(start, width)
                first.append(remote(theirs.at[:, :, span], got0.at[:, :, span], sibling))

    back, edges = [], []
    for load in loads[8:]:
        load.wait()

    def backward(a):
        dst = slice(a * BAND, (a + 1) * BAND)
        gn = nt(grad_all[dst].astype(BF16), wqkv[...]) * gain[...]
        norm = normed[dst]
        branch = inv_std[dst][:, 0:1] * (
            gn
            - jnp.mean(gn, axis=-1, keepdims=True)
            - norm * jnp.mean(gn * norm, axis=-1, keepdims=True)
        )
        done = cot_win[dst] + branch
        for j in range(3):
            at = [b * SPAN + j * PIECE for b in range(PER_BAND)]
            part = jnp.concatenate([done[i : i + PIECE] for i in at], axis=0).astype(BF16)
            slab = slice(a * BAND + j * TWO, a * BAND + (j + 1) * TWO)
            out_ext[slab] = nn(perm_t[...], part).astype(BF16)
        edges.append(nn(beside_t[a], done[LAST:].astype(BF16)))
        if a == BANDS - 1:
            back.append(remote(out_ext.at[pl.ds(TOKENS - LEAD, LEAD)], top, (down, lon)))
        if len(edges) == BANDS:
            back_side[...] = (edges[0] + edges[1] + edges[2] + edges[3]).astype(BF16)
            back.append(remote(back_side.at[main], left.at[main], (lat, east)))
            back.append(remote(back_side.at[angle], left.at[angle], (down, east)))

    def role(p, r, axis):
        first_order, second_order = PARTS[p][2:]
        return (1 - core) * int(first_order[r] == axis) + core * int(second_order[r] == axis)

    def by_role(p, steps):
        return {axis: sum(role(p, r, axis) * steps[r] for r in range(3)) for axis in "xyz"}

    def my_role(p, r):
        return sum(role(p, r, axis) * spot[axis] for axis in "xyz")

    def peer_at(p, steps):
        moved = by_role(p, steps)
        return device_at({axis: (spot[axis] + moved[axis]) % 4 for axis in "xyz"}, core)

    def summed0(p, chip):
        lo, width = PARTS[p][:2]
        lanes = slice(lo, lo + width)
        return mine[chip, :, lanes] + got0[chip, :, lanes].astype(F32)

    sent = [[] for _ in PARTS]

    def stage0(p):
        held, got = buffers[5 * p : 5 * p + 2]
        first[p].wait_recv()

        def add(i, carry):
            at = (i // 16, i // 4 % 4, i % 4)
            held[at] = summed0(p, chip_at(by_role(p, at))).astype(BF16)
            return carry

        lax.fori_loop(0, 64, add, 0, unroll=8)
        for k in (2, 1, 3):
            sent[p].append(
                remote(held.at[(my_role(p, 0) + k) % 4], got.at[k - 1], peer_at(p, (k, 0, 0)))
            )

    def stage1(p):
        got, nxt, nxt_got, keep = buffers[5 * p + 1 : 5 * p + 5]
        for copy in sent[p]:
            copy.wait_recv()
        here = my_role(p, 0)
        b, c = my_role(p, 1), my_role(p, 2)

        def total(i, j):
            x = summed0(p, chip_at(by_role(p, (here, i, j))))
            for k in range(3):
                x = x + got[k, i, j].astype(F32)
            return x

        def add(i, carry):
            nxt[i // 4, i % 4] = total(i // 4, i % 4).astype(BF16)
            return carry

        lax.fori_loop(0, 16, add, 0, unroll=8)
        keep[...] = total(b, c)
        for i in (2, 1, 3, 0):
            for j in (2, 1, 3, 0):
                if i or j:
                    sent[p].append(
                        remote(
                            nxt.at[(b + i) % 4, (c + j) % 4],
                            nxt_got.at[4 * i + j - 1],
                            peer_at(p, (0, i, j)),
                        )
                    )

    def stage2(p):
        got, keep = buffers[5 * p + 3 : 5 * p + 5]
        for copy in sent[p][3:]:
            copy.wait_recv()
        x = keep[...]
        for i in range(15):
            x = x + got[i].astype(F32)
        return x

    backward(BANDS - 1)
    stage0(0)
    stage0(1)
    stage0(2)
    for a in range(BANDS - 1):
        backward(a)
    for p in range(len(PARTS)):
        stage1(p)

    me = lat * lons + lon
    picked = lax.broadcasted_iota(jnp.int32, (8, C), 0) + me * 4
    picked = (picked == lax.broadcasted_iota(jnp.int32, (8, C), 1)).astype(F32)
    w_rows = nn(picked.astype(BF16), wqkv[...])
    gain_rows = jnp.sum(picked * gain[...], axis=1, keepdims=True)

    for copy in back:
        copy.wait_recv()
    out_ref[LEAD:] = (
        out_ext[0 : TOKENS - LEAD].astype(F32) + nn(pick_t[LEAD:, 0:SIDE], left[0:SIDE])
    ).astype(BF16)
    out_ref[0:LEAD] = (top[...].astype(F32) + nn(pick_t[0:LEAD], left[...])).astype(BF16)
    store = pltpu.make_async_copy(out_ref, out_hbm, local.at[2])
    store.start()

    for copy in halo + first + back + [c for part in sent for c in part[:3]]:
        copy.wait_send()
    total = jnp.concatenate([stage2(p) for p in range(len(PARTS))], axis=1)
    total = total * (1.0 / math.sqrt(TOKENS * lats * lons))
    gqkv = [total[4 * j : 4 * j + 4] for j in range(3)]
    gqkv_ref[...] = jnp.concatenate(gqkv, axis=1)
    gproj_ref[...] = total[12:16]
    dots = jnp.zeros((4, 1), F32)
    for j in range(3):
        dots = dots + jnp.sum(gqkv[j] * w_rows[0:4, j * C : (j + 1) * C], axis=1, keepdims=True)
    dots = dots / gain_rows[0:4]
    diagonal = lax.broadcasted_iota(jnp.int32, (4, 128), 0)
    diagonal = diagonal == lax.broadcasted_iota(jnp.int32, (4, 128), 1)
    ggain_ref[...] = jnp.sum(jnp.where(diagonal, dots, 0.0), axis=0, keepdims=True)
    for copy in [c for part in sent for c in part[3:]]:
        copy.wait_send()
    store.wait()


def sublayer(*args):
    vmem = pl.BlockSpec(memory_space=pltpu.VMEM)
    hbm = pl.BlockSpec(memory_space=pl.ANY)
    scratch = [
        pltpu.VMEM((2, TOKENS + LEAD, C), BF16),
        pltpu.VMEM((2, EDGE, C), BF16),
        pltpu.VMEM((2, EDGE, C), BF16),
        pltpu.VMEM((TOKENS, C), F32),
        pltpu.VMEM((TOKENS, 128), F32),
        pltpu.VMEM((TOKENS, C), F32),
        pltpu.VMEM((TOKENS, C), F32),
        pltpu.VMEM((TOKENS, 3 * C), F32),
        pltpu.VMEM((TOKENS, C), F32),
        pltpu.VMEM((TOKENS, C), F32),
        pltpu.VMEM((TOKENS, 3 * C), F32),
        pltpu.VMEM((TOKENS, C), BF16),
        pltpu.VMEM((EDGE, C), BF16),
        pltpu.VMEM((LEAD, C), BF16),
        pltpu.VMEM((EDGE, C), BF16),
        pltpu.VMEM((8, C, 256), F32),
        pltpu.VMEM((64, 16, C), F32),
        pltpu.VMEM((64, 16, C), BF16),
        pltpu.VMEM((64, 16, C), BF16),
        pltpu.VMEM((TOKENS, C), BF16),
    ]
    scratch += [pltpu.VMEM(x.shape, x.dtype) for x in args[2:]]
    for _, width, _, _ in PARTS:
        for dims in ((4, 4, 4), (3, 4, 4), (4, 4), (15,)):
            scratch.append(pltpu.VMEM(dims + (16, width), BF16))
        scratch.append(pltpu.VMEM((16, width), F32))
    copies = 3 + 3 + 19 * len(PARTS)
    return pl.pallas_call(
        sublayer_kernel,
        out_shape=(
            jax.ShapeDtypeStruct((TOKENS, C), BF16),
            jax.ShapeDtypeStruct((4, 3 * C), F32),
            jax.ShapeDtypeStruct((4, C), F32),
            jax.ShapeDtypeStruct((1, 128), F32),
        ),
        in_specs=[hbm] * 11,
        out_specs=(hbm, vmem, vmem, vmem),
        scratch_shapes=scratch
        + [
            pltpu.SemaphoreType.DMA((12,)),
            pltpu.SemaphoreType.DMA((copies,)),
            pltpu.SemaphoreType.DMA((copies,)),
        ],
        compiler_params=pltpu.CompilerParams(
            collective_id=1, has_side_effects=True, vmem_limit_bytes=62 * 1024 * 1024
        ),
        name="window_grads",
    )(*args)


def hand_on_kernel(out_ref, gqkv_ref, gproj_ref, gain_ref, out, gqkv, gproj, ggain):
    out[...] = out_ref[...]
    gqkv[...] = gqkv_ref[...]
    gproj[...] = gproj_ref[...]
    ggain[...] = gain_ref[0, 0:4]


def hand_on(*args):
    def whole(*shape):
        return pl.BlockSpec(shape, lambda i: (0,) * len(shape))

    tokens = pl.BlockSpec((TOKENS // 2, C), lambda i: (i, 0))
    return pl.pallas_call(
        hand_on_kernel,
        grid=(2,),
        out_shape=(
            jax.ShapeDtypeStruct((TOKENS, C), BF16),
            jax.ShapeDtypeStruct((4, 3 * C), F32),
            jax.ShapeDtypeStruct((4, C), F32),
            jax.ShapeDtypeStruct((4,), F32),
        ),
        in_specs=[tokens, whole(4, 3 * C), whole(4, C), whole(1, 128)],
        out_specs=(tokens, whole(4, 3 * C), whole(4, C), whole(4)),
        compiler_params=pltpu.CompilerParams(vmem_limit_bytes=62 * 1024 * 1024),
        name="hand_on",
    )(*args)


def on_device(activations, cotangent, norm_gain, qkv_weight, proj_weight):
    results = sublayer(
        activations.reshape(TOKENS, C),
        cotangent.reshape(TOKENS, C),
        norm_gain.reshape(1, C),
        qkv_weight,
        proj_weight,
        *orders(),
    )
    grad_input, gqkv, gproj, ggain = hand_on(*results)
    return grad_input.reshape(ROWS, COLS, C), gqkv, gproj, ggain


def solution(mesh):
    return jax.shard_map(
        on_device,
        mesh=mesh,
        in_specs=(P("lat", "lon", None), P("lat", "lon", None), P(), P(), P()),
        out_specs=(
            P("lat", "lon", None),
            P(("lat", "lon"), None),
            P(("lat", "lon"), None),
            P(("lat", "lon")),
        ),
        check_vma=False,
    )
```

```python
import math

import jax
import jax.numpy as jnp
import numpy as np
from jax import lax
from jax.experimental import pallas as pl
from jax.experimental.pallas import tpu as pltpu
from jax.sharding import PartitionSpec as P

C = 512
HEADS = 16
HEAD = C // HEADS
WIN_LAT = 6
WIN_LON = 12
SPAN = WIN_LAT * WIN_LON
ROWS = 24
COLS = 48
BANDS = ROWS // WIN_LAT
PER_BAND = COLS // WIN_LON
BAND = WIN_LAT * COLS
TOKENS = ROWS * COLS
HALF_LAT = WIN_LAT // 2
HALF_LON = WIN_LON // 2
SIDE = 128
EDGE = SIDE + 32
LAST = 208
TWO = 2 * COLS
PIECE = 2 * WIN_LON
GROUP = 128 // HEAD
F32 = jnp.float32
BF16 = jnp.bfloat16


def orders():
    perm = np.zeros((TWO, TWO), np.float32)
    beside = np.zeros((BANDS, BAND - LAST, EDGE), np.float32)
    pick = np.zeros((EDGE, TOKENS), np.float32)
    for b in range(PER_BAND):
        for r in range(WIN_LAT):
            for c in range(WIN_LON):
                col = WIN_LON * b + HALF_LON + c
                token = b * SPAN + r * WIN_LON + c
                if col < COLS:
                    if r < 2:
                        perm[b * PIECE + r * WIN_LON + c, r * COLS + col] = 1.0
                    continue
                for a in range(BANDS):
                    beside[a, token - LAST, edge_row(a * WIN_LAT + HALF_LAT + r, col - COLS)] = 1.0
    for row in range(ROWS):
        for c in range(HALF_LON):
            pick[edge_row(row + (ROWS if row < HALF_LAT else 0), c), row * COLS + c] = 1.0
    return [jnp.asarray(x, BF16) for x in (perm, perm.T, beside, beside.transpose(0, 2, 1), pick, pick.T)]


def edge_row(row, col):
    if row < ROWS:
        return (row - HALF_LAT) * HALF_LON + col
    return SIDE + (row - ROWS) * HALF_LON + col


def nn(a, b):
    return lax.dot_general(a, b, (((1,), (0,)), ((), ())), preferred_element_type=F32)


def nt(a, b):
    return lax.dot_general(a, b, (((1,), (1,)), ((), ())), preferred_element_type=F32)


def tn(a, b):
    return lax.dot_general(a, b, (((0,), (0,)), ((), ())), preferred_element_type=F32)


PARTS = ((0, 256, "zyx", "yxz"), (256, 128, "yxz", "zyx"), (384, 128, "xzy", "xzy"))
MESH = pl.DeviceIdType.MESH
LEAD = HALF_LAT * COLS


def place():
    lat, lon = lax.axis_index("lat"), lax.axis_index("lon")
    spot = {"z": lat // 2, "x": (lon // 2) % 2 * 2 + lat % 2, "y": lon // 4}
    return lat, lon, spot, lon % 2


def device_at(spot, core):
    return (spot["z"] * 2 + spot["x"] % 2, spot["y"] * 4 + spot["x"] // 2 * 2 + core)


def chip_at(at):
    return at["z"] * 16 + at["x"] % 2 * 8 + at["y"] * 2 + at["x"] // 2


def sublayer_kernel(
    own_in, own_cot, *rest,
):
    fetched, rest = rest[:9], rest[9:]
    (
        out_hbm, gqkv_ref, gproj_ref, ggain_ref,
        ext, side, side_out,
        normed, inv_std, scaled, cot_win, qkv, grad_att, att, grad_all,
        out_ext, back_side, top, left, grads, mine, theirs, got0, out_ref,
    ) = rest[:24]
    held_here, rest = rest[24:33], rest[33:]
    gain, wqkv, wproj, perm, perm_t, beside, beside_t, pick, pick_t = held_here
    buffers, (local, send, recv) = rest[:-3], rest[-3:]
    loads = [
        pltpu.make_async_copy(own_in, ext.at[0, pl.ds(0, TOKENS)], local.at[0]),
        pltpu.make_async_copy(own_cot, ext.at[1, pl.ds(0, TOKENS)], local.at[1]),
    ]
    for i in (7, 1, 3, 0, 2, 5, 4, 6, 8):
        loads.append(pltpu.make_async_copy(fetched[i], held_here[i], local.at[3 + i]))
    for load in loads:
        load.start()

    lat, lon, spot, core = place()
    lats, lons = lax.axis_size("lat"), lax.axis_size("lon")
    sibling = device_at(spot, 1 - core)
    down, up = (lat + 1) % lats, (lat + lats - 1) % lats
    east, west = (lon + 1) % lons, (lon + lons - 1) % lons
    peers = [sibling, (down, lon), (up, lon), (lat, east), (lat, west), (down, east), (up, west)]
    for axes in ("xy", "xz", "yz"):
        for i in range(4):
            for j in range(4):
                if (i or j) and (j or axes == "xy") and (i or axes != "yz"):
                    there = {axis: spot[axis] for axis in "xyz"}
                    there[axes[0]] = (spot[axes[0]] + i) % 4
                    there[axes[1]] = (spot[axes[1]] + j) % 4
                    peers.append(device_at(there, core))
    barrier = pltpu.get_barrier_semaphore()
    for peer in peers:
        pl.semaphore_signal(barrier, inc=1, device_id=peer, device_id_type=MESH)

    count = [0]

    def remote(src, dst, peer):
        i = count[0]
        count[0] += 1
        copy = pltpu.make_async_remote_copy(
            src_ref=src, dst_ref=dst, send_sem=send.at[i], recv_sem=recv.at[i],
            device_id=peer, device_id_type=MESH,
        )
        copy.start()
        return copy

    for load in loads[:3]:
        load.wait()
    for i in range(2):
        side_out[i] = nn(pick[...], ext[i, 0:TOKENS]).astype(BF16)
    pl.semaphore_wait(barrier, len(peers))
    main, angle = pl.ds(0, SIDE), pl.ds(SIDE, EDGE - SIDE)
    halo = [
        remote(side_out.at[:, main], side.at[:, main], (lat, west)),
        remote(ext.at[:, pl.ds(0, LEAD)], ext.at[:, pl.ds(TOKENS, LEAD)], (up, lon)),
        remote(side_out.at[:, angle], side.at[:, angle], (up, west)),
    ]

    def forward(pieces):
        gathered = []
        for i in range(2):
            parts = []
            for a, lo, hi in pieces:
                start = LEAD + a * BAND
                first = lo // SPAN * PIECE
                first_row = first // 16 * 16
                last = hi // SPAN * PIECE
                rows = perm[first_row : -(-last // 16) * 16]
                thirds = [
                    nn(rows, ext[i, start + j * TWO : start + (j + 1) * TWO])[first - first_row :]
                    for j in range(3)
                ]
                got = [
                    third[at : at + PIECE] for at in range(0, last - first, PIECE) for third in thirds
                ]
                got = jnp.concatenate(got, axis=0)
                if hi == BAND:
                    width = EDGE if a == BANDS - 1 else SIDE
                    edge = nn(beside[a, :, 0:width], side[i, 0:width])
                    if lo < LAST:
                        got = jnp.concatenate([got[: LAST - lo], got[LAST - lo :] + edge], axis=0)
                    else:
                        got = got + edge[lo - LAST :]
                parts.append(got)
            gathered.append(jnp.concatenate(parts, axis=0))
        x, cot = gathered
        center = x - jnp.mean(x, axis=-1, keepdims=True)
        inv = lax.rsqrt(jnp.mean(center * center, axis=-1, keepdims=True) + 1e-05)
        norm = center * inv
        sc = norm * gain[...]
        qkv_now = nn(sc.astype(BF16), wqkv[...]).astype(BF16).astype(F32)
        att_now = nt(cot.astype(BF16), wproj[...]).astype(BF16).astype(F32)
        at = 0
        for a, lo, hi in pieces:
            dst = slice(a * BAND + lo, a * BAND + hi)
            src = slice(at, at + hi - lo)
            at += hi - lo
            normed[dst] = norm[src]
            inv_std[dst] = jnp.broadcast_to(inv[src], (hi - lo, 128))
            scaled[dst] = sc[src]
            cot_win[dst] = cot[src]
            qkv[dst] = qkv_now[src]
            grad_att[dst] = att_now[src]

    lane = lax.broadcasted_iota(jnp.int32, (1, 128), 1) // HEAD
    masks = [(lane == j).astype(F32) for j in range(GROUP)]
    key_half = lax.broadcasted_iota(jnp.int32, (SPAN, SPAN), 0) >= HALF_LAT * WIN_LON
    query_half = lax.broadcasted_iota(jnp.int32, (SPAN, SPAN), 1) >= HALF_LAT * WIN_LON
    parted = jnp.where(key_half == query_half, 0.0, -1e30)
    parted = jnp.concatenate([parted] * GROUP, axis=1)

    def stacked(x):
        return jnp.concatenate([x * m for m in masks], axis=0).astype(BF16)

    def by_head(x):
        x = x.reshape(GROUP, SPAN, 128)
        y = x[GROUP - 1]
        for j in range(GROUP - 2, -1, -1):
            y = jnp.where(lane == j, x[j], y)
        return y

    scale = HEAD ** (-0.5)

    def attention(windows, edge=False):
        shut = parted * jnp.where(lat == lats - 1, 1.0, 0.0)
        todo = []
        for w in windows:
            rows = pl.ds(pl.multiple_of(w * SPAN, 8), SPAN)
            todo += [(rows, [slice(j * C + lo, j * C + lo + 128) for j in range(3)])
                     for lo in range(0, C, 128)]
        q = [stacked(qkv[rows, cols[0]]) for rows, cols in todo]
        k = [qkv[rows, cols[1]].astype(BF16) for rows, cols in todo]
        v = [qkv[rows, cols[2]].astype(BF16) for rows, cols in todo]
        da = [stacked(grad_att[rows, cols[0]]) for rows, cols in todo]
        n = range(len(todo))
        s = [nt(k[i], q[i]) * scale for i in n]
        if edge:
            s = [x + shut for x in s]
        gp = [nt(v[i], da[i]) for i in n]
        ex = [jnp.exp(x - jnp.max(x, axis=0, keepdims=True)) for x in s]
        prob = [x * (1.0 / jnp.sum(x, axis=0, keepdims=True)) for x in ex]
        inner = [jnp.sum(prob[i] * gp[i], axis=0, keepdims=True) for i in n]
        gs = [(prob[i] * (gp[i] - inner[i]) * scale).astype(BF16) for i in n]
        pb = [x.astype(BF16) for x in prob]
        found = [by_head(tn(pb[i], v[i])) for i in n]
        grad_q = [by_head(tn(gs[i], k[i])) for i in n]
        grad_k = [nn(gs[i], q[i]) for i in n]
        grad_v = [nn(pb[i], da[i]) for i in n]
        for i, (rows, cols) in enumerate(todo):
            att[rows, cols[0]] = found[i]
            grad_all[rows, cols[0]] = grad_q[i]
            grad_all[rows, cols[1]] = grad_k[i]
            grad_all[rows, cols[2]] = grad_v[i]

    for load in loads[3:8]:
        load.wait()
    inner = (PER_BAND - 1) * SPAN
    forward([(a, 0, inner) for a in range(BANDS - 1)])

    def early(i, carry):
        attention([i * PER_BAND + b for b in range(PER_BAND - 1)])
        return carry

    lax.fori_loop(0, BANDS - 1, early, 0)
    def weight_sums(pieces, halves, found):
        def tokens(ref, cols):
            parts = [ref[lo:hi, cols] for lo, hi in pieces]
            return jnp.concatenate(parts, axis=0).astype(BF16)

        if not found:
            found += [tokens(scaled, slice(0, C)).T, tokens(att, slice(0, C)).T]
        for half in halves:
            lo = half * 256
            for j in range(3):
                yield 4 * half + j, nn(found[0], tokens(grad_all, slice(j * C + lo, j * C + lo + 256)))
            yield 4 * half + 3, nn(found[1], tokens(cot_win, slice(lo, lo + 256)))

    starts = [a * BAND for a in range(BANDS - 1)]
    for i, value in weight_sums([(start, start + inner) for start in starts], (0, 1), []):
        grads[i] = value
    halo[0].wait_recv()
    forward([(a, inner, BAND) for a in range(BANDS - 1)])
    attention([a * PER_BAND + PER_BAND - 1 for a in range(BANDS - 1)])
    halo[1].wait_recv()
    halo[2].wait_recv()
    forward([(BANDS - 1, 0, BAND)])

    def late(i, carry):
        attention([(BANDS - 1) * PER_BAND + 2 * i + b for b in range(2)], edge=True)
        return carry

    lax.fori_loop(0, PER_BAND // 2, late, 0)

    late_rows = [(start + inner, start + BAND) for start in starts] + [(TOKENS - BAND, TOKENS)]
    turned_once = []
    upper = lax.broadcasted_iota(jnp.int32, (1, 8, 1), 1) < 4
    first_core = lax.broadcasted_iota(jnp.int32, (1, 8, 1), 1) * 0 + core == 0
    first = []
    for half in range(2):
        lo = half * 256
        lanes = slice(lo, lo + 256)
        for i, value in weight_sums(late_rows, (half,), turned_once):
            grads[i] += value

        def pack(i, carry):
            rows = pl.ds(pl.multiple_of(i * 64, 64), 64)
            chips = pl.ds(i * 8, 8)
            t = [grads[4 * half + j, rows].reshape(8, 8, 256) for j in range(4)]
            turned = [pltpu.roll(x, 4, 1) for x in t]
            block = []
            for near, far in ((t, turned), (turned, t)):
                block.append(
                    jnp.concatenate(
                        [jnp.where(upper, near[j], far[j + 1]) for j in (0, 2)], axis=1
                    )
                )
            is_first = jnp.concatenate([first_core, first_core], axis=1)
            mine[chips, :, lanes] = jnp.where(is_first, block[0], block[1])
            theirs[chips, :, lanes] = jnp.where(is_first, block[1], block[0]).astype(BF16)
            return carry

        lax.fori_loop(0, 8, pack, 0, unroll=2)
        for start, width, _, _ in PARTS:
            if lo <= start < lo + 256:
                span = pl.ds(start, width)
                first.append(remote(theirs.at[:, :, span], got0.at[:, :, span], sibling))

    back = []
    for load in loads[8:]:
        load.wait()

    def norm_grads(pieces):
        def tokens(ref):
            return jnp.concatenate([ref[lo:hi] for lo, hi in pieces], axis=0)

        gn = nt(tokens(grad_all).astype(BF16), wqkv[...]) * gain[...]
        norm = tokens(normed)
        branch = tokens(inv_std)[:, 0:1] * (
            gn
            - jnp.mean(gn, axis=-1, keepdims=True)
            - norm * jnp.mean(gn * norm, axis=-1, keepdims=True)
        )
        done = tokens(cot_win) + branch
        at = 0
        for lo, hi in pieces:
            normed[lo:hi] = done[at : at + hi - lo]
            at += hi - lo

    def to_slab(a):
        for j in range(3):
            at = [a * BAND + b * SPAN + j * PIECE for b in range(PER_BAND)]
            part = jnp.concatenate([normed[i : i + PIECE] for i in at], axis=0).astype(BF16)
            slab = slice(a * BAND + j * TWO, a * BAND + (j + 1) * TWO)
            out_ext[slab] = nn(perm_t[...], part).astype(BF16)

    def role(p, r, axis):
        first_order, second_order = PARTS[p][2:]
        return (1 - core) * int(first_order[r] == axis) + core * int(second_order[r] == axis)

    def by_role(p, steps):
        return {axis: sum(role(p, r, axis) * steps[r] for r in range(3)) for axis in "xyz"}

    def my_role(p, r):
        return sum(role(p, r, axis) * spot[axis] for axis in "xyz")

    def peer_at(p, steps):
        moved = by_role(p, steps)
        return device_at({axis: (spot[axis] + moved[axis]) % 4 for axis in "xyz"}, core)

    def summed0(p, chip):
        lo, width = PARTS[p][:2]
        lanes = slice(lo, lo + width)
        return mine[chip, :, lanes] + got0[chip, :, lanes].astype(F32)

    sent = [[] for _ in PARTS]

    def stage0(p):
        held, got = buffers[5 * p : 5 * p + 2]
        first[p].wait_recv()

        def add(i, carry):
            at = (i // 16, i // 4 % 4, i % 4)
            held[at] = summed0(p, chip_at(by_role(p, at))).astype(BF16)
            return carry

        lax.fori_loop(0, 64, add, 0, unroll=8)
        for k in (2, 1, 3):
            sent[p].append(
                remote(held.at[(my_role(p, 0) + k) % 4], got.at[k - 1], peer_at(p, (k, 0, 0)))
            )

    def stage1(p):
        got, nxt, nxt_got, keep = buffers[5 * p + 1 : 5 * p + 5]
        for copy in sent[p]:
            copy.wait_recv()
        here = my_role(p, 0)
        b, c = my_role(p, 1), my_role(p, 2)

        def total(i, j):
            x = summed0(p, chip_at(by_role(p, (here, i, j))))
            for k in range(3):
                x = x + got[k, i, j].astype(F32)
            return x

        def add(i, carry):
            nxt[i // 4, i % 4] = total(i // 4, i % 4).astype(BF16)
            return carry

        lax.fori_loop(0, 16, add, 0, unroll=8)
        keep[...] = total(b, c)
        for i in (2, 1, 3, 0):
            for j in (2, 1, 3, 0):
                if i or j:
                    sent[p].append(
                        remote(
                            nxt.at[(b + i) % 4, (c + j) % 4],
                            nxt_got.at[4 * i + j - 1],
                            peer_at(p, (0, i, j)),
                        )
                    )

    def stage2(p):
        got, keep = buffers[5 * p + 3 : 5 * p + 5]
        for copy in sent[p][3:]:
            copy.wait_recv()
        x = keep[...]
        for i in range(15):
            x = x + got[i].astype(F32)
        return x

    norm_grads([(TOKENS - BAND, TOKENS)])
    to_slab(BANDS - 1)
    back.append(remote(out_ext.at[pl.ds(TOKENS - LEAD, LEAD)], top, (down, lon)))
    stage0(0)
    stage0(1)
    stage0(2)
    norm_grads([(start + inner, start + BAND) for start in starts])
    edges = jnp.zeros((EDGE, C), F32)
    for a in range(BANDS):
        rows = normed[a * BAND + LAST : (a + 1) * BAND].astype(BF16)
        edges = edges + nn(beside_t[a], rows)
    back_side[...] = edges.astype(BF16)
    back.append(remote(back_side.at[main], left.at[main], (lat, east)))
    back.append(remote(back_side.at[angle], left.at[angle], (down, east)))
    norm_grads([(start, start + inner) for start in starts])
    for a in range(BANDS - 1):
        to_slab(a)
    for p in range(len(PARTS)):
        stage1(p)

    me = lat * lons + lon
    picked = lax.broadcasted_iota(jnp.int32, (8, C), 0) + me * 4
    picked = (picked == lax.broadcasted_iota(jnp.int32, (8, C), 1)).astype(F32)
    w_rows = nn(picked.astype(BF16), wqkv[...])
    gain_rows = jnp.sum(picked * gain[...], axis=1, keepdims=True)

    for copy in back:
        copy.wait_recv()
    out_ref[LEAD:] = (
        out_ext[0 : TOKENS - LEAD].astype(F32) + nn(pick_t[LEAD:, 0:SIDE], left[0:SIDE])
    ).astype(BF16)
    out_ref[0:LEAD] = (top[...].astype(F32) + nn(pick_t[0:LEAD], left[...])).astype(BF16)
    store = pltpu.make_async_copy(out_ref, out_hbm, local.at[2])
    store.start()

    for copy in halo + first + back + [c for part in sent for c in part[:3]]:
        copy.wait_send()
    total = jnp.concatenate([stage2(p) for p in range(len(PARTS))], axis=1)
    total = total * (1.0 / math.sqrt(TOKENS * lats * lons))
    gqkv = [total[4 * j : 4 * j + 4] for j in range(3)]
    gqkv_ref[...] = jnp.concatenate(gqkv, axis=1)
    gproj_ref[...] = total[12:16]
    dots = jnp.zeros((4, 1), F32)
    for j in range(3):
        dots = dots + jnp.sum(gqkv[j] * w_rows[0:4, j * C : (j + 1) * C], axis=1, keepdims=True)
    dots = dots / gain_rows[0:4]
    diagonal = lax.broadcasted_iota(jnp.int32, (4, 128), 0)
    diagonal = diagonal == lax.broadcasted_iota(jnp.int32, (4, 128), 1)
    ggain_ref[...] = jnp.sum(jnp.where(diagonal, dots, 0.0), axis=0, keepdims=True)
    for copy in [c for part in sent for c in part[3:]]:
        copy.wait_send()
    store.wait()


def sublayer(*args):
    vmem = pl.BlockSpec(memory_space=pltpu.VMEM)
    hbm = pl.BlockSpec(memory_space=pl.ANY)
    scratch = [
        pltpu.VMEM((2, TOKENS + LEAD, C), BF16),
        pltpu.VMEM((2, EDGE, C), BF16),
        pltpu.VMEM((2, EDGE, C), BF16),
        pltpu.VMEM((TOKENS, C), F32),
        pltpu.VMEM((TOKENS, 128), F32),
        pltpu.VMEM((TOKENS, C), F32),
        pltpu.VMEM((TOKENS, C), F32),
        pltpu.VMEM((TOKENS, 3 * C), F32),
        pltpu.VMEM((TOKENS, C), F32),
        pltpu.VMEM((TOKENS, C), F32),
        pltpu.VMEM((TOKENS, 3 * C), F32),
        pltpu.VMEM((TOKENS, C), BF16),
        pltpu.VMEM((EDGE, C), BF16),
        pltpu.VMEM((LEAD, C), BF16),
        pltpu.VMEM((EDGE, C), BF16),
        pltpu.VMEM((8, C, 256), F32),
        pltpu.VMEM((64, 16, C), F32),
        pltpu.VMEM((64, 16, C), BF16),
        pltpu.VMEM((64, 16, C), BF16),
        pltpu.VMEM((TOKENS, C), BF16),
    ]
    scratch += [pltpu.VMEM(x.shape, x.dtype) for x in args[2:]]
    for _, width, _, _ in PARTS:
        for dims in ((4, 4, 4), (3, 4, 4), (4, 4), (15,)):
            scratch.append(pltpu.VMEM(dims + (16, width), BF16))
        scratch.append(pltpu.VMEM((16, width), F32))
    copies = 3 + 3 + 19 * len(PARTS)
    return pl.pallas_call(
        sublayer_kernel,
        out_shape=(
            jax.ShapeDtypeStruct((TOKENS, C), BF16),
            jax.ShapeDtypeStruct((4, 3 * C), F32),
            jax.ShapeDtypeStruct((4, C), F32),
            jax.ShapeDtypeStruct((1, 128), F32),
        ),
        in_specs=[hbm] * 11,
        out_specs=(hbm, vmem, vmem, vmem),
        scratch_shapes=scratch
        + [
            pltpu.SemaphoreType.DMA((12,)),
            pltpu.SemaphoreType.DMA((copies,)),
            pltpu.SemaphoreType.DMA((copies,)),
        ],
        compiler_params=pltpu.CompilerParams(
            collective_id=1, has_side_effects=True, vmem_limit_bytes=62 * 1024 * 1024
        ),
        name="window_grads",
    )(*args)


def hand_on_kernel(out_ref, gqkv_ref, gproj_ref, gain_ref, out, gqkv, gproj, ggain):
    out[...] = out_ref[...]
    gqkv[...] = gqkv_ref[...]
    gproj[...] = gproj_ref[...]
    ggain[...] = gain_ref[0, 0:4]


def hand_on(*args):
    def whole(*shape):
        return pl.BlockSpec(shape, lambda i: (0,) * len(shape))

    tokens = pl.BlockSpec((TOKENS // 2, C), lambda i: (i, 0))
    return pl.pallas_call(
        hand_on_kernel,
        grid=(2,),
        out_shape=(
            jax.ShapeDtypeStruct((TOKENS, C), BF16),
            jax.ShapeDtypeStruct((4, 3 * C), F32),
            jax.ShapeDtypeStruct((4, C), F32),
            jax.ShapeDtypeStruct((4,), F32),
        ),
        in_specs=[tokens, whole(4, 3 * C), whole(4, C), whole(1, 128)],
        out_specs=(tokens, whole(4, 3 * C), whole(4, C), whole(4)),
        compiler_params=pltpu.CompilerParams(vmem_limit_bytes=62 * 1024 * 1024),
        name="hand_on",
    )(*args)


def on_device(activations, cotangent, norm_gain, qkv_weight, proj_weight):
    results = sublayer(
        activations.reshape(TOKENS, C),
        cotangent.reshape(TOKENS, C),
        norm_gain.reshape(1, C),
        qkv_weight,
        proj_weight,
        *orders(),
    )
    grad_input, gqkv, gproj, ggain = hand_on(*results)
    return grad_input.reshape(ROWS, COLS, C), gqkv, gproj, ggain


def solution(mesh):
    return jax.shard_map(
        on_device,
        mesh=mesh,
        in_specs=(P("lat", "lon", None), P("lat", "lon", None), P(), P(), P()),
        out_specs=(
            P("lat", "lon", None),
            P(("lat", "lon"), None),
            P(("lat", "lon"), None),
            P(("lat", "lon")),
        ),
        check_vma=False,
    )
```

```python
import math

import jax
import jax.numpy as jnp
import numpy as np
from jax import lax
from jax.experimental import pallas as pl
from jax.experimental.pallas import tpu as pltpu
from jax.sharding import PartitionSpec as P

C = 512
HEADS = 16
HEAD = C // HEADS
WIN_LAT = 6
WIN_LON = 12
SPAN = WIN_LAT * WIN_LON
ROWS = 24
COLS = 48
BANDS = ROWS // WIN_LAT
PER_BAND = COLS // WIN_LON
BAND = WIN_LAT * COLS
TOKENS = ROWS * COLS
HALF_LAT = WIN_LAT // 2
HALF_LON = WIN_LON // 2
SIDE = 128
EDGE = SIDE + 32
LAST = 208
TWO = 2 * COLS
PIECE = 2 * WIN_LON
GROUP = 128 // HEAD
F32 = jnp.float32
BF16 = jnp.bfloat16


def orders():
    perm = np.zeros((TWO, TWO), np.float32)
    beside = np.zeros((BANDS, BAND - LAST, EDGE), np.float32)
    pick = np.zeros((EDGE, TOKENS), np.float32)
    for b in range(PER_BAND):
        for r in range(WIN_LAT):
            for c in range(WIN_LON):
                col = WIN_LON * b + HALF_LON + c
                token = b * SPAN + r * WIN_LON + c
                if col < COLS:
                    if r < 2:
                        perm[b * PIECE + r * WIN_LON + c, r * COLS + col] = 1.0
                    continue
                for a in range(BANDS):
                    beside[a, token - LAST, edge_row(a * WIN_LAT + HALF_LAT + r, col - COLS)] = 1.0
    for row in range(ROWS):
        for c in range(HALF_LON):
            pick[edge_row(row + (ROWS if row < HALF_LAT else 0), c), row * COLS + c] = 1.0
    return [jnp.asarray(x, BF16) for x in (perm, perm.T, beside, beside.transpose(0, 2, 1), pick, pick.T)]


def edge_row(row, col):
    if row < ROWS:
        return (row - HALF_LAT) * HALF_LON + col
    return SIDE + (row - ROWS) * HALF_LON + col


def nn(a, b):
    return lax.dot_general(a, b, (((1,), (0,)), ((), ())), preferred_element_type=F32)


def nt(a, b):
    return lax.dot_general(a, b, (((1,), (1,)), ((), ())), preferred_element_type=F32)


def tn(a, b):
    return lax.dot_general(a, b, (((0,), (0,)), ((), ())), preferred_element_type=F32)


PARTS = ((0, 256, "zyx", "yxz"), (256, 128, "yxz", "zyx"), (384, 128, "xzy", "xzy"))
MESH = pl.DeviceIdType.MESH
LEAD = HALF_LAT * COLS


def place():
    lat, lon = lax.axis_index("lat"), lax.axis_index("lon")
    spot = {"z": lat // 2, "x": (lon // 2) % 2 * 2 + lat % 2, "y": lon // 4}
    return lat, lon, spot, lon % 2


def device_at(spot, core):
    return (spot["z"] * 2 + spot["x"] % 2, spot["y"] * 4 + spot["x"] // 2 * 2 + core)


def chip_at(at):
    return at["z"] * 16 + at["x"] % 2 * 8 + at["y"] * 2 + at["x"] // 2


def sublayer_kernel(
    own_in, own_cot, *rest,
):
    fetched, rest = rest[:9], rest[9:]
    (
        out_hbm, gqkv_ref, gproj_ref, ggain_ref,
        ext, side, side_out,
        normed, inv_std, scaled, cot_win, qkv, grad_att, att, grad_all,
        out_ext, back_side, top, left, grads, mine, theirs, got0, out_ref,
    ) = rest[:24]
    held_here, rest = rest[24:33], rest[33:]
    gain, wqkv, wproj, perm, perm_t, beside, beside_t, pick, pick_t = held_here
    buffers, (local, send, recv) = rest[:-3], rest[-3:]
    loads = [
        pltpu.make_async_copy(own_in, ext.at[0, pl.ds(0, TOKENS)], local.at[0]),
        pltpu.make_async_copy(own_cot, ext.at[1, pl.ds(0, TOKENS)], local.at[1]),
    ]
    for i in (7, 1, 3, 0, 2, 5, 4, 6, 8):
        loads.append(pltpu.make_async_copy(fetched[i], held_here[i], local.at[3 + i]))
    for load in loads:
        load.start()

    lat, lon, spot, core = place()
    lats, lons = lax.axis_size("lat"), lax.axis_size("lon")
    sibling = device_at(spot, 1 - core)
    down, up = (lat + 1) % lats, (lat + lats - 1) % lats
    east, west = (lon + 1) % lons, (lon + lons - 1) % lons
    peers = [sibling, (down, lon), (up, lon), (lat, east), (lat, west), (down, east), (up, west)]
    for axes in ("xy", "xz", "yz"):
        for i in range(4):
            for j in range(4):
                if (i or j) and (j or axes == "xy") and (i or axes != "yz"):
                    there = {axis: spot[axis] for axis in "xyz"}
                    there[axes[0]] = (spot[axes[0]] + i) % 4
                    there[axes[1]] = (spot[axes[1]] + j) % 4
                    peers.append(device_at(there, core))
    barrier = pltpu.get_barrier_semaphore()
    for peer in peers:
        pl.semaphore_signal(barrier, inc=1, device_id=peer, device_id_type=MESH)

    count = [0]

    def remote(src, dst, peer):
        i = count[0]
        count[0] += 1
        copy = pltpu.make_async_remote_copy(
            src_ref=src, dst_ref=dst, send_sem=send.at[i], recv_sem=recv.at[i],
            device_id=peer, device_id_type=MESH,
        )
        copy.start()
        return copy

    for load in loads[:3]:
        load.wait()
    for i in range(2):
        side_out[i] = nn(pick[...], ext[i, 0:TOKENS]).astype(BF16)
    pl.semaphore_wait(barrier, len(peers))
    main, angle = pl.ds(0, SIDE), pl.ds(SIDE, EDGE - SIDE)
    halo = [
        remote(side_out.at[:, main], side.at[:, main], (lat, west)),
        remote(ext.at[:, pl.ds(0, LEAD)], ext.at[:, pl.ds(TOKENS, LEAD)], (up, lon)),
        remote(side_out.at[:, angle], side.at[:, angle], (up, west)),
    ]

    def forward(pieces):
        gathered = []
        for i in range(2):
            parts = []
            for a, lo, hi in pieces:
                start = LEAD + a * BAND
                first = lo // SPAN * PIECE
                first_row = first // 16 * 16
                last = hi // SPAN * PIECE
                rows = perm[first_row : -(-last // 16) * 16]
                thirds = [
                    nn(rows, ext[i, start + j * TWO : start + (j + 1) * TWO])[first - first_row :]
                    for j in range(3)
                ]
                got = [
                    third[at : at + PIECE] for at in range(0, last - first, PIECE) for third in thirds
                ]
                got = jnp.concatenate(got, axis=0)
                if hi == BAND:
                    width = EDGE if a == BANDS - 1 else SIDE
                    edge = nn(beside[a, :, 0:width], side[i, 0:width])
                    if lo < LAST:
                        got = jnp.concatenate([got[: LAST - lo], got[LAST - lo :] + edge], axis=0)
                    else:
                        got = got + edge[lo - LAST :]
                parts.append(got)
            gathered.append(jnp.concatenate(parts, axis=0))
        x, cot = gathered
        center = x - jnp.mean(x, axis=-1, keepdims=True)
        inv = lax.rsqrt(jnp.mean(center * center, axis=-1, keepdims=True) + 1e-05)
        norm = center * inv
        sc = norm * gain[...]
        qkv_now = nn(sc.astype(BF16), wqkv[...]).astype(BF16).astype(F32)
        att_now = nt(cot.astype(BF16), wproj[...]).astype(BF16).astype(F32)
        at = 0
        for a, lo, hi in pieces:
            dst = slice(a * BAND + lo, a * BAND + hi)
            src = slice(at, at + hi - lo)
            at += hi - lo
            normed[dst] = norm[src]
            inv_std[dst] = jnp.broadcast_to(inv[src], (hi - lo, 128))
            scaled[dst] = sc[src]
            cot_win[dst] = cot[src]
            qkv[dst] = qkv_now[src]
            grad_att[dst] = att_now[src]

    lane = lax.broadcasted_iota(jnp.int32, (1, 128), 1) // HEAD
    masks = [(lane == j).astype(F32) for j in range(GROUP)]
    key_half = lax.broadcasted_iota(jnp.int32, (SPAN, SPAN), 0) >= HALF_LAT * WIN_LON
    query_half = lax.broadcasted_iota(jnp.int32, (SPAN, SPAN), 1) >= HALF_LAT * WIN_LON
    parted = jnp.where(key_half == query_half, 0.0, -1e30)
    parted = jnp.concatenate([parted] * GROUP, axis=1)

    def stacked(x):
        return jnp.concatenate([x * m for m in masks], axis=0).astype(BF16)

    def by_head(x):
        x = x.reshape(GROUP, SPAN, 128)
        y = x[GROUP - 1]
        for j in range(GROUP - 2, -1, -1):
            y = jnp.where(lane == j, x[j], y)
        return y

    scale = HEAD ** (-0.5)

    def attention(windows, edge=False):
        shut = parted * jnp.where(lat == lats - 1, 1.0, 0.0)
        todo = []
        for w in windows:
            rows = pl.ds(pl.multiple_of(w * SPAN, 8), SPAN)
            todo += [(rows, [slice(j * C + lo, j * C + lo + 128) for j in range(3)])
                     for lo in range(0, C, 128)]
        q = [stacked(qkv[rows, cols[0]]) for rows, cols in todo]
        k = [qkv[rows, cols[1]].astype(BF16) for rows, cols in todo]
        v = [qkv[rows, cols[2]].astype(BF16) for rows, cols in todo]
        da = [stacked(grad_att[rows, cols[0]]) for rows, cols in todo]
        n = range(len(todo))
        s = [nt(k[i], q[i]) * scale for i in n]
        if edge:
            s = [x + shut for x in s]
        gp = [nt(v[i], da[i]) for i in n]
        ex = [jnp.exp(x - jnp.max(x, axis=0, keepdims=True)) for x in s]
        prob = [x * (1.0 / jnp.sum(x, axis=0, keepdims=True)) for x in ex]
        inner = [jnp.sum(prob[i] * gp[i], axis=0, keepdims=True) for i in n]
        gs = [(prob[i] * (gp[i] - inner[i]) * scale).astype(BF16) for i in n]
        pb = [x.astype(BF16) for x in prob]
        found = [by_head(tn(pb[i], v[i])) for i in n]
        grad_q = [by_head(tn(gs[i], k[i])) for i in n]
        grad_k = [nn(gs[i], q[i]) for i in n]
        grad_v = [nn(pb[i], da[i]) for i in n]
        for i, (rows, cols) in enumerate(todo):
            att[rows, cols[0]] = found[i]
            grad_all[rows, cols[0]] = grad_q[i]
            grad_all[rows, cols[1]] = grad_k[i]
            grad_all[rows, cols[2]] = grad_v[i]

    for load in loads[3:8]:
        load.wait()
    inner = (PER_BAND - 1) * SPAN
    forward([(a, 0, inner) for a in range(BANDS - 1)])

    def early(i, carry):
        attention([i * PER_BAND + b for b in range(PER_BAND - 1)])
        return carry

    lax.fori_loop(0, BANDS - 1, early, 0)
    def weight_sums(pieces, halves, found):
        def tokens(ref, cols):
            parts = [ref[lo:hi, cols] for lo, hi in pieces]
            return jnp.concatenate(parts, axis=0).astype(BF16)

        if not found:
            found += [tokens(scaled, slice(0, C)).T, tokens(att, slice(0, C)).T]
        for half in halves:
            lo = half * 256
            for j in range(3):
                yield 4 * half + j, nn(found[0], tokens(grad_all, slice(j * C + lo, j * C + lo + 256)))
            yield 4 * half + 3, nn(found[1], tokens(cot_win, slice(lo, lo + 256)))

    starts = [a * BAND for a in range(BANDS - 1)]
    for i, value in weight_sums([(start, start + inner) for start in starts], (0, 1), []):
        grads[i] = value
    halo[0].wait_recv()
    forward([(a, inner, BAND) for a in range(BANDS - 1)])
    attention([a * PER_BAND + PER_BAND - 1 for a in range(BANDS - 1)])
    halo[1].wait_recv()
    halo[2].wait_recv()
    forward([(BANDS - 1, 0, BAND)])

    def late(i, carry):
        attention([(BANDS - 1) * PER_BAND + 2 * i + b for b in range(2)], edge=True)
        return carry

    lax.fori_loop(0, PER_BAND // 2, late, 0)

    late_rows = [(start + inner, start + BAND) for start in starts] + [(TOKENS - BAND, TOKENS)]
    turned_once = []
    upper = lax.broadcasted_iota(jnp.int32, (1, 8, 1), 1) < 4
    first_core = lax.broadcasted_iota(jnp.int32, (1, 8, 1), 1) * 0 + core == 0
    first = []
    for half in range(2):
        lo = half * 256
        lanes = slice(lo, lo + 256)
        for i, value in weight_sums(late_rows, (half,), turned_once):
            grads[i] += value

        def pack(i, carry):
            rows = pl.ds(pl.multiple_of(i * 64, 64), 64)
            chips = pl.ds(i * 8, 8)
            t = [grads[4 * half + j, rows].reshape(8, 8, 256) for j in range(4)]
            turned = [pltpu.roll(x, 4, 1) for x in t]
            block = []
            for near, far in ((t, turned), (turned, t)):
                block.append(
                    jnp.concatenate(
                        [jnp.where(upper, near[j], far[j + 1]) for j in (0, 2)], axis=1
                    )
                )
            is_first = jnp.concatenate([first_core, first_core], axis=1)
            mine[chips, :, lanes] = jnp.where(is_first, block[0], block[1])
            theirs[chips, :, lanes] = jnp.where(is_first, block[1], block[0]).astype(BF16)
            return carry

        lax.fori_loop(0, 8, pack, 0, unroll=2)
        for start, width, _, _ in PARTS:
            if lo <= start < lo + 256:
                span = pl.ds(start, width)
                first.append(remote(theirs.at[:, :, span], got0.at[:, :, span], sibling))

    back = []
    for load in loads[8:]:
        load.wait()

    def norm_grads(pieces):
        def tokens(ref):
            return jnp.concatenate([ref[lo:hi] for lo, hi in pieces], axis=0)

        gn = nt(tokens(grad_all).astype(BF16), wqkv[...]) * gain[...]
        norm = tokens(normed)
        branch = tokens(inv_std)[:, 0:1] * (
            gn
            - jnp.mean(gn, axis=-1, keepdims=True)
            - norm * jnp.mean(gn * norm, axis=-1, keepdims=True)
        )
        done = tokens(cot_win) + branch
        at = 0
        for lo, hi in pieces:
            normed[lo:hi] = done[at : at + hi - lo]
            at += hi - lo

    def to_slab(a):
        for j in range(3):
            at = [a * BAND + b * SPAN + j * PIECE for b in range(PER_BAND)]
            part = jnp.concatenate([normed[i : i + PIECE] for i in at], axis=0).astype(BF16)
            slab = slice(a * BAND + j * TWO, a * BAND + (j + 1) * TWO)
            out_ext[slab] = nn(perm_t[...], part).astype(BF16)

    def role(p, r, axis):
        first_order, second_order = PARTS[p][2:]
        return (1 - core) * int(first_order[r] == axis) + core * int(second_order[r] == axis)

    def by_role(p, steps):
        return {axis: sum(role(p, r, axis) * steps[r] for r in range(3)) for axis in "xyz"}

    def my_role(p, r):
        return sum(role(p, r, axis) * spot[axis] for axis in "xyz")

    def peer_at(p, steps):
        moved = by_role(p, steps)
        return device_at({axis: (spot[axis] + moved[axis]) % 4 for axis in "xyz"}, core)

    def summed0(p, chip):
        lo, width = PARTS[p][:2]
        lanes = slice(lo, lo + width)
        return mine[chip, :, lanes] + got0[chip, :, lanes].astype(F32)

    sent = [[] for _ in PARTS]

    def stage0(p):
        held, got = buffers[5 * p : 5 * p + 2]
        first[p].wait_recv()

        def add(i, carry):
            at = (i // 16, i // 4 % 4, i % 4)
            held[at] = summed0(p, chip_at(by_role(p, at))).astype(BF16)
            return carry

        lax.fori_loop(0, 64, add, 0, unroll=8)
        for k in (2, 1, 3):
            sent[p].append(
                remote(held.at[(my_role(p, 0) + k) % 4], got.at[k - 1], peer_at(p, (k, 0, 0)))
            )

    def stage1(p):
        got, nxt, nxt_got, keep = buffers[5 * p + 1 : 5 * p + 5]
        for copy in sent[p]:
            copy.wait_recv()
        here = my_role(p, 0)
        b, c = my_role(p, 1), my_role(p, 2)

        def total(i, j):
            x = summed0(p, chip_at(by_role(p, (here, i, j))))
            for k in range(3):
                x = x + got[k, i, j].astype(F32)
            return x

        def add(i, carry):
            nxt[i // 4, i % 4] = total(i // 4, i % 4).astype(BF16)
            return carry

        lax.fori_loop(0, 16, add, 0, unroll=8)
        keep[...] = total(b, c)
        for i in (2, 1, 3, 0):
            for j in (2, 1, 3, 0):
                if i or j:
                    sent[p].append(
                        remote(
                            nxt.at[(b + i) % 4, (c + j) % 4],
                            nxt_got.at[4 * i + j - 1],
                            peer_at(p, (0, i, j)),
                        )
                    )

    def stage2(p):
        got, keep = buffers[5 * p + 3 : 5 * p + 5]
        for copy in sent[p][3:]:
            copy.wait_recv()
        x = keep[...]
        for i in range(15):
            x = x + got[i].astype(F32)
        return x

    norm_grads([(TOKENS - BAND, TOKENS)])
    to_slab(BANDS - 1)
    back.append(remote(out_ext.at[pl.ds(TOKENS - LEAD, LEAD)], top, (down, lon)))
    stage0(0)
    stage0(1)
    stage0(2)
    norm_grads([(start + inner, start + BAND) for start in starts])
    edges = jnp.zeros((EDGE, C), F32)
    for a in range(BANDS):
        rows = normed[a * BAND + LAST : (a + 1) * BAND].astype(BF16)
        edges = edges + nn(beside_t[a], rows)
    back_side[...] = edges.astype(BF16)
    back.append(remote(back_side.at[main], left.at[main], (lat, east)))
    back.append(remote(back_side.at[angle], left.at[angle], (down, east)))
    norm_grads([(start, start + inner) for start in starts])
    for a in range(BANDS - 1):
        to_slab(a)
    for p in range(len(PARTS)):
        stage1(p)

    me = lat * lons + lon
    picked = lax.broadcasted_iota(jnp.int32, (8, C), 0) + me * 4
    picked = (picked == lax.broadcasted_iota(jnp.int32, (8, C), 1)).astype(F32)
    w_rows = nn(picked.astype(BF16), wqkv[...])
    gain_rows = jnp.sum(picked * gain[...], axis=1, keepdims=True)

    stores = []

    def put(lo, hi, value):
        out_ref[lo:hi] = value.astype(BF16)
        rows = pl.ds(lo, hi - lo)
        copy = pltpu.make_async_copy(out_ref.at[rows], out_hbm.at[rows], local.at[12 + len(stores)])
        copy.start()
        stores.append(copy)

    back[1].wait_recv()
    for lo in range(LEAD, TOKENS, 336):
        hi = lo + 336
        put(lo, hi, out_ext[lo - LEAD : hi - LEAD].astype(F32) + nn(pick_t[lo:hi, 0:SIDE], left[0:SIDE]))
    back[0].wait_recv()
    back[2].wait_recv()
    put(0, LEAD, top[...].astype(F32) + nn(pick_t[0:LEAD], left[...]))

    for copy in halo + first + back + [c for part in sent for c in part[:3]]:
        copy.wait_send()
    total = jnp.concatenate([stage2(p) for p in range(len(PARTS))], axis=1)
    total = total * (1.0 / math.sqrt(TOKENS * lats * lons))
    gqkv = [total[4 * j : 4 * j + 4] for j in range(3)]
    gqkv_ref[...] = jnp.concatenate(gqkv, axis=1)
    gproj_ref[...] = total[12:16]
    dots = jnp.zeros((4, 1), F32)
    for j in range(3):
        dots = dots + jnp.sum(gqkv[j] * w_rows[0:4, j * C : (j + 1) * C], axis=1, keepdims=True)
    dots = dots / gain_rows[0:4]
    diagonal = lax.broadcasted_iota(jnp.int32, (4, 128), 0)
    diagonal = diagonal == lax.broadcasted_iota(jnp.int32, (4, 128), 1)
    ggain_ref[...] = jnp.sum(jnp.where(diagonal, dots, 0.0), axis=0, keepdims=True)
    for copy in [c for part in sent for c in part[3:]]:
        copy.wait_send()
    for copy in stores:
        copy.wait()


def sublayer(*args):
    vmem = pl.BlockSpec(memory_space=pltpu.VMEM)
    hbm = pl.BlockSpec(memory_space=pl.ANY)
    scratch = [
        pltpu.VMEM((2, TOKENS + LEAD, C), BF16),
        pltpu.VMEM((2, EDGE, C), BF16),
        pltpu.VMEM((2, EDGE, C), BF16),
        pltpu.VMEM((TOKENS, C), F32),
        pltpu.VMEM((TOKENS, 128), F32),
        pltpu.VMEM((TOKENS, C), F32),
        pltpu.VMEM((TOKENS, C), F32),
        pltpu.VMEM((TOKENS, 3 * C), F32),
        pltpu.VMEM((TOKENS, C), F32),
        pltpu.VMEM((TOKENS, C), F32),
        pltpu.VMEM((TOKENS, 3 * C), F32),
        pltpu.VMEM((TOKENS, C), BF16),
        pltpu.VMEM((EDGE, C), BF16),
        pltpu.VMEM((LEAD, C), BF16),
        pltpu.VMEM((EDGE, C), BF16),
        pltpu.VMEM((8, C, 256), F32),
        pltpu.VMEM((64, 16, C), F32),
        pltpu.VMEM((64, 16, C), BF16),
        pltpu.VMEM((64, 16, C), BF16),
        pltpu.VMEM((TOKENS, C), BF16),
    ]
    scratch += [pltpu.VMEM(x.shape, x.dtype) for x in args[2:]]
    for _, width, _, _ in PARTS:
        for dims in ((4, 4, 4), (3, 4, 4), (4, 4), (15,)):
            scratch.append(pltpu.VMEM(dims + (16, width), BF16))
        scratch.append(pltpu.VMEM((16, width), F32))
    copies = 3 + 3 + 19 * len(PARTS)
    return pl.pallas_call(
        sublayer_kernel,
        out_shape=(
            jax.ShapeDtypeStruct((TOKENS, C), BF16),
            jax.ShapeDtypeStruct((4, 3 * C), F32),
            jax.ShapeDtypeStruct((4, C), F32),
            jax.ShapeDtypeStruct((1, 128), F32),
        ),
        in_specs=[hbm] * 11,
        out_specs=(hbm, vmem, vmem, vmem),
        scratch_shapes=scratch
        + [
            pltpu.SemaphoreType.DMA((16,)),
            pltpu.SemaphoreType.DMA((copies,)),
            pltpu.SemaphoreType.DMA((copies,)),
        ],
        compiler_params=pltpu.CompilerParams(
            collective_id=1, has_side_effects=True, vmem_limit_bytes=62 * 1024 * 1024
        ),
        name="window_grads",
    )(*args)


def hand_on_kernel(out_ref, gqkv_ref, gproj_ref, gain_ref, out, gqkv, gproj, ggain):
    out[...] = out_ref[...]
    gqkv[...] = gqkv_ref[...]
    gproj[...] = gproj_ref[...]
    ggain[...] = gain_ref[0, 0:4]


def hand_on(*args):
    def whole(*shape):
        return pl.BlockSpec(shape, lambda i: (0,) * len(shape))

    tokens = pl.BlockSpec((TOKENS // 2, C), lambda i: (i, 0))
    return pl.pallas_call(
        hand_on_kernel,
        grid=(2,),
        out_shape=(
            jax.ShapeDtypeStruct((TOKENS, C), BF16),
            jax.ShapeDtypeStruct((4, 3 * C), F32),
            jax.ShapeDtypeStruct((4, C), F32),
            jax.ShapeDtypeStruct((4,), F32),
        ),
        in_specs=[tokens, whole(4, 3 * C), whole(4, C), whole(1, 128)],
        out_specs=(tokens, whole(4, 3 * C), whole(4, C), whole(4)),
        compiler_params=pltpu.CompilerParams(vmem_limit_bytes=62 * 1024 * 1024),
        name="hand_on",
    )(*args)


def on_device(activations, cotangent, norm_gain, qkv_weight, proj_weight):
    results = sublayer(
        activations.reshape(TOKENS, C),
        cotangent.reshape(TOKENS, C),
        norm_gain.reshape(1, C),
        qkv_weight,
        proj_weight,
        *orders(),
    )
    grad_input, gqkv, gproj, ggain = hand_on(*results)
    return grad_input.reshape(ROWS, COLS, C), gqkv, gproj, ggain


def solution(mesh):
    return jax.shard_map(
        on_device,
        mesh=mesh,
        in_specs=(P("lat", "lon", None), P("lat", "lon", None), P(), P(), P()),
        out_specs=(
            P("lat", "lon", None),
            P(("lat", "lon"), None),
            P(("lat", "lon"), None),
            P(("lat", "lon")),
        ),
        check_vma=False,
    )
```
